128 devices in a mesh: ctx: 32 (over z, y_lo, x), wsh: 4 (over y_hi, core).
Axes of the slice: x: 4, y: 4 (y_hi: 2, y_lo: 2; y = y_hi * 2 + y_lo), z: 4, core: 2. Of those that a mesh axis runs over, the one named last changes fastest.
Arguments:
- tokens: bfloat16 [4, 8192, 768], P('wsh', 'ctx'), may hold values from -6 to 6
- cotangent: bfloat16 [4, 8192, 768], P('wsh', 'ctx'), may hold values from -6 to 6
- pairing: int32 [32], replicated, may hold values from 0 to 31, each once
- first_gain: bfloat16 [768], P('wsh'), may hold values from 0.5 to 1.5
- first_shift: bfloat16 [768], P('wsh'), may hold values from -4 to 4
- qkv_weight: bfloat16 [768, 2304], P('wsh'), may hold values from -0.3125 to 0.3125
- qkv_bias: bfloat16 [2304], P('wsh'), may hold values from -4 to 4
- dense_weight: bfloat16 [768, 768], P('wsh'), may hold values from -1.25 to 1.25
- second_gain: bfloat16 [768], P('wsh'), may hold values from 0.5 to 1.5
- second_shift: bfloat16 [768], P('wsh'), may hold values from -4 to 4
- up_weight: bfloat16 [768, 3072], P('wsh'), may hold values from -0.21875 to 0.21875
- up_bias: bfloat16 [3072], P('wsh'), may hold values from -6 to 6
- down_weight: bfloat16 [3072, 768], P('wsh'), may hold values from -0.109375 to 0.109375
- out_bias: bfloat16 [768], P('wsh'), may hold values from -6 to 6
Outputs:
- layer_output: bfloat16 [4, 8192, 768], P('wsh', 'ctx')
- input_grad: bfloat16 [4, 8192, 768], P('wsh', 'ctx')
- first_gain_grad: float32 [768], P('wsh')
- first_shift_grad: float32 [768], P('wsh')
- qkv_weight_grad: float32 [768, 2304], P('wsh')
- qkv_bias_grad: float32 [2304], P('wsh')
- dense_weight_grad: float32 [768, 768], P('wsh')
- second_gain_grad: float32 [768], P('wsh')
- second_shift_grad: float32 [768], P('wsh')
- up_weight_grad: float32 [768, 3072], P('wsh')
- up_bias_grad: float32 [3072], P('wsh')
- down_weight_grad: float32 [3072, 768], P('wsh')
- out_bias_grad: float32 [768], P('wsh')
The draws below stay inside these ranges and needn't reach their ends.
All inputs are finite; a program needn't handle non-finite values.
Results may differ from the reference program's by a relative error of at most 0.03.
Values may be sent and summed in bfloat16 or wider, within the bound.
A program may use at most 320 MiB of HBM per device.

```python
import jax
import jax.numpy as jnp
from jax import lax

D = 768
HEADS = 12
HD = 64
ROT = 16
FF = 3072
BLK = 128
SEQ = 8192
SEQS = 4
N_CTX = 32


def steps_of(stream_key, extent, shards, low, high):
    def one(dim, parts):
        steps = jax.random.uniform(jax.random.fold_in(jax.random.fold_in(stream_key, 6), dim), (parts,), jnp.float32, low / len(shards), high / len(shards))
        return jnp.repeat(jnp.exp(steps), extent[dim] // parts).reshape((-1,) + (1,) * (len(extent) - dim - 1))

    loudness = one(*shards[0])
    for cut in shards[1:]:
        loudness = loudness * one(*cut)
    return loudness


def noise(rng, dims, scale, bound, cuts=(), kind=jnp.bfloat16):
    array = scale * jax.random.normal(rng, dims, jnp.float32)
    if cuts:
        array = array * steps_of(rng, dims, cuts, -0.22, 0.18)
    return jnp.clip(array, -bound, bound).astype(kind)


def setup_inputs(seed: int = 0) -> dict:
    streams_of = jax.random.split(jax.random.key(seed), 15)
    return {
        "tokens": noise(streams_of[0], (SEQS, SEQ, D), 1.0, 6.0, ((0, 4), (1, 32))),
        "cotangent": noise(streams_of[1], (SEQS, SEQ, D), 1.0, 6.0, ((0, 4), (1, 32))),
        "pairing": jax.random.permutation(streams_of[2], N_CTX).astype(jnp.int32),
        "first_gain": jnp.clip(1.0 + 0.1 * jax.random.normal(streams_of[3], (D,), jnp.float32), 0.5, 1.5).astype(jnp.bfloat16),
        "first_shift": noise(streams_of[4], (D,), 0.3, 4.0, ((0, 4),)),
        "qkv_weight": noise(streams_of[5], (D, 3 * D), (D // 2) ** -0.5, 0.3125, ((0, 4),)),
        "qkv_bias": noise(streams_of[6], (3 * D,), 0.3, 4.0, ((0, 4),)),
        "dense_weight": noise(streams_of[7], (D, D), (max(16, D // 32)) ** -0.5, 1.25, ((0, 4),)),
        "second_gain": jnp.clip(1.0 + 0.1 * jax.random.normal(streams_of[8], (D,), jnp.float32), 0.5, 1.5).astype(jnp.bfloat16),
        "second_shift": noise(streams_of[9], (D,), 0.3, 4.0, ((0, 4),)),
        "up_weight": noise(streams_of[10], (D, FF), D ** -0.5, 0.21875, ((0, 4),)),
        "up_bias": noise(streams_of[11], (FF,), 0.5, 6.0, ((0, 4),)),
        "down_weight": noise(streams_of[12], (FF, D), FF ** -0.5, 0.109375, ((0, 4),)),
        "out_bias": noise(streams_of[13], (D,), 0.5, 6.0, ((0, 4),)),
    }


@jax.custom_vjp
def low(v):
    return lax.optimization_barrier(v.astype(jnp.bfloat16)).astype(jnp.float32)

@jax.custom_vjp
def low_back(v):
    return v

def low_keep(v):
    return (low(v), None)

def low_pass(kept, grad):
    return (grad,)

def back_keep(v):
    return (v, None)

def back_low(kept, grad):
    return (low(grad),)
low.defvjp(low_keep, low_pass)
low_back.defvjp(back_keep, back_low)

def product(left_side, right_side):
    return jnp.dot(left_side, right_side, precision=lax.Precision.HIGHEST, preferred_element_type=jnp.float32)

def layer_norm(values, norm_gain, norm_shift):
    row_mean = lax.optimization_barrier(jnp.mean(values, -1, keepdims=True))
    centered = values - row_mean
    row_var = lax.optimization_barrier(jnp.mean(centered * centered, -1, keepdims=True))
    return centered * lax.rsqrt(row_var + 1e-05) * norm_gain + norm_shift

def rotate(tensor, cosine, sine_table):
    half_dims = ROT // 2
    lower_part = tensor[..., :half_dims]
    upper_part = tensor[..., half_dims:ROT]
    turned = jnp.concatenate([-upper_part, lower_part], -1)
    moved = tensor[..., :ROT] * cosine + turned * sine_table
    return jnp.concatenate([moved, tensor[..., ROT:]], -1)

def rotary_tables(positions):
    half_dims = ROT // 2
    exponents = jnp.arange(half_dims).astype(jnp.float32) * 2.0 / ROT
    inverse = 10000.0 ** (-exponents)
    angles = positions.astype(jnp.float32)[:, None] * inverse[None, :]
    angles = jnp.concatenate([angles, angles], -1)[:, None, :]
    return (jnp.cos(angles), jnp.sin(angles))

def layout_positions(pairing):
    total_blocks = 2 * N_CTX
    seq_blocks = jnp.stack([pairing, total_blocks - 1 - pairing], 1).reshape(-1).astype(jnp.int32)
    offsets = jnp.arange(BLK, dtype=jnp.int32)
    return (seq_blocks[:, None] * BLK + offsets[None, :]).reshape(-1).astype(jnp.int32)

def attention(queries, key_rows, value_rows, positions):
    length = queries.shape[0]
    block_size = min(512, length)
    block_count = length // block_size
    query_blocks = queries.reshape(block_count, block_size, HEADS, HD)
    query_pos = positions.reshape(block_count, block_size)

    def one_block(inputs):
        query_block, block_pos = inputs
        scores = low_back(jnp.einsum('qhd,khd->hqk', query_block, key_rows, precision=lax.Precision.HIGHEST, preferred_element_type=jnp.float32))
        allowed = positions[None, None, :] <= block_pos[None, :, None]
        scores = jnp.where(allowed, scores, -jnp.inf)
        attn_probs = low(jax.nn.softmax(scores, axis=-1))
        return jnp.einsum('hqk,khd->qhd', attn_probs, value_rows, precision=lax.Precision.HIGHEST, preferred_element_type=jnp.float32)
    outputs = lax.map(jax.checkpoint(one_block), (query_blocks, query_pos))
    return outputs.reshape(length, HEADS * HD)

def sequence_layer(inputs, params, positions, cosine, sine_table):
    first_gain, first_shift, qkv_weight, qkv_bias, dense_weight, second_gain, second_shift, up_weight, up_bias, down_weight, out_bias = params
    length = inputs.shape[0]
    normed_one = low(layer_norm(inputs, first_gain, first_shift))
    mixed = low_back(product(normed_one, qkv_weight) + qkv_bias)
    query_raw = mixed[:, :D].reshape(length, HEADS, HD)
    key_raw = mixed[:, D:2 * D].reshape(length, HEADS, HD)
    value_raw = mixed[:, 2 * D:].reshape(length, HEADS, HD)
    queries = low(rotate(query_raw, cosine, sine_table) * HD ** (-0.5))
    key_rows = low(rotate(key_raw, cosine, sine_table))
    value_rows = low(value_raw)
    attended = attention(queries, key_rows, value_rows, positions)
    attended = low(low_back(attended))
    normed_two = low(layer_norm(inputs, second_gain, second_shift))
    upper_rows = low_back(product(normed_two, up_weight) + up_bias)
    activated = low(jax.nn.gelu(upper_rows, approximate=False))
    return inputs + product(attended, dense_weight) + product(activated, down_weight) + out_bias

def reference(tokens, cotangent, pairing, first_gain, first_shift, qkv_weight, qkv_bias, dense_weight, second_gain, second_shift, up_weight, up_bias, down_weight, out_bias):
    positions = layout_positions(pairing)
    cosine, sine_table = rotary_tables(positions)
    params = (first_gain.astype(jnp.float32), first_shift.astype(jnp.float32), qkv_weight.astype(jnp.float32), qkv_bias.astype(jnp.float32), dense_weight.astype(jnp.float32), second_gain.astype(jnp.float32), second_shift.astype(jnp.float32), up_weight.astype(jnp.float32), up_bias.astype(jnp.float32), down_weight.astype(jnp.float32), out_bias.astype(jnp.float32))

    def all_sequences(inputs, weights_in):
        return lax.map(lambda seq_rows: sequence_layer(seq_rows, weights_in, positions, cosine, sine_table), inputs)
    result, backward = jax.vjp(all_sequences, tokens.astype(jnp.float32), params)
    input_grad, param_grads = backward(cotangent.astype(jnp.float32))
    gain_one_grad, shift_one_grad, qkv_grad, qkv_offset_grad, dense_grad, gain_two_grad, shift_two_grad, up_grad, up_offset_grad, down_grad, out_offset_grad = param_grads
    return (result.astype(jnp.bfloat16), input_grad.astype(jnp.bfloat16), gain_one_grad, shift_one_grad, qkv_grad, qkv_offset_grad, dense_grad, gain_two_grad, shift_two_grad, up_grad, up_offset_grad, down_grad, out_offset_grad)
```

```python
import functools

import jax
import jax.numpy as jnp
from jax import lax
from jax.experimental import pallas as pl
from jax.experimental.pallas import tpu as pltpu
from jax.sharding import PartitionSpec as P

G = 3; BLK = 128; LOG2E = 1.4426950408889634
NEG = -1e30

def attn_kernel(chunk, qpos, lay, qdo, kv_hbm, odq, dkv_hbm, kv, kvt, acc, stage, sem, osem):
    blocks = chunk // BLK
    nblk = kv.shape[0] // BLK
    f32, bf = jnp.float32, jnp.bfloat16

    def load(i, _):
        pltpu.make_async_copy(kv_hbm.at[pl.ds(pl.multiple_of(lay[i] * BLK, BLK), BLK)], kv.at[pl.ds(pl.multiple_of(i * BLK, BLK), BLK)], sem.at[i]).start()
        return 0
    lax.fori_loop(0, nblk, load, 0)

    def land(i, _):
        rows = pl.ds(pl.multiple_of(i * BLK, BLK), BLK)
        pltpu.make_async_copy(kv_hbm.at[pl.ds(0, BLK)], kv.at[rows], sem.at[i]).wait()
        acc[rows] = jnp.zeros((BLK, G * 128), f32)
        kvt[:, rows] = kv[rows].T
        return 0
    lax.fori_loop(0, nblk, land, 0)

    upper = lax.broadcasted_iota(jnp.int32, (128, 128), 0) < 64
    left = lax.broadcasted_iota(jnp.int32, (128, 128), 1) < 64

    def q_block(i, _):
        b = qpos[i]
        qrows = pl.ds(pl.multiple_of(i * BLK, BLK), BLK)
        last = b // blocks
        pairs = [qdo[qrows, h * 128:(h + 1) * 128] for h in range(G)]
        turned = [p.astype(f32).T for p in pairs]
        q_side = [jnp.where(upper, t, 0.0).astype(bf) for t in turned]
        wide = [jnp.concatenate([q_side[h], jnp.where(upper, 0.0, turned[h]).astype(bf)], 1) for h in range(G)]
        key_i = lax.broadcasted_iota(jnp.int32, (chunk, BLK), 0)
        row_i = lax.broadcasted_iota(jnp.int32, (chunk, BLK), 1) + (b - last * blocks) * BLK

        def fwd(c, state, masked):
            at = pl.ds(pl.multiple_of(c * chunk, chunk), chunk)
            out = []
            for h in range(G):
                m, l, o = state[h]
                s = jnp.dot(kv[at, h * 128:(h + 1) * 128], q_side[h], preferred_element_type=f32)
                if masked:
                    s = jnp.where(key_i <= row_i, s, NEG)
                new = jnp.maximum(m, jnp.max(s, 0, keepdims=True))
                p = jnp.exp(s - new)
                a = jnp.exp(m - new)
                l = l * a + jnp.sum(p, 0, keepdims=True)
                o = o * a + jnp.dot(kvt[h * 128 + 64:(h + 1) * 128, at], p.astype(bf), preferred_element_type=f32)
                out.append((new, l, o))
            return tuple(out)

        state = tuple((jnp.full((1, BLK), NEG, f32), jnp.zeros((1, BLK), f32), jnp.zeros((64, BLK), f32)) for _ in range(G))
        state = lax.fori_loop(0, last, lambda c, s: fwd(c, s, False), state)
        state = fwd(last, state, True)
        lse, delta, outs = [], [], []
        for h in range(G):
            m, l, o = state[h]
            o = o / l
            outs.append(o)
            lse.append(m + jnp.log(l))
            delta.append(jnp.sum(o * turned[h][64:], 0, keepdims=True))
        narrow = [jnp.concatenate([jnp.where(left, pairs[h], jnp.zeros_like(pairs[h])), jnp.where(left, jnp.zeros_like(pairs[h]), pairs[h])], 0) for h in range(G)]

        def bwd(c, state, masked):
            at = pl.ds(pl.multiple_of(c * chunk, chunk), chunk)
            out = []
            for h in range(G):
                cols = slice(h * 128, (h + 1) * 128)
                both = jnp.dot(kv[at, cols], wide[h], preferred_element_type=f32)
                p = jnp.exp(both[:, :128] - lse[h])
                if masked:
                    p = jnp.where(key_i <= row_i, p, 0.0)
                ds = (p * (both[:, 128:] - delta[h])).astype(bf)
                pair = jnp.concatenate([ds, p.astype(bf)], 1)
                acc[at, cols] += jnp.dot(pair, narrow[h], preferred_element_type=f32)
                out.append(state[h] + jnp.dot(kvt[h * 128:h * 128 + 64, at], ds, preferred_element_type=f32))
            return tuple(out)

        dq = tuple(jnp.zeros((64, BLK), f32) for _ in range(G))
        dq = lax.fori_loop(0, last, lambda c, s: bwd(c, s, False), dq)
        dq = bwd(last, dq, True)
        for h in range(G):
            odq[qrows, h * 128:(h + 1) * 128] = jnp.concatenate([outs[h], dq[h]], 0).T.astype(bf)
        return 0
    lax.fori_loop(0, qpos.shape[0], q_block, 0)

    def send(i, _):
        slot = lax.rem(i, 8)
        @pl.when(i >= 8)
        def _():
            pltpu.make_async_copy(stage.at[slot], dkv_hbm.at[pl.ds(0, BLK)], osem.at[slot]).wait()
        stage[slot] = acc[pl.ds(pl.multiple_of(i * BLK, BLK), BLK)].astype(bf)
        pltpu.make_async_copy(stage.at[slot], dkv_hbm.at[pl.ds(pl.multiple_of(lay[i] * BLK, BLK), BLK)], osem.at[slot]).start()
        return 0
    lax.fori_loop(0, nblk, send, 0)
    for slot in range(8):
        pltpu.make_async_copy(stage.at[slot], dkv_hbm.at[pl.ds(0, BLK)], osem.at[slot]).wait()

def attention(qpos, lay, qdo, kv, chunk=1024):
    n = kv.shape[0]
    smem = pl.BlockSpec(memory_space=pltpu.SMEM)
    vmem = pl.BlockSpec(memory_space=pltpu.VMEM)
    hbm = pl.BlockSpec(memory_space=pl.ANY)
    return pl.pallas_call(
        functools.partial(attn_kernel, chunk),
        out_shape=(jax.ShapeDtypeStruct(qdo.shape, jnp.bfloat16), jax.ShapeDtypeStruct(kv.shape, jnp.bfloat16)),
        in_specs=[smem, smem, vmem, hbm], out_specs=(vmem, hbm),
        scratch_shapes=[pltpu.VMEM((n, G * 128), jnp.bfloat16), pltpu.VMEM((G * 128, n), jnp.bfloat16),
            pltpu.VMEM((n, G * 128), jnp.float32), pltpu.VMEM((8, BLK, G * 128), jnp.bfloat16),
            pltpu.SemaphoreType.DMA((n // BLK,)), pltpu.SemaphoreType.DMA((8,))],
        compiler_params=pltpu.CompilerParams(vmem_limit_bytes=56 * 2**20),
        name="attention",
    )(qpos, lay, qdo, kv)


MESH = pl.DeviceIdType.MESH
ROWS, WIDE = 256, 384


def place():
    c, w = lax.axis_index("ctx"), lax.axis_index("wsh")
    return c // 8, lax.rem(c // 4, 2), lax.rem(c, 4), w // 2, lax.rem(w, 2)


def device(z, yl, x, yh, core):
    return (z * 8 + yl * 4 + x, yh * 2 + core)


def greet(devices, extra=None, extra_count=0):
    barrier = pltpu.get_barrier_semaphore()
    for d in devices:
        pl.semaphore_signal(barrier, inc=1, device_id=d, device_id_type=MESH)
    if extra is not None:
        @pl.when(extra_count == 1)
        def _():
            pl.semaphore_signal(barrier, inc=1, device_id=extra, device_id_type=MESH)
    pl.semaphore_wait(barrier, len(devices) + extra_count)


def landed(ref, sem):
    pltpu.make_async_copy(ref, ref, sem).wait()


def spread_kernel(kvs, qds, kv_all, qdo, kv_send, kv_recv, q_send, q_recv, z_send, z_recv, half_send, half_recv, sib_send, sib_recv):
    z, yl, x, yh, core = place()
    swap = yl != core
    partner = [device(z, core, lax.rem(x + d, 4), yh, yl) for d in range(4)]
    up = device(lax.rem(z + 1, 4), yl, x, yh, core)
    down = device(lax.rem(z + 3, 4), yl, x, yh, core)
    sib = device(z, yl, x, yh, 1 - core)
    greet(partner[1:] + [up, down, sib], partner[0], lax.rem(yl + core, 2))

    def slot(zz, cc, d):
        return kv_all.at[lax.rem(zz, 4) * 8 + cc * 4 + lax.rem(x + 4 - d, 4)]

    def remote(src, dst, send, recv, to):
        copy = pltpu.make_async_remote_copy(src_ref=src, dst_ref=dst, send_sem=send, recv_sem=recv, device_id=to, device_id_type=MESH)
        copy.start()
        return copy

    def exchange(src, dst_of, send, recv):
        sent = [None] * 4
        for d in (0, 2, 1, 3):
            h = lax.rem(x + d, 4)
            args = (src.at[h], dst_of, send.at[d], recv.at[d], partner[d])
            if d == 0:
                @pl.when(swap)
                def _():
                    remote(*args)
                @pl.when(jnp.logical_not(swap))
                def _():
                    pltpu.make_async_copy(args[0], args[1], args[3]).start()
            else:
                remote(*args)
            sent[d] = pltpu.make_async_remote_copy(src_ref=args[0], dst_ref=args[1], send_sem=args[2], recv_sem=args[3], device_id=args[4], device_id_type=MESH)
        return sent

    waits = []
    mine = z * 8 + yl * 4 + x
    sent_kv = exchange(kvs, kv_all.at[mine], kv_send, kv_recv)
    sent_q = exchange(qds, qdo.at[x], q_send, q_recv)
    for d in (0, 1, 3, 2):
        here = slot(z, core, d)
        landed(here, kv_recv.at[d])
        waits.append(remote(here, here, z_send.at[0, d], z_recv.at[0, d], up))
        waits.append(remote(here, here, z_send.at[1, d], z_recv.at[1, d], down))
        waits.append(remote(here, here, sib_send.at[0, d], sib_recv.at[0, d], sib))
    half = ROWS // 2
    for d in (0, 1, 3, 2):
        for way, zz, to in ((0, z + 3, up), (1, z + 1, down)):
            here = slot(zz, core, d)
            landed(here, z_recv.at[way, d])
            part = here.at[pl.ds(way * half, half)]
            waits.append(remote(part, part, half_send.at[way, d], half_recv.at[way, d], to))
            waits.append(remote(here, here, sib_send.at[1 + way, d], sib_recv.at[1 + way, d], sib))
    for d in (0, 1, 3, 2):
        for way in (0, 1):
            part = slot(z + 2, core, d).at[pl.ds(way * half, half)]
            landed(part, half_recv.at[way, d])
            waits.append(remote(part, part, sib_send.at[3 + way, d], sib_recv.at[3 + way, d], sib))
    other = 1 - core
    for d in range(4):
        landed(slot(z, other, d), sib_recv.at[0, d])
        landed(slot(z + 3, other, d), sib_recv.at[1, d])
        landed(slot(z + 1, other, d), sib_recv.at[2, d])
        for way in (0, 1):
            landed(slot(z + 2, other, d).at[pl.ds(way * half, half)], sib_recv.at[3 + way, d])
        landed(qdo.at[lax.rem(x + 4 - d, 4)], q_recv.at[d])
    for copy in waits:
        copy.wait_send()
    for sent in (sent_kv, sent_q):
        for d in range(4):
            if d == 0:
                @pl.when(swap)
                def _():
                    sent[d].wait_send()
            else:
                sent[d].wait_send()


def spread(kvs, qds, collective_id=0):
    hbm = pl.BlockSpec(memory_space=pl.ANY)
    dma = pltpu.SemaphoreType.DMA
    return pl.pallas_call(
        spread_kernel,
        out_shape=(jax.ShapeDtypeStruct((32, ROWS, WIDE), jnp.bfloat16), jax.ShapeDtypeStruct((4, ROWS, WIDE), jnp.bfloat16)),
        in_specs=[hbm, hbm], out_specs=(hbm, hbm),
        scratch_shapes=[dma((4,)), dma((4,)), dma((4,)), dma((4,)), dma((2, 4)), dma((2, 4)), dma((2, 4)), dma((2, 4)), dma((5, 4)), dma((5, 4))],
        compiler_params=pltpu.CompilerParams(collective_id=collective_id, has_side_effects=True),
        name="spread",
    )(kvs, qds)


def collect_kernel(odq, dkv, odq_own, dkv_own, own, sib_in, far_in, near_out, near_in, done,
                   load_sem, o_send, o_recv, sib_send, sib_recv, far_send, far_recv, near_send, near_recv, g_send, g_recv):
    z, yl, x, yh, core = place()
    swap = yl != core
    partner = [device(z, core, lax.rem(x + d, 4), yh, yl) for d in range(4)]
    up = device(lax.rem(z + 1, 4), yl, x, yh, core)
    down = device(lax.rem(z + 3, 4), yl, x, yh, core)
    sib = device(z, yl, x, yh, 1 - core)
    greet(partner[1:] + [up, down, sib], partner[0], lax.rem(yl + core, 2))
    f32, bf = jnp.float32, jnp.bfloat16

    def remote(src, dst, send, recv, to):
        copy = pltpu.make_async_remote_copy(src_ref=src, dst_ref=dst, send_sem=send, recv_sem=recv, device_id=to, device_id_type=MESH)
        copy.start()
        return copy

    def exchange(src, dst_of, send, recv, d):
        args = (src.at[lax.rem(x + d, 4)], dst_of, send.at[d], recv.at[d], partner[d])
        if d == 0:
            @pl.when(swap)
            def _():
                remote(*args)
            @pl.when(jnp.logical_not(swap))
            def _():
                pltpu.make_async_copy(args[0], args[1], args[3]).start()
        else:
            remote(*args)
        return pltpu.make_async_remote_copy(src_ref=args[0], dst_ref=args[1], send_sem=args[2], recv_sem=args[3], device_id=args[4], device_id_type=MESH)

    def group(zz, cc):
        return dkv.at[pl.ds(lax.rem(zz, 4) * 8 + cc * 4, 4)]

    waits, loads = [], []
    order = (z + 2, z + 1, z + 3, z)
    for k, zz in enumerate(order):
        waits.append(remote(group(zz, 1 - core), sib_in.at[k], sib_send.at[k], sib_recv.at[k], sib))
        load = pltpu.make_async_copy(group(zz, core), own.at[k], load_sem.at[k])
        load.start()
        loads.append(load)
    sent_o = [exchange(odq, odq_own.at[x], o_send, o_recv, d) for d in range(4)]

    def add(first, k, also=()):
        def step(i, _):
            j, r = i // 2, pl.ds(pl.multiple_of(lax.rem(i, 2) * 128, 128), 128)
            total = own[k, j, r].astype(f32) + sib_in[k, j, r].astype(f32)
            for ref, low, high in also:
                if (low, high) == (0, 4):
                    total = total + ref[j, r].astype(f32)
            first[j, r] = total.astype(bf)
            return 0
        lax.fori_loop(0, 8, step, 0)

    loads[0].wait()
    landed(sib_in.at[0], sib_recv.at[0])
    add(done, 0)
    for way, to in ((0, up), (1, down)):
        waits.append(remote(done.at[pl.ds(2 * way, 2)], far_in.at[way], far_send.at[way], far_recv.at[way], to))
    for way, to in ((0, up), (1, down)):
        k = 1 + way
        loads[k].wait()
        landed(sib_in.at[k], sib_recv.at[k])
        add(near_out.at[way], k)
        landed(far_in.at[way], far_recv.at[way])

        def more(i, _):
            j, r = i // 2, pl.ds(pl.multiple_of(lax.rem(i, 2) * 128, 128), 128)
            near_out[way, 2 * way + j, r] = (own[k, 2 * way + j, r].astype(f32) + sib_in[k, 2 * way + j, r].astype(f32) + far_in[way, j, r].astype(f32)).astype(bf)
            return 0
        lax.fori_loop(0, 4, more, 0)
        waits.append(remote(near_out.at[way], near_in.at[way], near_send.at[way], near_recv.at[way], to))
    loads[3].wait()
    landed(sib_in.at[3], sib_recv.at[3])
    for way in (0, 1):
        landed(near_in.at[way], near_recv.at[way])
    for copy in waits[4:6]:
        copy.wait_send()
    sent_g = []
    for d in range(4):
        j = lax.rem(x + d, 4)
        done[j] = (own[3, j].astype(f32) + sib_in[3, j].astype(f32) + near_in[0, j].astype(f32) + near_in[1, j].astype(f32)).astype(bf)
        sent_g.append(exchange(done, dkv_own.at[x], g_send, g_recv, d))
    for d in range(4):
        h = lax.rem(x + 4 - d, 4)
        landed(odq_own.at[h], o_recv.at[d])
        landed(dkv_own.at[h], g_recv.at[d])
    for i, copy in enumerate(waits):
        if i not in (4, 5):
            copy.wait_send()
    for sent in (sent_o, sent_g):
        for d in range(4):
            if d == 0:
                @pl.when(swap)
                def _():
                    sent[d].wait_send()
            else:
                sent[d].wait_send()


def collect(odq, dkv, collective_id=1):
    hbm = pl.BlockSpec(memory_space=pl.ANY)
    dma = pltpu.SemaphoreType.DMA
    bf = jnp.bfloat16
    one = jax.ShapeDtypeStruct((4, ROWS, WIDE), bf)
    return pl.pallas_call(
        collect_kernel,
        out_shape=(one, one),
        in_specs=[hbm, hbm], out_specs=(hbm, hbm),
        scratch_shapes=[pltpu.VMEM((4, 4, ROWS, WIDE), bf), pltpu.VMEM((4, 4, ROWS, WIDE), bf), pltpu.VMEM((2, 2, ROWS, WIDE), bf),
            pltpu.VMEM((2, 4, ROWS, WIDE), bf), pltpu.VMEM((2, 4, ROWS, WIDE), bf), pltpu.VMEM((4, ROWS, WIDE), bf),
            dma((4,)), dma((4,)), dma((4,)), dma((4,)), dma((4,)), dma((2,)), dma((2,)), dma((2,)), dma((2,)), dma((4,)), dma((4,))],
        compiler_params=pltpu.CompilerParams(collective_id=collective_id, has_side_effects=True, vmem_limit_bytes=40 * 2**20),
        name="collect",
    )(odq, dkv)


PARTS = ((192, 768, True), (192, 768, False), (192, 384, True), (192, 384, False), (64, 128, True))


def reduce_kernel(wide, upper, lower, tiny, *refs):
    outs, refs = refs[:5], refs[5:]
    own, sib_in, far_in, near_in, far_two, near_two, y_in = (refs[5 * i : 5 * i + 5] for i in range(7))
    load_sem, send_sem, recv_sem = refs[35:]
    z, yl, x, yh, core = place()
    f32, bf = jnp.float32, jnp.bfloat16
    xs = [device(z, yl, lax.rem(x + d, 4), yh, core) for d in (1, 3)]
    zs = [device(lax.rem(z + d, 4), yl, x, yh, core) for d in (1, 3)]
    ys = [device(z, 1 - yl, x, yh, core), device(z, yl, x, 1 - yh, core), device(z, 1 - yl, x, 1 - yh, core)]
    sib = device(z, yl, x, yh, 1 - core)
    greet([sib] + xs + zs + ys)
    count = [0]
    sent = []

    def remote(src, dst, to, sem=None):
        if sem is None:
            sem = count[0]
            count[0] += 1
        copy = pltpu.make_async_remote_copy(src_ref=src, dst_ref=dst, send_sem=send_sem.at[sem], recv_sem=recv_sem.at[sem], device_id=to, device_id_type=MESH)
        copy.start()
        sent.append((src, sem, copy))
        return sem

    def arrive(ref, sem):
        landed(ref, recv_sem.at[sem])

    def piece(p, w, a):
        if p < 2:
            return (wide, upper)[p].at[pl.ds(pl.multiple_of(w * 192, 192), 192), pl.ds(pl.multiple_of(a * 768, 768), 768)]
        if p < 4:
            return lower.at[pl.ds(pl.multiple_of(w * 768 + a * 192, 192), 192), pl.ds(384 * (p - 2), 384)]
        return tiny.at[w, a]

    first = [x if part[2] else z for part in PARTS]
    second = [z if part[2] else x for part in PARTS]
    ring_one = [xs if part[2] else zs for part in PARTS]
    ring_two = [zs if part[2] else xs for part in PARTS]
    everyone = range(5)

    sib_sem = {}
    pairs = []
    for k, ahead in enumerate((2, 1, 3, 0)):
        for p in everyone:
            a = lax.rem(first[p] + ahead, 4)
            sem = count[0]
            count[0] += 1
            sib_sem[p, k] = sem
            for s in (0, 1):
                pltpu.make_async_copy(piece(p, 2 * s + core, a), own[p].at[k, s], load_sem.at[p * 4 + k]).start()
                pltpu.make_async_remote_copy(src_ref=piece(p, 2 * s + 1 - core, a), dst_ref=sib_in[p].at[k, s], send_sem=send_sem.at[sem], recv_sem=recv_sem.at[sem], device_id=sib, device_id_type=MESH).start()
            pairs.append((sib_in[p].at[k], sem))

    def gather_one(p, k):
        landed(own[p].at[k], load_sem.at[p * 4 + k])
        arrive(sib_in[p].at[k], sib_sem[p, k])

    def add(p, rows, into, terms):
        step = 16 if PARTS[p][1] > 384 or rows % 32 else 32

        def body(i, _):
            at = pl.ds(pl.multiple_of(i * step, step), step)
            total = into[at].astype(f32)
            for term in terms:
                total = total + term[at].astype(f32)
            into[at] = total.astype(bf)
            return 0
        lax.fori_loop(0, rows // step, body, 0)

    far_sem, near_sem = {}, {}
    for p in everyone:
        gather_one(p, 0)
        for s in (0, 1):
            add(p, PARTS[p][0], own[p].at[0, s], [sib_in[p].at[0, s]])
            far_sem[p, s] = remote(own[p].at[0, s], far_in[p].at[s], ring_one[p][s])
    for way in (0, 1):
        for p in everyone:
            k = 1 + way
            gather_one(p, k)
            add(p, PARTS[p][0], own[p].at[k, 1 - way], [sib_in[p].at[k, 1 - way]])
            arrive(far_in[p].at[way], far_sem[p, way])
            add(p, PARTS[p][0], own[p].at[k, way], [sib_in[p].at[k, way], far_in[p].at[way]])
            near_sem[p, way] = remote(own[p].at[k], near_in[p].at[way], ring_one[p][way])

    def quarter(p, b):
        rows = PARTS[p][0] // 4
        return pl.ds(pl.multiple_of(lax.rem(b, 4) * rows, rows), rows)

    far_sem2, near_sem2, y_sem = {}, {}, {}
    for p in everyone:
        gather_one(p, 3)
        for way in (0, 1):
            arrive(near_in[p].at[way], near_sem[p, way])
        for s in (0, 1):
            add(p, PARTS[p][0], own[p].at[3, s], [sib_in[p].at[3, s], near_in[p].at[0, s], near_in[p].at[1, s]])
        at = quarter(p, second[p] + 2)
        for s in (0, 1):
            far_sem2[p, s] = remote(own[p].at[3, s, at], far_two[p].at[s], ring_two[p][s])
    for way in (0, 1):
        for p in everyone:
            at = quarter(p, second[p] + 1 + 2 * way)
            arrive(far_two[p].at[way], far_sem2[p, way])
            add(p, PARTS[p][0] // 4, own[p].at[3, way, at], [far_two[p].at[way]])
            near_sem2[p, way] = remote(own[p].at[3, :, at], near_two[p].at[way], ring_two[p][way])
    for p in everyone:
        at = quarter(p, second[p])
        for way in (0, 1):
            arrive(near_two[p].at[way], near_sem2[p, way])
        for s in (0, 1):
            add(p, PARTS[p][0] // 4, own[p].at[3, s, at], [near_two[p].at[0, s], near_two[p].at[1, s]])
        for i, half in enumerate((yh, 1 - yh, 1 - yh)):
            y_sem[p, i] = remote(own[p].at[3, half, at], y_in[p].at[i], ys[i])
    ring_sem = {}
    for p in everyone:
        at = quarter(p, second[p])
        for i in range(3):
            arrive(y_in[p].at[i], y_sem[p, i])
        rows = PARTS[p][0] // 4
        total = own[p][3, yh, at].astype(f32)
        for i in range(3):
            total = total + y_in[p][i].astype(f32)
        outs[p][first[p], at] = total.astype(bf)
        mine = outs[p].at[first[p], at]
        for way in (0, 1):
            ring_sem[p, way] = remote(mine, mine, ring_two[p][way])

    relay_sem = {}
    for way in (0, 1):
        for p in everyone:
            b = lax.rem(second[p] + 3 - 2 * way, 4)
            arrive(outs[p].at[first[p], quarter(p, b)], ring_sem[p, way])
            rows = PARTS[p][0] // 4
            low, high = ((0, 32), (32, 48))[way] if rows == 48 else ((0, 16), (16, 16))[way]
            if high > low:
                part = outs[p].at[first[p], pl.ds(pl.multiple_of(b * rows + low, 16), high - low)]
                relay_sem[p, way] = (remote(part, part, ring_two[p][way]), low, high)
    last_sem = {}
    for p in everyone:
        rows = PARTS[p][0] // 4
        b = lax.rem(second[p] + 2, 4)
        for way in (0, 1):
            if (p, way) in relay_sem:
                sem, low, high = relay_sem[p, way]
                arrive(outs[p].at[first[p], pl.ds(pl.multiple_of(b * rows + low, 16), high - low)], sem)
        mine = outs[p].at[first[p]]
        for way in (0, 1):
            last_sem[p, way] = remote(mine, mine, ring_one[p][way])
    end_sem = {}
    for way in (0, 1):
        for p in everyone:
            block = outs[p].at[lax.rem(first[p] + 3 - 2 * way, 4)]
            arrive(block, last_sem[p, way])
            half = PARTS[p][0] // 2
            part = block.at[pl.ds(way * half, half)]
            end_sem[p, way] = remote(part, part, ring_one[p][way])
    for way in (0, 1):
        for p in everyone:
            half = PARTS[p][0] // 2
            arrive(outs[p].at[lax.rem(first[p] + 2, 4)].at[pl.ds(way * half, half)], end_sem[p, way])
    for ref, sem in pairs:
        landed(ref, send_sem.at[sem])
    for src, sem, copy in sent:
        copy.wait_send()


def reduce_all(wide, upper, lower, tiny, collective_id=2):
    hbm = pl.BlockSpec(memory_space=pl.ANY)
    vmem = pl.BlockSpec(memory_space=pltpu.VMEM)
    dma = pltpu.SemaphoreType.DMA
    bf = jnp.bfloat16
    scratch = []
    for lead in ((4, 2, 1), (4, 2, 1), (2, 0, 1), (2, 2, 1), (2, 0, 4), (2, 2, 4), (3, 0, 4)):
        for rows, columns, _ in PARTS:
            front = tuple(n for n in lead[:2] if n)
            scratch.append(pltpu.VMEM(front + (rows // lead[2], columns), bf))
    return pl.pallas_call(
        reduce_kernel,
        out_shape=tuple(jax.ShapeDtypeStruct((4, rows, columns), bf) for rows, columns, _ in PARTS),
        in_specs=[hbm] * 4, out_specs=(vmem,) * 5,
        scratch_shapes=scratch + [dma((20,)), dma((140,)), dma((140,))],
        compiler_params=pltpu.CompilerParams(collective_id=collective_id, has_side_effects=True, vmem_limit_bytes=50 * 2**20),
        name="reduce",
    )(wide, upper, lower, tiny)


def sum_gradients(gain_one, shift_one, qkv, qkv_bias, dense, gain_two, shift_two, up, up_bias, down, out_bias):
    bf, f32 = jnp.bfloat16, jnp.float32
    small = (gain_one, shift_one, gain_two, shift_two, out_bias, qkv_bias, up_bias)
    flat = jnp.concatenate([v.reshape(4, -1) for v in small], 1).astype(bf)
    tiny = jnp.pad(flat.reshape(4, 16, 144), ((0, 0), (0, 0), (0, 2048 - 144))).reshape(4, 4, 64, 128)
    wide = jnp.concatenate([qkv.astype(bf), dense.astype(bf)], 1)
    wide, upper, left, right, tiny = reduce_all(wide, up.astype(bf), down.astype(bf), tiny)
    wide = wide.astype(f32).transpose(1, 0, 2).reshape(192, 3072)
    upper = upper.astype(f32).transpose(1, 0, 2).reshape(192, 3072)
    lower = jnp.concatenate([left.astype(f32), right.astype(f32)], 2).reshape(768, 768)
    flat = tiny.astype(f32).reshape(16, 2048)[:, :144].reshape(-1)
    parts, start = [], 0
    for v in small:
        parts.append(flat[start : start + v.shape[0] // 4])
        start += v.shape[0] // 4
    gain_one, shift_one, gain_two, shift_two, out_bias, qkv_bias, up_bias = parts
    return gain_one, shift_one, wide[:, :2304], qkv_bias, wide[:, 2304:], gain_two, shift_two, upper, up_bias, lower, out_bias


D = 768
HEADS = 12
HD = 64
ROT = 16
TOK_DEV = 256


def layer_norm(values, norm_gain, norm_shift):
    row_mean = jnp.mean(values, -1, keepdims=True)
    centered = values - row_mean
    row_var = jnp.mean(centered * centered, -1, keepdims=True)
    return centered * lax.rsqrt(row_var + 1e-05) * norm_gain + norm_shift


def rotary_tables(positions):
    half_dims = ROT // 2
    exponents = jnp.arange(half_dims).astype(jnp.float32) * 2.0 / ROT
    inverse = 10000.0 ** (-exponents)
    angles = positions.astype(jnp.float32)[:, None] * inverse[None, :]
    cosine, sine = jnp.cos(angles), jnp.sin(angles)
    rest = jnp.ones((positions.shape[0], HD - ROT), jnp.float32)
    none = jnp.zeros((positions.shape[0], half_dims), jnp.float32)
    keep = jnp.concatenate([cosine, cosine, rest], 1)
    ahead = jnp.concatenate([-sine, none, 0.0 * rest], 1)
    behind = jnp.concatenate([none, sine, 0.0 * rest], 1)
    return tuple(jnp.tile(table, (1, HEADS)) for table in (keep, ahead, behind))


def rotate(rows, tables):
    keep, ahead, behind = tables
    return rows * keep + jnp.roll(rows, -8, 1) * ahead + jnp.roll(rows, 8, 1) * behind


def rotate_back(rows, tables):
    keep, ahead, behind = tables
    return rows * keep + jnp.roll(rows * ahead, 8, 1) + jnp.roll(rows * behind, -8, 1)


def contract(left_side, right_side, left_dim, right_dim):
    return lax.dot_general(
        left_side,
        right_side,
        (((left_dim,), (right_dim,)), ((), ())),
        preferred_element_type=jnp.float32,
    )


def gelu_exact(values):
    return jax.nn.gelu(values, approximate=False)


def slabs(first, second):
    both = jnp.stack([first.reshape(TOK_DEV, HEADS, HD), second.reshape(TOK_DEV, HEADS, HD)], 2)
    return both.reshape(TOK_DEV, 4, WIDE).transpose(1, 0, 2)


def unslab(pairs):
    both = pairs.transpose(1, 0, 2).reshape(TOK_DEV, HEADS, 2, HD)
    return both[:, :, 0].reshape(TOK_DEV, D), both[:, :, 1].reshape(TOK_DEV, D)


def on_device(
    tokens, cotangent, pairing, first_gain, first_shift, qkv_weight, qkv_bias, dense_weight,
    second_gain, second_shift, up_weight, up_bias, down_weight, out_bias,
):
    bf, f32 = jnp.bfloat16, jnp.float32
    total_blocks = 64
    offsets = jnp.arange(BLK, dtype=jnp.int32)
    ctx_index = lax.axis_index("ctx")
    core = lax.rem(lax.axis_index("wsh"), 2)
    seq_of_layout = jnp.stack([pairing, total_blocks - 1 - pairing], 1).reshape(-1)
    layout_of_seq = (
        jnp.zeros((total_blocks,), jnp.int32)
        .at[seq_of_layout]
        .set(jnp.arange(total_blocks, dtype=jnp.int32))
    )
    own_blocks = lax.dynamic_slice(seq_of_layout, (2 * ctx_index,), (2,))
    row_blocks = lax.dynamic_slice(seq_of_layout, (16 * (ctx_index // 8) + 8 * core,), (8,))
    local_pos = (own_blocks[:, None] * BLK + offsets[None, :]).reshape(-1)
    tables = rotary_tables(local_pos)
    query_scale = HD ** (-0.5)

    small = (first_gain, first_shift, second_gain, second_shift, out_bias, qkv_bias, up_bias)
    sizes = [v.shape[0] for v in small]
    gathered = lax.all_gather(jnp.concatenate(small), "wsh", axis=0)
    vectors, start = [], 0
    for size in sizes:
        vectors.append(gathered[:, start : start + size].reshape(-1).astype(f32))
        start += size
    gain_one, shift_one, gain_two, shift_two, out_offset, qkv_offset, up_offset = vectors
    qkv_matrix = lax.all_gather(qkv_weight, "wsh", axis=0, tiled=True)
    dense_matrix = lax.all_gather(dense_weight, "wsh", axis=0, tiled=True)
    up_matrix = lax.all_gather(up_weight, "wsh", axis=0, tiled=True)
    down_matrix = lax.all_gather(down_weight, "wsh", axis=0, tiled=True)

    inputs = tokens[0].astype(f32)
    grad_rows = cotangent[0]
    grad_float = grad_rows.astype(f32)
    normed_one = layer_norm(inputs, gain_one, shift_one).astype(bf)
    mixed = jnp.dot(normed_one, qkv_matrix, preferred_element_type=f32) + qkv_offset
    queries = (rotate(mixed[:, :D], tables) * query_scale).astype(bf)
    key_rows = rotate(mixed[:, D : 2 * D], tables).astype(bf)
    value_rows = mixed[:, 2 * D :].astype(bf)
    grad_attended = contract(grad_rows, dense_matrix, 1, 1).astype(bf)

    keys_values, queries_grads = spread(slabs(key_rows, value_rows), slabs(queries, grad_attended))
    attended_dq, grad_kv = attention(row_blocks, layout_of_seq, queries_grads.reshape(1024, WIDE), keys_values.reshape(8192, WIDE))
    attended_dq, grad_kv = collect(attended_dq.reshape(4, ROWS, WIDE), grad_kv.reshape(32, ROWS, WIDE))
    attended_low, grad_queries = unslab(attended_dq)
    grad_keys, grad_values = unslab(grad_kv)

    attention_out = jnp.dot(attended_low, dense_matrix, preferred_element_type=f32)
    normed_two = layer_norm(inputs, gain_two, shift_two).astype(bf)
    upper_rows = jnp.dot(normed_two, up_matrix, preferred_element_type=f32) + up_offset
    activated = gelu_exact(upper_rows).astype(bf)
    mlp_out = jnp.dot(activated, down_matrix, preferred_element_type=f32)
    layer_output = (inputs + attention_out + mlp_out + out_offset).astype(bf)[None]

    out_offset_grad = jnp.sum(grad_float, 0)
    dense_grad = contract(attended_low, grad_rows, 0, 0)
    down_grad = contract(activated, grad_rows, 0, 0)
    grad_activated = contract(grad_rows, down_matrix, 1, 1)
    gelu_back = jax.vjp(gelu_exact, upper_rows)[1]
    grad_upper = gelu_back(grad_activated)[0].astype(bf)
    up_grad = contract(normed_two, grad_upper, 0, 0)
    up_offset_grad = jnp.sum(grad_upper.astype(f32), 0)
    grad_normed_two = contract(grad_upper, up_matrix, 1, 1)

    grad_mixed = jnp.concatenate(
        [
            rotate_back(grad_queries.astype(f32) * query_scale, tables).astype(bf),
            rotate_back(grad_keys.astype(f32), tables).astype(bf),
            grad_values,
        ],
        1,
    )
    qkv_grad = contract(normed_one, grad_mixed, 0, 0)
    qkv_offset_grad = jnp.sum(grad_mixed.astype(f32), 0)
    grad_normed_one = contract(grad_mixed, qkv_matrix, 1, 1)
    grad_in_one, gain_one_grad, shift_one_grad = jax.vjp(layer_norm, inputs, gain_one, shift_one)[1](grad_normed_one)
    grad_in_two, gain_two_grad, shift_two_grad = jax.vjp(layer_norm, inputs, gain_two, shift_two)[1](grad_normed_two)
    input_grad = (grad_float + grad_in_one + grad_in_two).astype(bf)[None]

    return (layer_output, input_grad) + sum_gradients(
        gain_one_grad, shift_one_grad, qkv_grad, qkv_offset_grad, dense_grad, gain_two_grad, shift_two_grad,
        up_grad, up_offset_grad, down_grad, out_offset_grad,
    )


def solution(mesh):
    rows, split, flat = P("wsh", "ctx", None), P("wsh", None), P("wsh")
    return jax.shard_map(
        on_device,
        mesh=mesh,
        in_specs=(rows, rows, P(), flat, flat, split, flat, split, flat, flat, split, flat, split, flat),
        out_specs=(rows, rows, flat, flat, split, flat, split, flat, flat, split, flat, split, flat),
        check_vma=False,
    )
```

```python
import functools

import jax
import jax.numpy as jnp
from jax import lax
from jax.experimental import pallas as pl
from jax.experimental.pallas import tpu as pltpu
from jax.sharding import PartitionSpec as P

G = 3; BLK = 128; LOG2E = 1.4426950408889634
NEG = -1e30

def attn_kernel(chunk, qpos, lay, qdo, kv_hbm, odq, dkv_hbm, kv, kvt, acc, probs, grads, tops, stage, sem, osem):
    blocks = chunk // BLK
    nblk = kv.shape[0] // BLK
    f32, bf = jnp.float32, jnp.bfloat16

    def load(i, _):
        pltpu.make_async_copy(kv_hbm.at[pl.ds(pl.multiple_of(lay[i] * BLK, BLK), BLK)], kv.at[pl.ds(pl.multiple_of(i * BLK, BLK), BLK)], sem.at[i]).start()
        return 0
    lax.fori_loop(0, nblk, load, 0)

    def land(i, _):
        rows = pl.ds(pl.multiple_of(i * BLK, BLK), BLK)
        pltpu.make_async_copy(kv_hbm.at[pl.ds(0, BLK)], kv.at[rows], sem.at[i]).wait()
        acc[rows] = jnp.zeros((BLK, G * 128), f32)
        kvt[:, rows] = kv[rows].T
        return 0
    lax.fori_loop(0, nblk, land, 0)

    upper = lax.broadcasted_iota(jnp.int32, (128, 128), 0) < 64
    left = lax.broadcasted_iota(jnp.int32, (128, 128), 1) < 64

    def q_block(i, _):
        b = qpos[i]
        qrows = pl.ds(pl.multiple_of(i * BLK, BLK), BLK)
        last = b // blocks
        pairs = [qdo[qrows, h * 128:(h + 1) * 128] for h in range(G)]
        turned = [p.astype(f32).T for p in pairs]
        wide = [jnp.concatenate([jnp.where(upper, turned[h], 0.0).astype(bf), jnp.where(upper, 0.0, turned[h]).astype(bf)], 1) for h in range(G)]
        key_i = lax.broadcasted_iota(jnp.int32, (chunk, BLK), 0)
        row_i = lax.broadcasted_iota(jnp.int32, (chunk, BLK), 1) + (b - last * blocks) * BLK

        def fwd(c, state, masked):
            at = pl.ds(pl.multiple_of(c * chunk, chunk), chunk)
            out = []
            every = [jnp.dot(kv[at, h * 128:(h + 1) * 128], wide[h], preferred_element_type=f32) for h in range(G)]
            kept = []
            for h in range(G):
                m, l, o = state[h]
                s = every[h][:, :128]
                grads[at, h * 128:(h + 1) * 128] = every[h][:, 128:]
                if masked:
                    s = jnp.where(key_i <= row_i, s, NEG)
                new = jnp.maximum(m, jnp.max(s, 0, keepdims=True))
                p = jnp.exp(s - new)
                a = jnp.exp(m - new)
                l = l * a + jnp.sum(p, 0, keepdims=True)
                p = p.astype(bf)
                probs[at, h * 128:(h + 1) * 128] = p
                tops[c, h] = jnp.broadcast_to(new, (8, BLK))
                kept.append((new, l, o * a, p))
            for h in range(G):
                new, l, o, p = kept[h]
                o = o + jnp.dot(kvt[h * 128 + 64:(h + 1) * 128, at], p, preferred_element_type=f32)
                out.append((new, l, o))
            return tuple(out)

        state = tuple((jnp.full((1, BLK), NEG, f32), jnp.zeros((1, BLK), f32), jnp.zeros((64, BLK), f32)) for _ in range(G))
        state = lax.fori_loop(0, last, lambda c, s: fwd(c, s, False), state)
        state = fwd(last, state, True)
        lse, delta, outs = [], [], []
        for h in range(G):
            m, l, o = state[h]
            o = o / l
            outs.append(o)
            lse.append(m + jnp.log(l))
            delta.append(jnp.sum(o * turned[h][64:], 0, keepdims=True))
        narrow = [jnp.concatenate([jnp.where(left, pairs[h], jnp.zeros_like(pairs[h])), jnp.where(left, jnp.zeros_like(pairs[h]), pairs[h])], 0) for h in range(G)]

        def bwd(c, state):
            at = pl.ds(pl.multiple_of(c * chunk, chunk), chunk)
            out, work = [], []
            for h in range(G):
                cols = slice(h * 128, (h + 1) * 128)
                p = probs[at, cols].astype(f32) * jnp.exp(tops[c, h, 0:1] - lse[h])
                ds = (p * (grads[at, cols] - delta[h])).astype(bf)
                work.append((jnp.concatenate([ds, p.astype(bf)], 1), ds))
            for h in range(G):
                pair, ds = work[h]
                acc[at, h * 128:(h + 1) * 128] += jnp.dot(pair, narrow[h], preferred_element_type=f32)
                out.append(state[h] + jnp.dot(kvt[h * 128:h * 128 + 64, at], ds, preferred_element_type=f32))
            return tuple(out)

        dq = tuple(jnp.zeros((64, BLK), f32) for _ in range(G))
        dq = lax.fori_loop(0, last + 1, bwd, dq)
        for h in range(G):
            odq[qrows, h * 128:(h + 1) * 128] = jnp.concatenate([outs[h], dq[h]], 0).T.astype(bf)
        return 0
    lax.fori_loop(0, qpos.shape[0], q_block, 0)

    def send(i, _):
        slot = lax.rem(i, 8)
        @pl.when(i >= 8)
        def _():
            pltpu.make_async_copy(stage.at[slot], dkv_hbm.at[pl.ds(0, BLK)], osem.at[slot]).wait()
        stage[slot] = acc[pl.ds(pl.multiple_of(i * BLK, BLK), BLK)].astype(bf)
        pltpu.make_async_copy(stage.at[slot], dkv_hbm.at[pl.ds(pl.multiple_of(lay[i] * BLK, BLK), BLK)], osem.at[slot]).start()
        return 0
    lax.fori_loop(0, nblk, send, 0)
    for slot in range(8):
        pltpu.make_async_copy(stage.at[slot], dkv_hbm.at[pl.ds(0, BLK)], osem.at[slot]).wait()

def attention(qpos, lay, qdo, kv, chunk=1024):
    n = kv.shape[0]
    smem = pl.BlockSpec(memory_space=pltpu.SMEM)
    vmem = pl.BlockSpec(memory_space=pltpu.VMEM)
    hbm = pl.BlockSpec(memory_space=pl.ANY)
    return pl.pallas_call(
        functools.partial(attn_kernel, chunk),
        out_shape=(jax.ShapeDtypeStruct(qdo.shape, jnp.bfloat16), jax.ShapeDtypeStruct(kv.shape, jnp.bfloat16)),
        in_specs=[smem, smem, vmem, hbm], out_specs=(vmem, hbm),
        scratch_shapes=[pltpu.VMEM((n, G * 128), jnp.bfloat16), pltpu.VMEM((G * 128, n), jnp.bfloat16),
            pltpu.VMEM((n, G * 128), jnp.float32), pltpu.VMEM((n, G * 128), jnp.bfloat16), pltpu.VMEM((n, G * 128), jnp.float32), pltpu.VMEM((n // chunk, G, 8, BLK), jnp.float32),
            pltpu.VMEM((8, BLK, G * 128), jnp.bfloat16),
            pltpu.SemaphoreType.DMA((n // BLK,)), pltpu.SemaphoreType.DMA((8,))],
        compiler_params=pltpu.CompilerParams(vmem_limit_bytes=62 * 2**20),
        name="attention",
    )(qpos, lay, qdo, kv)


MESH = pl.DeviceIdType.MESH
ROWS, WIDE = 256, 384


def place():
    c, w = lax.axis_index("ctx"), lax.axis_index("wsh")
    return c // 8, lax.rem(c // 4, 2), lax.rem(c, 4), w // 2, lax.rem(w, 2)


def device(z, yl, x, yh, core):
    return (z * 8 + yl * 4 + x, yh * 2 + core)


def greet(devices, extra=None, extra_count=0):
    barrier = pltpu.get_barrier_semaphore()
    for d in devices:
        pl.semaphore_signal(barrier, inc=1, device_id=d, device_id_type=MESH)
    if extra is not None:
        @pl.when(extra_count == 1)
        def _():
            pl.semaphore_signal(barrier, inc=1, device_id=extra, device_id_type=MESH)
    pl.semaphore_wait(barrier, len(devices) + extra_count)


def landed(ref, sem):
    pltpu.make_async_copy(ref, ref, sem).wait()


TILE = 384


def erf(values):
    v = jnp.clip(values, -4.0, 4.0)
    s = v * v
    top = jnp.float32(-2.72614225801306e-10)
    for coefficient in (2.77068142495902e-08, -2.10102402082508e-06, -5.69250639462346e-05, -7.34990630326855e-04, -2.95459980854025e-03, -1.60960333262415e-02):
        top = top * s + coefficient
    low = jnp.float32(-1.45660718464996e-05)
    for coefficient in (-2.13374055278905e-04, -1.68282697438203e-03, -7.37332916720468e-03, -1.42647390514189e-02):
        low = low * s + coefficient
    return v * top / low


def collect_kernel(odq, dkv, normed, grad, up_hbm, up_bias, down_hbm, odq_own, dkv_own, mlp_out, back_out, up_grad, down_grad, bias_grad, own, sib_in, far_in, near_out, near_in, done,
                   load_sem, o_send, o_recv, sib_send, sib_recv, far_send, far_recv, near_send, near_recv, g_send, g_recv,
                   up, down_w, up_stage, down_stage, up_sem, down_sem, in_sem):
    z, yl, x, yh, core = place()
    swap = yl != core
    partner = [device(z, core, lax.rem(x + d, 4), yh, yl) for d in range(4)]
    above = device(lax.rem(z + 1, 4), yl, x, yh, core)
    below = device(lax.rem(z + 3, 4), yl, x, yh, core)
    sib = device(z, yl, x, yh, 1 - core)
    greet(partner[1:] + [above, below, sib], partner[0], lax.rem(yl + core, 2))
    f32, bf = jnp.float32, jnp.bfloat16
    fetch = [pltpu.make_async_copy(up_hbm, up, in_sem.at[0]), pltpu.make_async_copy(down_hbm, down_w, in_sem.at[1])]
    for copy in fetch:
        copy.start()

    def dot(left, right, left_dim, right_dim):
        return lax.dot_general(left, right, (((left_dim,), (right_dim,)), ((), ())), preferred_element_type=f32)

    def feed(t, _):
        at = pl.ds(pl.multiple_of(t * TILE, TILE), TILE)
        values = dot(normed[...], up[:, at], 1, 0) + up_bias[0:1, at]
        inner = 0.5 + 0.5 * erf(values * 0.7071067811865476)
        slope = inner + values * (0.3989422804014327 * jnp.exp(-0.5 * values * values))
        active = (values * inner).astype(bf)
        grads = (dot(grad[...], down_w[at], 1, 1) * slope).astype(bf)
        mlp_out[...] += dot(active, down_w[at], 1, 0)
        back_out[...] += dot(grads, up[:, at], 1, 1)
        bias_grad[0:1, at] = jnp.sum(grads.astype(f32), 0, keepdims=True)
        up_stage[t] = dot(normed[...], grads, 0, 0).astype(bf)
        down_stage[at] = dot(active, grad[...], 0, 0).astype(bf)
        pltpu.make_async_copy(up_stage.at[t], up_grad.at[:, at], up_sem.at[t]).start()
        pltpu.make_async_copy(down_stage.at[at], down_grad.at[at], down_sem.at[t]).start()
        return 0

    def remote(src, dst, send, recv, to):
        copy = pltpu.make_async_remote_copy(src_ref=src, dst_ref=dst, send_sem=send, recv_sem=recv, device_id=to, device_id_type=MESH)
        copy.start()
        return copy

    def exchange(src, dst_of, send, recv, d):
        args = (src.at[lax.rem(x + d, 4)], dst_of, send.at[d], recv.at[d], partner[d])
        if d == 0:
            @pl.when(swap)
            def _():
                remote(*args)
            @pl.when(jnp.logical_not(swap))
            def _():
                pltpu.make_async_copy(args[0], args[1], args[3]).start()
        else:
            remote(*args)
        return pltpu.make_async_remote_copy(src_ref=args[0], dst_ref=args[1], send_sem=args[2], recv_sem=args[3], device_id=args[4], device_id_type=MESH)

    def group(zz, cc):
        return dkv.at[pl.ds(lax.rem(zz, 4) * 8 + cc * 4, 4)]

    waits, loads = [], []
    order = (z + 2, z + 1, z + 3, z)
    for k, zz in enumerate(order):
        waits.append(remote(group(zz, 1 - core), sib_in.at[k], sib_send.at[k], sib_recv.at[k], sib))
        load = pltpu.make_async_copy(group(zz, core), own.at[k], load_sem.at[k])
        load.start()
        loads.append(load)
    sent_o = [exchange(odq, odq_own.at[x], o_send, o_recv, d) for d in range(4)]

    def add(first, k, also=()):
        def step(i, _):
            j, r = i // 2, pl.ds(pl.multiple_of(lax.rem(i, 2) * 128, 128), 128)
            total = own[k, j, r].astype(f32) + sib_in[k, j, r].astype(f32)
            for ref, low, high in also:
                if (low, high) == (0, 4):
                    total = total + ref[j, r].astype(f32)
            first[j, r] = total.astype(bf)
            return 0
        lax.fori_loop(0, 8, step, 0)

    mlp_out[...] = jnp.zeros_like(mlp_out)
    back_out[...] = jnp.zeros_like(back_out)
    for copy in fetch:
        copy.wait()
    lax.fori_loop(0, 1, feed, 0)
    loads[0].wait()
    landed(sib_in.at[0], sib_recv.at[0])
    add(done, 0)
    for way, to in ((0, above), (1, below)):
        waits.append(remote(done.at[pl.ds(2 * way, 2)], far_in.at[way], far_send.at[way], far_recv.at[way], to))
    lax.fori_loop(1, 3, feed, 0)
    for way, to in ((0, above), (1, below)):
        k = 1 + way
        loads[k].wait()
        landed(sib_in.at[k], sib_recv.at[k])
        add(near_out.at[way], k)
        landed(far_in.at[way], far_recv.at[way])

        def more(i, _):
            j, r = i // 2, pl.ds(pl.multiple_of(lax.rem(i, 2) * 128, 128), 128)
            near_out[way, 2 * way + j, r] = (own[k, 2 * way + j, r].astype(f32) + sib_in[k, 2 * way + j, r].astype(f32) + far_in[way, j, r].astype(f32)).astype(bf)
            return 0
        lax.fori_loop(0, 4, more, 0)
        waits.append(remote(near_out.at[way], near_in.at[way], near_send.at[way], near_recv.at[way], to))
    lax.fori_loop(3, 5, feed, 0)
    loads[3].wait()
    landed(sib_in.at[3], sib_recv.at[3])
    for way in (0, 1):
        landed(near_in.at[way], near_recv.at[way])
    for copy in waits[4:6]:
        copy.wait_send()
    sent_g = []
    for d in range(4):
        j = lax.rem(x + d, 4)
        done[j] = (own[3, j].astype(f32) + sib_in[3, j].astype(f32) + near_in[0, j].astype(f32) + near_in[1, j].astype(f32)).astype(bf)
        sent_g.append(exchange(done, dkv_own.at[x], g_send, g_recv, d))
    lax.fori_loop(5, 8, feed, 0)
    for t in range(8):
        at = pl.ds(t * TILE, TILE)
        pltpu.make_async_copy(up_stage.at[t], up_grad.at[:, at], up_sem.at[t]).wait()
        pltpu.make_async_copy(down_stage.at[at], down_grad.at[at], down_sem.at[t]).wait()
    for d in range(4):
        h = lax.rem(x + 4 - d, 4)
        landed(odq_own.at[h], o_recv.at[d])
        landed(dkv_own.at[h], g_recv.at[d])
    for i, copy in enumerate(waits):
        if i not in (4, 5):
            copy.wait_send()
    for sent in (sent_o, sent_g):
        for d in range(4):
            if d == 0:
                @pl.when(swap)
                def _():
                    sent[d].wait_send()
            else:
                sent[d].wait_send()


def collect(odq, dkv, normed, grad, up, up_bias, down, collective_id=1):
    hbm = pl.BlockSpec(memory_space=pl.ANY)
    vmem = pl.BlockSpec(memory_space=pltpu.VMEM)
    dma = pltpu.SemaphoreType.DMA
    bf, f32 = jnp.bfloat16, jnp.float32
    one = jax.ShapeDtypeStruct((4, ROWS, WIDE), bf)
    rows = jax.ShapeDtypeStruct((ROWS, 768), f32)
    return pl.pallas_call(
        collect_kernel,
        out_shape=(one, one, rows, rows, jax.ShapeDtypeStruct((768, 3072), bf), jax.ShapeDtypeStruct((3072, 768), bf), jax.ShapeDtypeStruct((8, 3072), f32)),
        in_specs=[hbm, hbm, vmem, vmem, hbm, vmem, hbm], out_specs=(hbm, hbm, vmem, vmem, hbm, hbm, vmem),
        scratch_shapes=[pltpu.VMEM((4, 4, ROWS, WIDE), bf), pltpu.VMEM((4, 4, ROWS, WIDE), bf), pltpu.VMEM((2, 2, ROWS, WIDE), bf),
            pltpu.VMEM((2, 4, ROWS, WIDE), bf), pltpu.VMEM((2, 4, ROWS, WIDE), bf), pltpu.VMEM((4, ROWS, WIDE), bf),
            dma((4,)), dma((4,)), dma((4,)), dma((4,)), dma((4,)), dma((2,)), dma((2,)), dma((2,)), dma((2,)), dma((4,)), dma((4,)),
            pltpu.VMEM((768, 3072), bf), pltpu.VMEM((3072, 768), bf), pltpu.VMEM((8, 768, TILE), bf), pltpu.VMEM((3072, 768), bf),
            dma((8,)), dma((8,)), dma((2,))],
        compiler_params=pltpu.CompilerParams(collective_id=collective_id, has_side_effects=True, vmem_limit_bytes=60 * 2**20),
        name="collect",
    )(odq, dkv, normed, grad, up, up_bias, down)


def front_kernel(tokens, grad, tables, qkv, dense, vectors, kv_all, qdo, normed_one, normed_two, all_vectors, weights_out,
                 weights, vec_in, kvs, qds, local_sem, send_sem, recv_sem, kv_send, kv_recv, q_send, q_recv):
    z, yl, x, yh, core = place()
    f32, bf = jnp.float32, jnp.bfloat16
    me = yh * 2 + core
    far = (1 - yh) * 2 + core
    other = (1 - yh) * 2 + 1 - core
    swap = yl != core
    partner = [device(z, core, lax.rem(x + d, 4), yh, yl) for d in range(4)]
    sib = device(z, yl, x, yh, 1 - core)
    cross = device(z, 1 - yl, x, 1 - yh, core)
    others = [device(z, yl, x, 1 - yh, core), device(z, yl, x, 1 - yh, 1 - core)]
    xs = [device(z, yl, lax.rem(x + d, 4), yh, core) for d in (1, 3)]
    zs = [device(lax.rem(z + d, 4), yl, x, yh, core) for d in (1, 3)]
    greet([sib, cross] + others + xs + zs + partner[1:], partner[0], lax.rem(yl + core, 2))
    count = [0]
    sent = []

    def remote(src, dst, to):
        sem = count[0]
        count[0] += 1
        copy = pltpu.make_async_remote_copy(src_ref=src, dst_ref=dst, send_sem=send_sem.at[sem], recv_sem=recv_sem.at[sem], device_id=to, device_id_type=MESH)
        copy.start()
        sent.append(copy)
        return sem

    def arrive(ref, sem):
        landed(ref, recv_sem.at[sem])

    def rows(i, start, size):
        return weights.at[i, pl.ds(pl.multiple_of(start, 16), size)]

    shards = [qkv.at[:, pl.ds(768, 768)], qkv.at[:, pl.ds(1536, 768)], qkv.at[:, pl.ds(0, 768)], dense]
    quarter = [x, z, x, z]
    ring = [xs, zs, xs, zs]
    vec_sem = [remote(vectors, vec_in.at[i], to) for i, to in enumerate([sib] + others)]
    cross_sem = [remote(shards[i].at[pl.ds(pl.multiple_of(quarter[i] * 48, 16), 48)], rows(i, me * 192 + quarter[i] * 48, 48), cross) for i in range(4)]
    own, late = [], [[], [], [], []]
    for i in range(4):
        copy = pltpu.make_async_copy(shards[i], rows(i, me * 192, 192), local_sem.at[i])
        copy.start()
        own.append(copy)
        late[i].append((rows(i, (yh * 2 + 1 - core) * 192, 192), remote(shards[i], rows(i, me * 192, 192), sib)))

    values = tokens[...].astype(f32)
    centered = values - jnp.mean(values, -1, keepdims=True)
    unit = centered * lax.rsqrt(jnp.mean(centered * centered, -1, keepdims=True) + 1e-05)
    for i in range(3):
        arrive(vec_in.at[i], vec_sem[i])
    vec = vectors[...].astype(f32) + vec_in[0].astype(f32) + vec_in[1].astype(f32) + vec_in[2].astype(f32)
    all_vectors[...] = vec
    normed_one[...] = (unit * vec[0:1] + vec[1:2]).astype(bf)
    normed_two[...] = (unit * vec[2:3] + vec[3:4]).astype(bf)

    cuts = ((0, 32), (32, 16))
    ring_sem, half_sem = {}, {}

    def start_ring(i):
        mine = rows(i, far * 192 + quarter[i] * 48, 48)
        arrive(mine, cross_sem[i])
        for way in (0, 1):
            ring_sem[i, way] = remote(mine, mine, ring[i][way])
        late[i].append((rows(i, other * 192 + quarter[i] * 48, 48), remote(mine, mine, sib)))

    def relay(i):
        for way in (0, 1):
            b = lax.rem(quarter[i] + 3 - 2 * way, 4)
            got = rows(i, far * 192 + b * 48, 48)
            arrive(got, ring_sem[i, way])
            part = rows(i, far * 192 + b * 48 + cuts[way][0], cuts[way][1])
            half_sem[i, way] = remote(part, part, ring[i][way])
            late[i].append((rows(i, other * 192 + b * 48, 48), remote(got, got, sib)))

    def finish(i):
        for way in (0, 1):
            start = lax.rem(quarter[i] + 2, 4) * 48 + cuts[way][0]
            got = rows(i, far * 192 + start, cuts[way][1])
            arrive(got, half_sem[i, way])
            late[i].append((rows(i, other * 192 + start, cuts[way][1]), remote(got, got, sib)))

    def complete(i):
        for ref, sem in late[i]:
            arrive(ref, sem)
        own[i].wait()

    left = lax.broadcasted_iota(jnp.int32, (ROWS, 128), 1) < 64
    keep, ahead, behind = tables[0], tables[1], tables[2]

    def turn(tile):
        return tile * keep + pltpu.roll(tile, 120, 1) * ahead + pltpu.roll(tile, 8, 1) * behind

    def pack(into, first, second):
        for t in range(6):
            lanes = slice(128 * t, 128 * t + 128)
            a, b = first(lanes), second(lanes)
            for head, tile in ((2 * t, jnp.where(left, a, pltpu.roll(b, 64, 1))), (2 * t + 1, jnp.where(left, pltpu.roll(a, 64, 1), b))):
                into[head // 3, :, 128 * (head % 3):128 * (head % 3) + 128] = tile.astype(bf)

    def dot(a, b):
        return jnp.dot(a, b, preferred_element_type=f32)

    def exchange(src, dst_of, send, recv):
        out = []
        for d in (0, 2, 1, 3):
            args = (src.at[lax.rem(x + d, 4)], dst_of, send.at[d], recv.at[d], partner[d])
            copy = pltpu.make_async_remote_copy(src_ref=args[0], dst_ref=args[1], send_sem=args[2], recv_sem=args[3], device_id=args[4], device_id_type=MESH)
            if d == 0:
                @pl.when(swap)
                def _():
                    copy.start()
                @pl.when(jnp.logical_not(swap))
                def _():
                    pltpu.make_async_copy(args[0], args[1], args[3]).start()
            else:
                copy.start()
            out.append((d, copy))
        return out

    for i in range(4):
        start_ring(i)
    for i in (0, 1):
        relay(i)
    for i in (0, 1):
        finish(i)
    for i in (0, 1):
        complete(i)
    one = normed_one[...]
    pack(kvs,
         lambda lanes: turn(dot(one, weights[0, :, lanes]) + vec[6:7, lanes]),
         lambda lanes: dot(one, weights[1, :, lanes]) + vec[7:8, lanes])
    mine = z * 8 + yl * 4 + x
    sent_kv = exchange(kvs, kv_all.at[mine], kv_send, kv_recv)
    for i in (2, 3):
        relay(i)
    for i in (2, 3):
        finish(i)
    for i in (2, 3):
        complete(i)
    g = grad[...]
    pack(qds,
         lambda lanes: turn(dot(one, weights[2, :, lanes]) + vec[5:6, lanes]) * 0.125,
         lambda lanes: lax.dot_general(g, weights[3, lanes, :], (((1,), (1,)), ((), ())), preferred_element_type=f32))
    sent_q = exchange(qds, qdo.at[x], q_send, q_recv)
    keep_out = pltpu.make_async_copy(weights, weights_out, local_sem.at[4])
    keep_out.start()

    def slot(zz, cc, d):
        return kv_all.at[lax.rem(zz, 4) * 8 + cc * 4 + lax.rem(x + 4 - d, 4)]

    half = ROWS // 2
    up_sem, part_sem, sib_sem = {}, {}, {}
    for d in (0, 1, 3, 2):
        here = slot(z, core, d)
        landed(here, kv_recv.at[d])
        for way in (0, 1):
            up_sem[way, d] = remote(here, here, zs[way])
        sib_sem[0, d] = remote(here, here, sib)
    for d in (0, 1, 3, 2):
        for way in (0, 1):
            here = slot(z + 3 - 2 * way, core, d)
            arrive(here, up_sem[way, d])
            part = here.at[pl.ds(way * half, half)]
            part_sem[way, d] = remote(part, part, zs[way])
            sib_sem[1 + way, d] = remote(here, here, sib)
    for d in (0, 1, 3, 2):
        for way in (0, 1):
            part = slot(z + 2, core, d).at[pl.ds(way * half, half)]
            arrive(part, part_sem[way, d])
            sib_sem[3 + way, d] = remote(part, part, sib)
    for d in range(4):
        arrive(slot(z, 1 - core, d), sib_sem[0, d])
        for way in (0, 1):
            arrive(slot(z + 3 - 2 * way, 1 - core, d), sib_sem[1 + way, d])
            arrive(slot(z + 2, 1 - core, d).at[pl.ds(way * half, half)], sib_sem[3 + way, d])
        landed(qdo.at[lax.rem(x + 4 - d, 4)], q_recv.at[d])
    keep_out.wait()
    for copy in sent:
        copy.wait_send()
    for d, copy in sent_kv + sent_q:
        if d == 0:
            @pl.when(swap)
            def _():
                copy.wait_send()
        else:
            copy.wait_send()


def front(tokens, grad, tables, qkv, dense, vectors, collective_id=0):
    hbm = pl.BlockSpec(memory_space=pl.ANY)
    vmem = pl.BlockSpec(memory_space=pltpu.VMEM)
    dma = pltpu.SemaphoreType.DMA
    bf, f32 = jnp.bfloat16, jnp.float32
    rows = jax.ShapeDtypeStruct((ROWS, 768), bf)
    return pl.pallas_call(
        front_kernel,
        out_shape=(jax.ShapeDtypeStruct((32, ROWS, WIDE), bf), jax.ShapeDtypeStruct((4, ROWS, WIDE), bf), rows, rows,
                   jax.ShapeDtypeStruct((16, 768), f32), jax.ShapeDtypeStruct((4, 768, 768), bf)),
        in_specs=[vmem, vmem, vmem, hbm, hbm, vmem], out_specs=(hbm, hbm, vmem, vmem, vmem, hbm),
        scratch_shapes=[pltpu.VMEM((4, 768, 768), bf), pltpu.VMEM((3, 16, 768), bf), pltpu.VMEM((4, ROWS, WIDE), bf), pltpu.VMEM((4, ROWS, WIDE), bf),
                        dma((5,)), dma((100,)), dma((100,)), dma((4,)), dma((4,)), dma((4,)), dma((4,))],
        compiler_params=pltpu.CompilerParams(collective_id=collective_id, has_side_effects=True, vmem_limit_bytes=40 * 2**20),
        name="front",
    )(tokens, grad, tables, qkv, dense, vectors)


PARTS = ((192, 768, True), (192, 768, False), (192, 384, True), (192, 384, False), (64, 128, True))


def reduce_kernel(wide, upper, lower, tiny, *refs):
    outs, refs = refs[:5], refs[5:]
    own, sib_in, far_in, near_in, far_two, near_two, y_in = (refs[5 * i : 5 * i + 5] for i in range(7))
    load_sem, send_sem, recv_sem = refs[35:]
    z, yl, x, yh, core = place()
    f32, bf = jnp.float32, jnp.bfloat16
    xs = [device(z, yl, lax.rem(x + d, 4), yh, core) for d in (1, 3)]
    zs = [device(lax.rem(z + d, 4), yl, x, yh, core) for d in (1, 3)]
    ys = [device(z, 1 - yl, x, yh, core), device(z, yl, x, 1 - yh, core), device(z, 1 - yl, x, 1 - yh, core)]
    sib = device(z, yl, x, yh, 1 - core)
    greet([sib] + xs + zs + ys)
    count = [0]
    sent = []

    def remote(src, dst, to, sem=None):
        if sem is None:
            sem = count[0]
            count[0] += 1
        copy = pltpu.make_async_remote_copy(src_ref=src, dst_ref=dst, send_sem=send_sem.at[sem], recv_sem=recv_sem.at[sem], device_id=to, device_id_type=MESH)
        copy.start()
        sent.append((src, sem, copy))
        return sem

    def arrive(ref, sem):
        landed(ref, recv_sem.at[sem])

    def piece(p, w, a):
        if p < 2:
            return (wide, upper)[p].at[pl.ds(pl.multiple_of(w * 192, 192), 192), pl.ds(pl.multiple_of(a * 768, 768), 768)]
        if p < 4:
            return lower.at[pl.ds(pl.multiple_of(w * 768 + a * 192, 192), 192), pl.ds(384 * (p - 2), 384)]
        return tiny.at[w, a]

    first = [x if part[2] else z for part in PARTS]
    second = [z if part[2] else x for part in PARTS]
    ring_one = [xs if part[2] else zs for part in PARTS]
    ring_two = [zs if part[2] else xs for part in PARTS]
    everyone = range(5)

    sib_sem = {}
    pairs = []
    for k, ahead in enumerate((2, 1, 3, 0)):
        for p in everyone:
            a = lax.rem(first[p] + ahead, 4)
            sem = count[0]
            count[0] += 1
            sib_sem[p, k] = sem
            for s in (0, 1):
                pltpu.make_async_copy(piece(p, 2 * s + core, a), own[p].at[k, s], load_sem.at[p * 4 + k]).start()
                pltpu.make_async_remote_copy(src_ref=piece(p, 2 * s + 1 - core, a), dst_ref=sib_in[p].at[k, s], send_sem=send_sem.at[sem], recv_sem=recv_sem.at[sem], device_id=sib, device_id_type=MESH).start()
            pairs.append((sib_in[p].at[k], sem))

    def gather_one(p, k):
        landed(own[p].at[k], load_sem.at[p * 4 + k])
        arrive(sib_in[p].at[k], sib_sem[p, k])

    def add(p, rows, into, terms):
        step = 16 if PARTS[p][1] > 384 or rows % 32 else 32

        def body(i, _):
            at = pl.ds(pl.multiple_of(i * step, step), step)
            total = into[at].astype(f32)
            for term in terms:
                total = total + term[at].astype(f32)
            into[at] = total.astype(bf)
            return 0
        lax.fori_loop(0, rows // step, body, 0)

    far_sem, near_sem = {}, {}
    for p in everyone:
        gather_one(p, 0)
        for s in (0, 1):
            add(p, PARTS[p][0], own[p].at[0, s], [sib_in[p].at[0, s]])
            far_sem[p, s] = remote(own[p].at[0, s], far_in[p].at[s], ring_one[p][s])
    for way in (0, 1):
        for p in everyone:
            k = 1 + way
            gather_one(p, k)
            add(p, PARTS[p][0], own[p].at[k, 1 - way], [sib_in[p].at[k, 1 - way]])
            arrive(far_in[p].at[way], far_sem[p, way])
            add(p, PARTS[p][0], own[p].at[k, way], [sib_in[p].at[k, way], far_in[p].at[way]])
            near_sem[p, way] = remote(own[p].at[k], near_in[p].at[way], ring_one[p][way])

    def quarter(p, b):
        rows = PARTS[p][0] // 4
        return pl.ds(pl.multiple_of(lax.rem(b, 4) * rows, rows), rows)

    far_sem2, near_sem2, y_sem = {}, {}, {}
    for p in everyone:
        gather_one(p, 3)
        for way in (0, 1):
            arrive(near_in[p].at[way], near_sem[p, way])
        for s in (0, 1):
            add(p, PARTS[p][0], own[p].at[3, s], [sib_in[p].at[3, s], near_in[p].at[0, s], near_in[p].at[1, s]])
        at = quarter(p, second[p] + 2)
        for s in (0, 1):
            far_sem2[p, s] = remote(own[p].at[3, s, at], far_two[p].at[s], ring_two[p][s])
    for way in (0, 1):
        for p in everyone:
            at = quarter(p, second[p] + 1 + 2 * way)
            arrive(far_two[p].at[way], far_sem2[p, way])
            add(p, PARTS[p][0] // 4, own[p].at[3, way, at], [far_two[p].at[way]])
            near_sem2[p, way] = remote(own[p].at[3, :, at], near_two[p].at[way], ring_two[p][way])
    for p in everyone:
        at = quarter(p, second[p])
        for way in (0, 1):
            arrive(near_two[p].at[way], near_sem2[p, way])
        for s in (0, 1):
            add(p, PARTS[p][0] // 4, own[p].at[3, s, at], [near_two[p].at[0, s], near_two[p].at[1, s]])
        for i, half in enumerate((yh, 1 - yh, 1 - yh)):
            y_sem[p, i] = remote(own[p].at[3, half, at], y_in[p].at[i], ys[i])
    ring_sem = {}
    for p in everyone:
        at = quarter(p, second[p])
        for i in range(3):
            arrive(y_in[p].at[i], y_sem[p, i])
        rows = PARTS[p][0] // 4
        total = own[p][3, yh, at].astype(f32)
        for i in range(3):
            total = total + y_in[p][i].astype(f32)
        outs[p][first[p], at] = total.astype(bf)
        mine = outs[p].at[first[p], at]
        for way in (0, 1):
            ring_sem[p, way] = remote(mine, mine, ring_two[p][way])

    relay_sem = {}
    for way in (0, 1):
        for p in everyone:
            b = lax.rem(second[p] + 3 - 2 * way, 4)
            arrive(outs[p].at[first[p], quarter(p, b)], ring_sem[p, way])
            rows = PARTS[p][0] // 4
            low, high = ((0, 32), (32, 48))[way] if rows == 48 else ((0, 16), (16, 16))[way]
            if high > low:
                part = outs[p].at[first[p], pl.ds(pl.multiple_of(b * rows + low, 16), high - low)]
                relay_sem[p, way] = (remote(part, part, ring_two[p][way]), low, high)
    last_sem = {}
    for p in everyone:
        rows = PARTS[p][0] // 4
        b = lax.rem(second[p] + 2, 4)
        for way in (0, 1):
            if (p, way) in relay_sem:
                sem, low, high = relay_sem[p, way]
                arrive(outs[p].at[first[p], pl.ds(pl.multiple_of(b * rows + low, 16), high - low)], sem)
        mine = outs[p].at[first[p]]
        for way in (0, 1):
            last_sem[p, way] = remote(mine, mine, ring_one[p][way])
    end_sem = {}
    for way in (0, 1):
        for p in everyone:
            block = outs[p].at[lax.rem(first[p] + 3 - 2 * way, 4)]
            arrive(block, last_sem[p, way])
            half = PARTS[p][0] // 2
            part = block.at[pl.ds(way * half, half)]
            end_sem[p, way] = remote(part, part, ring_one[p][way])
    for way in (0, 1):
        for p in everyone:
            half = PARTS[p][0] // 2
            arrive(outs[p].at[lax.rem(first[p] + 2, 4)].at[pl.ds(way * half, half)], end_sem[p, way])
    for ref, sem in pairs:
        landed(ref, send_sem.at[sem])
    for src, sem, copy in sent:
        copy.wait_send()


def reduce_all(wide, upper, lower, tiny, collective_id=2):
    hbm = pl.BlockSpec(memory_space=pl.ANY)
    vmem = pl.BlockSpec(memory_space=pltpu.VMEM)
    dma = pltpu.SemaphoreType.DMA
    bf = jnp.bfloat16
    scratch = []
    for lead in ((4, 2, 1), (4, 2, 1), (2, 0, 1), (2, 2, 1), (2, 0, 4), (2, 2, 4), (3, 0, 4)):
        for rows, columns, _ in PARTS:
            front = tuple(n for n in lead[:2] if n)
            scratch.append(pltpu.VMEM(front + (rows // lead[2], columns), bf))
    return pl.pallas_call(
        reduce_kernel,
        out_shape=tuple(jax.ShapeDtypeStruct((4, rows, columns), bf) for rows, columns, _ in PARTS),
        in_specs=[hbm] * 4, out_specs=(vmem,) * 5,
        scratch_shapes=scratch + [dma((20,)), dma((140,)), dma((140,))],
        compiler_params=pltpu.CompilerParams(collective_id=collective_id, has_side_effects=True, vmem_limit_bytes=60 * 2**20),
        name="reduce",
    )(wide, upper, lower, tiny)


def sum_gradients(gain_one, shift_one, qkv, qkv_bias, dense, gain_two, shift_two, up, up_bias, down, out_bias):
    bf, f32 = jnp.bfloat16, jnp.float32
    small = (gain_one, shift_one, gain_two, shift_two, out_bias, qkv_bias, up_bias)
    flat = jnp.concatenate([v.reshape(4, -1) for v in small], 1).astype(bf)
    tiny = jnp.pad(flat.reshape(4, 16, 144), ((0, 0), (0, 0), (0, 2048 - 144))).reshape(4, 4, 64, 128)
    wide = jnp.concatenate([qkv.astype(bf), dense.astype(bf)], 1)
    wide, upper, left, right, tiny = reduce_all(wide, up.astype(bf), down.astype(bf), tiny)
    wide = wide.astype(f32).transpose(1, 0, 2).reshape(192, 3072)
    upper = upper.astype(f32).transpose(1, 0, 2).reshape(192, 3072)
    lower = jnp.concatenate([left.astype(f32), right.astype(f32)], 2).reshape(768, 768)
    flat = tiny.astype(f32).reshape(16, 2048)[:, :144].reshape(-1)
    parts, start = [], 0
    for v in small:
        parts.append(flat[start : start + v.shape[0] // 4])
        start += v.shape[0] // 4
    gain_one, shift_one, gain_two, shift_two, out_bias, qkv_bias, up_bias = parts
    return gain_one, shift_one, wide[:, :2304], qkv_bias, wide[:, 2304:], gain_two, shift_two, upper, up_bias, lower, out_bias


D = 768
HEADS = 12
HD = 64
ROT = 16
TOK_DEV = 256


def layer_norm(values, norm_gain, norm_shift):
    row_mean = jnp.mean(values, -1, keepdims=True)
    centered = values - row_mean
    row_var = jnp.mean(centered * centered, -1, keepdims=True)
    return centered * lax.rsqrt(row_var + 1e-05) * norm_gain + norm_shift


def rotary_tables(positions):
    lanes = jnp.arange(128) % HD
    exponents = (lanes % 8).astype(jnp.float32) * 2.0 / ROT
    inverse = 10000.0 ** (-exponents)
    angles = positions.astype(jnp.float32)[:, None] * inverse[None, :]
    cosine, sine = jnp.cos(angles), jnp.sin(angles)
    keep = jnp.where(lanes < ROT, cosine, 1.0)
    ahead = jnp.where(lanes < 8, -sine, 0.0)
    behind = jnp.where((lanes >= 8) & (lanes < ROT), sine, 0.0)
    return jnp.stack([keep, ahead, behind])


def rotate_back(rows, tables):
    keep, ahead, behind = (jnp.tile(table, (1, 6)) for table in tables)
    return rows * keep + jnp.roll(rows * ahead, 8, 1) + jnp.roll(rows * behind, -8, 1)


def contract(left_side, right_side, left_dim, right_dim):
    return lax.dot_general(
        left_side,
        right_side,
        (((left_dim,), (right_dim,)), ((), ())),
        preferred_element_type=jnp.float32,
    )


def unslab(pairs):
    both = pairs.transpose(1, 0, 2).reshape(TOK_DEV, HEADS, 2, HD)
    return both[:, :, 0].reshape(TOK_DEV, D), both[:, :, 1].reshape(TOK_DEV, D)


def on_device(
    tokens, cotangent, pairing, first_gain, first_shift, qkv_weight, qkv_bias, dense_weight,
    second_gain, second_shift, up_weight, up_bias, down_weight, out_bias,
):
    bf, f32 = jnp.bfloat16, jnp.float32
    total_blocks = 64
    offsets = jnp.arange(BLK, dtype=jnp.int32)
    ctx_index = lax.axis_index("ctx")
    core = lax.rem(lax.axis_index("wsh"), 2)
    seq_of_layout = jnp.stack([pairing, total_blocks - 1 - pairing], 1).reshape(-1)
    layout_of_seq = (
        jnp.zeros((total_blocks,), jnp.int32)
        .at[seq_of_layout]
        .set(jnp.arange(total_blocks, dtype=jnp.int32))
    )
    own_blocks = lax.dynamic_slice(seq_of_layout, (2 * ctx_index,), (2,))
    row_blocks = lax.dynamic_slice(seq_of_layout, (16 * (ctx_index // 8) + 8 * core,), (8,))
    local_pos = (own_blocks[:, None] * BLK + offsets[None, :]).reshape(-1)
    tables = rotary_tables(local_pos)
    query_scale = HD ** (-0.5)

    shard = lax.broadcasted_iota(jnp.int32, (4, 1), 0) == lax.axis_index("wsh")
    small = (first_gain, first_shift, second_gain, second_shift, out_bias, qkv_bias, up_bias)
    spots = [jnp.where(shard, v[None, :], 0.0).astype(bf).reshape(-1) for v in small]
    vectors = jnp.concatenate(spots + [jnp.zeros((4 * D,), bf)]).reshape(16, D)
    inputs = tokens[0].astype(f32)
    grad_rows = cotangent[0]
    grad_float = grad_rows.astype(f32)
    keys_values, queries_grads, normed_one, normed_two, vectors, matrices = front(
        tokens[0], grad_rows, tables, qkv_weight, dense_weight, vectors
    )
    gain_one, shift_one, gain_two, shift_two, out_offset = (vectors[i] for i in range(5))
    up_offset = vectors[8:12].reshape(-1)
    dense_matrix = matrices[3]
    up_shard, down_shard, keys_values = lax.optimization_barrier((up_weight, down_weight, keys_values))
    up_matrix = lax.all_gather(up_shard, "wsh", axis=0, tiled=True)
    down_matrix = lax.all_gather(down_shard, "wsh", axis=0, tiled=True)
    attended_dq, grad_kv = attention(row_blocks, layout_of_seq, queries_grads.reshape(1024, WIDE), keys_values.reshape(8192, WIDE))
    attended_dq, grad_kv, mlp_out, grad_normed_two, up_grad, down_grad, up_offset_grad = collect(
        attended_dq.reshape(4, ROWS, WIDE), grad_kv.reshape(32, ROWS, WIDE), normed_two, grad_rows,
        up_matrix, jnp.broadcast_to(up_offset, (8, 3072)), down_matrix,
    )
    up_offset_grad = up_offset_grad[0]
    attended_low, grad_queries = unslab(attended_dq)
    grad_keys, grad_values = unslab(grad_kv)

    attention_out = jnp.dot(attended_low, dense_matrix, preferred_element_type=f32)
    layer_output = (inputs + attention_out + mlp_out + out_offset).astype(bf)[None]

    out_offset_grad = jnp.sum(grad_float, 0)
    dense_grad = contract(attended_low, grad_rows, 0, 0)
    grad_mixed = jnp.concatenate(
        [
            rotate_back(grad_queries.astype(f32) * query_scale, tables).astype(bf),
            rotate_back(grad_keys.astype(f32), tables).astype(bf),
            grad_values,
        ],
        1,
    )
    qkv_grad = contract(normed_one, grad_mixed, 0, 0)
    qkv_offset_grad = jnp.sum(grad_mixed.astype(f32), 0)
    grad_normed_one = (
        contract(grad_mixed[:, :D], matrices[2], 1, 1)
        + contract(grad_mixed[:, D : 2 * D], matrices[0], 1, 1)
        + contract(grad_mixed[:, 2 * D :], matrices[1], 1, 1)
    )
    grad_in_one, gain_one_grad, shift_one_grad = jax.vjp(layer_norm, inputs, gain_one, shift_one)[1](grad_normed_one)
    grad_in_two, gain_two_grad, shift_two_grad = jax.vjp(layer_norm, inputs, gain_two, shift_two)[1](grad_normed_two)
    input_grad = (grad_float + grad_in_one + grad_in_two).astype(bf)[None]

    return (layer_output, input_grad) + sum_gradients(
        gain_one_grad, shift_one_grad, qkv_grad, qkv_offset_grad, dense_grad, gain_two_grad, shift_two_grad,
        up_grad, up_offset_grad, down_grad, out_offset_grad,
    )


def solution(mesh):
    rows, split, flat = P("wsh", "ctx", None), P("wsh", None), P("wsh")
    return jax.shard_map(
        on_device,
        mesh=mesh,
        in_specs=(rows, rows, P(), flat, flat, split, flat, split, flat, flat, split, flat, split, flat),
        out_specs=(rows, rows, flat, flat, split, flat, split, flat, flat, split, flat, split, flat),
        check_vma=False,
    )
```

```python
import functools

import jax
import jax.numpy as jnp
from jax import lax
from jax.experimental import pallas as pl
from jax.experimental.pallas import tpu as pltpu
from jax.sharding import PartitionSpec as P

G = 3; BLK = 128; LOG2E = 1.4426950408889634
NEG = -1e30

def attn_kernel(chunk, qpos, lay, qdo, kv_hbm, odq, dkv_hbm, kv, kvt, acc, probs, grads, tops, stage, sem, osem):
    blocks = chunk // BLK
    nblk = kv.shape[0] // BLK
    f32, bf = jnp.float32, jnp.bfloat16

    def load(i, _):
        pltpu.make_async_copy(kv_hbm.at[pl.ds(pl.multiple_of(lay[i] * BLK, BLK), BLK)], kv.at[pl.ds(pl.multiple_of(i * BLK, BLK), BLK)], sem.at[i]).start()
        return 0
    lax.fori_loop(0, nblk, load, 0)

    def land(i, _):
        rows = pl.ds(pl.multiple_of(i * BLK, BLK), BLK)
        pltpu.make_async_copy(kv_hbm.at[pl.ds(0, BLK)], kv.at[rows], sem.at[i]).wait()
        acc[rows] = jnp.zeros((BLK, G * 128), f32)
        kvt[:, rows] = kv[rows].T
        return 0
    lax.fori_loop(0, nblk, land, 0)

    upper = lax.broadcasted_iota(jnp.int32, (128, 128), 0) < 64
    left = lax.broadcasted_iota(jnp.int32, (128, 128), 1) < 64

    def q_block(i, _):
        b = qpos[i]
        qrows = pl.ds(pl.multiple_of(i * BLK, BLK), BLK)
        last = b // blocks
        pairs = [qdo[qrows, h * 128:(h + 1) * 128] for h in range(G)]
        turned = [p.astype(f32).T for p in pairs]
        wide = [jnp.concatenate([jnp.where(upper, turned[h], 0.0).astype(bf), jnp.where(upper, 0.0, turned[h]).astype(bf)], 1) for h in range(G)]
        key_i = lax.broadcasted_iota(jnp.int32, (chunk, BLK), 0)
        row_i = lax.broadcasted_iota(jnp.int32, (chunk, BLK), 1) + (b - last * blocks) * BLK

        def fwd(c, state, masked):
            at = pl.ds(pl.multiple_of(c * chunk, chunk), chunk)
            out = []
            every = [jnp.dot(kv[at, h * 128:(h + 1) * 128], wide[h], preferred_element_type=f32) for h in range(G)]
            kept = []
            for h in range(G):
                m, l, o = state[h]
                s = every[h][:, :128]
                grads[at, h * 128:(h + 1) * 128] = every[h][:, 128:]
                if masked:
                    s = jnp.where(key_i <= row_i, s, NEG)
                new = jnp.maximum(m, jnp.max(s, 0, keepdims=True))
                p = jnp.exp(s - new)
                a = jnp.exp(m - new)
                l = l * a + jnp.sum(p, 0, keepdims=True)
                p = p.astype(bf)
                probs[at, h * 128:(h + 1) * 128] = p
                tops[c, h] = jnp.broadcast_to(new, (8, BLK))
                kept.append((new, l, o * a, p))
            for h in range(G):
                new, l, o, p = kept[h]
                o = o + jnp.dot(kvt[h * 128 + 64:(h + 1) * 128, at], p, preferred_element_type=f32)
                out.append((new, l, o))
            return tuple(out)

        state = tuple((jnp.full((1, BLK), NEG, f32), jnp.zeros((1, BLK), f32), jnp.zeros((64, BLK), f32)) for _ in range(G))
        state = lax.fori_loop(0, last, lambda c, s: fwd(c, s, False), state)
        state = fwd(last, state, True)
        lse, delta, outs = [], [], []
        for h in range(G):
            m, l, o = state[h]
            o = o / l
            outs.append(o)
            lse.append(m + jnp.log(l))
            delta.append(jnp.sum(o * turned[h][64:], 0, keepdims=True))
        narrow = [jnp.concatenate([jnp.where(left, pairs[h], jnp.zeros_like(pairs[h])), jnp.where(left, jnp.zeros_like(pairs[h]), pairs[h])], 0) for h in range(G)]

        def bwd(c, state):
            at = pl.ds(pl.multiple_of(c * chunk, chunk), chunk)
            out, work = [], []
            for h in range(G):
                cols = slice(h * 128, (h + 1) * 128)
                p = probs[at, cols].astype(f32) * jnp.exp(tops[c, h, 0:1] - lse[h])
                ds = (p * (grads[at, cols] - delta[h])).astype(bf)
                work.append((jnp.concatenate([ds, p.astype(bf)], 1), ds))
            for h in range(G):
                pair, ds = work[h]
                acc[at, h * 128:(h + 1) * 128] += jnp.dot(pair, narrow[h], preferred_element_type=f32)
                out.append(state[h] + jnp.dot(kvt[h * 128:h * 128 + 64, at], ds, preferred_element_type=f32))
            return tuple(out)

        dq = tuple(jnp.zeros((64, BLK), f32) for _ in range(G))
        dq = lax.fori_loop(0, last + 1, bwd, dq)
        for h in range(G):
            odq[qrows, h * 128:(h + 1) * 128] = jnp.concatenate([outs[h], dq[h]], 0).T.astype(bf)
        return 0
    lax.fori_loop(0, qpos.shape[0], q_block, 0)

    def send(i, _):
        slot = lax.rem(i, 8)
        @pl.when(i >= 8)
        def _():
            pltpu.make_async_copy(stage.at[slot], dkv_hbm.at[pl.ds(0, BLK)], osem.at[slot]).wait()
        stage[slot] = acc[pl.ds(pl.multiple_of(i * BLK, BLK), BLK)].astype(bf)
        pltpu.make_async_copy(stage.at[slot], dkv_hbm.at[pl.ds(pl.multiple_of(lay[i] * BLK, BLK), BLK)], osem.at[slot]).start()
        return 0
    lax.fori_loop(0, nblk, send, 0)
    for slot in range(8):
        pltpu.make_async_copy(stage.at[slot], dkv_hbm.at[pl.ds(0, BLK)], osem.at[slot]).wait()

def attention(qpos, lay, qdo, kv, chunk=1024):
    n = kv.shape[0]
    smem = pl.BlockSpec(memory_space=pltpu.SMEM)
    vmem = pl.BlockSpec(memory_space=pltpu.VMEM)
    hbm = pl.BlockSpec(memory_space=pl.ANY)
    return pl.pallas_call(
        functools.partial(attn_kernel, chunk),
        out_shape=(jax.ShapeDtypeStruct(qdo.shape, jnp.bfloat16), jax.ShapeDtypeStruct(kv.shape, jnp.bfloat16)),
        in_specs=[smem, smem, vmem, hbm], out_specs=(vmem, hbm),
        scratch_shapes=[pltpu.VMEM((n, G * 128), jnp.bfloat16), pltpu.VMEM((G * 128, n), jnp.bfloat16),
            pltpu.VMEM((n, G * 128), jnp.float32), pltpu.VMEM((n, G * 128), jnp.bfloat16), pltpu.VMEM((n, G * 128), jnp.float32), pltpu.VMEM((n // chunk, G, 8, BLK), jnp.float32),
            pltpu.VMEM((8, BLK, G * 128), jnp.bfloat16),
            pltpu.SemaphoreType.DMA((n // BLK,)), pltpu.SemaphoreType.DMA((8,))],
        compiler_params=pltpu.CompilerParams(vmem_limit_bytes=62 * 2**20),
        name="attention",
    )(qpos, lay, qdo, kv)


MESH = pl.DeviceIdType.MESH
ROWS, WIDE = 256, 384


def place():
    c, w = lax.axis_index("ctx"), lax.axis_index("wsh")
    return c // 8, lax.rem(c // 4, 2), lax.rem(c, 4), w // 2, lax.rem(w, 2)


def device(z, yl, x, yh, core):
    return (z * 8 + yl * 4 + x, yh * 2 + core)


def greet(devices, extra=None, extra_count=0):
    barrier = pltpu.get_barrier_semaphore()
    for d in devices:
        pl.semaphore_signal(barrier, inc=1, device_id=d, device_id_type=MESH)
    if extra is not None:
        @pl.when(extra_count == 1)
        def _():
            pl.semaphore_signal(barrier, inc=1, device_id=extra, device_id_type=MESH)
    pl.semaphore_wait(barrier, len(devices) + extra_count)


def landed(ref, sem):
    pltpu.make_async_copy(ref, ref, sem).wait()


def front_kernel(tokens, grad, tables, qkv, dense, vectors, kv_all, qdo, normed_one, normed_two, all_vectors, weights_out,
                 weights, vec_in, kvs, qds, local_sem, send_sem, recv_sem, kv_send, kv_recv, q_send, q_recv):
    z, yl, x, yh, core = place()
    f32, bf = jnp.float32, jnp.bfloat16
    me = yh * 2 + core
    far = (1 - yh) * 2 + core
    other = (1 - yh) * 2 + 1 - core
    swap = yl != core
    partner = [device(z, core, lax.rem(x + d, 4), yh, yl) for d in range(4)]
    sib = device(z, yl, x, yh, 1 - core)
    cross = device(z, 1 - yl, x, 1 - yh, core)
    others = [device(z, yl, x, 1 - yh, core), device(z, yl, x, 1 - yh, 1 - core)]
    xs = [device(z, yl, lax.rem(x + d, 4), yh, core) for d in (1, 3)]
    zs = [device(lax.rem(z + d, 4), yl, x, yh, core) for d in (1, 3)]
    greet([sib, cross] + others + xs + zs + partner[1:], partner[0], lax.rem(yl + core, 2))
    count = [0]
    sent = []

    def remote(src, dst, to):
        sem = count[0]
        count[0] += 1
        copy = pltpu.make_async_remote_copy(src_ref=src, dst_ref=dst, send_sem=send_sem.at[sem], recv_sem=recv_sem.at[sem], device_id=to, device_id_type=MESH)
        copy.start()
        sent.append(copy)
        return sem

    def arrive(ref, sem):
        landed(ref, recv_sem.at[sem])

    def rows(i, start, size):
        return weights.at[i, pl.ds(pl.multiple_of(start, 16), size)]

    shards = [qkv.at[:, pl.ds(768, 768)], qkv.at[:, pl.ds(1536, 768)], qkv.at[:, pl.ds(0, 768)], dense]
    quarter = [x, z, x, z]
    ring = [xs, zs, xs, zs]
    vec_sem = [remote(vectors, vec_in.at[i], to) for i, to in enumerate([sib] + others)]
    cross_sem = [remote(shards[i].at[pl.ds(pl.multiple_of(quarter[i] * 48, 16), 48)], rows(i, me * 192 + quarter[i] * 48, 48), cross) for i in range(4)]
    own, late = [], [[], [], [], []]
    for i in range(4):
        copy = pltpu.make_async_copy(shards[i], rows(i, me * 192, 192), local_sem.at[i])
        copy.start()
        own.append(copy)
        late[i].append((rows(i, (yh * 2 + 1 - core) * 192, 192), remote(shards[i], rows(i, me * 192, 192), sib)))

    values = tokens[...].astype(f32)
    centered = values - jnp.mean(values, -1, keepdims=True)
    unit = centered * lax.rsqrt(jnp.mean(centered * centered, -1, keepdims=True) + 1e-05)
    for i in range(3):
        arrive(vec_in.at[i], vec_sem[i])
    vec = vectors[...].astype(f32) + vec_in[0].astype(f32) + vec_in[1].astype(f32) + vec_in[2].astype(f32)
    all_vectors[...] = vec
    normed_one[...] = (unit * vec[0:1] + vec[1:2]).astype(bf)
    normed_two[...] = (unit * vec[2:3] + vec[3:4]).astype(bf)

    cuts = ((0, 32), (32, 16))
    ring_sem, half_sem = {}, {}

    def start_ring(i):
        mine = rows(i, far * 192 + quarter[i] * 48, 48)
        arrive(mine, cross_sem[i])
        for way in (0, 1):
            ring_sem[i, way] = remote(mine, mine, ring[i][way])
        late[i].append((rows(i, other * 192 + quarter[i] * 48, 48), remote(mine, mine, sib)))

    def relay(i):
        for way in (0, 1):
            b = lax.rem(quarter[i] + 3 - 2 * way, 4)
            got = rows(i, far * 192 + b * 48, 48)
            arrive(got, ring_sem[i, way])
            part = rows(i, far * 192 + b * 48 + cuts[way][0], cuts[way][1])
            half_sem[i, way] = remote(part, part, ring[i][way])
            late[i].append((rows(i, other * 192 + b * 48, 48), remote(got, got, sib)))

    def finish(i):
        for way in (0, 1):
            start = lax.rem(quarter[i] + 2, 4) * 48 + cuts[way][0]
            got = rows(i, far * 192 + start, cuts[way][1])
            arrive(got, half_sem[i, way])
            late[i].append((rows(i, other * 192 + start, cuts[way][1]), remote(got, got, sib)))

    def complete(i):
        for ref, sem in late[i]:
            arrive(ref, sem)
        own[i].wait()

    left = lax.broadcasted_iota(jnp.int32, (ROWS, 128), 1) < 64
    keep, ahead, behind = tables[0], tables[1], tables[2]

    def turn(tile):
        return tile * keep + pltpu.roll(tile, 120, 1) * ahead + pltpu.roll(tile, 8, 1) * behind

    def pack(into, first, second):
        for t in range(6):
            lanes = slice(128 * t, 128 * t + 128)
            a, b = first(lanes), second(lanes)
            for head, tile in ((2 * t, jnp.where(left, a, pltpu.roll(b, 64, 1))), (2 * t + 1, jnp.where(left, pltpu.roll(a, 64, 1), b))):
                into[head // 3, :, 128 * (head % 3):128 * (head % 3) + 128] = tile.astype(bf)

    def dot(a, b):
        return jnp.dot(a, b, preferred_element_type=f32)

    def exchange(src, dst_of, send, recv):
        out = []
        for d in (0, 2, 1, 3):
            args = (src.at[lax.rem(x + d, 4)], dst_of, send.at[d], recv.at[d], partner[d])
            copy = pltpu.make_async_remote_copy(src_ref=args[0], dst_ref=args[1], send_sem=args[2], recv_sem=args[3], device_id=args[4], device_id_type=MESH)
            if d == 0:
                @pl.when(swap)
                def _():
                    copy.start()
                @pl.when(jnp.logical_not(swap))
                def _():
                    pltpu.make_async_copy(args[0], args[1], args[3]).start()
            else:
                copy.start()
            out.append((d, copy))
        return out

    for i in range(4):
        start_ring(i)
    for i in (0, 1):
        relay(i)
    for i in (0, 1):
        finish(i)
    for i in (0, 1):
        complete(i)
    one = normed_one[...]
    pack(kvs,
         lambda lanes: turn(dot(one, weights[0, :, lanes]) + vec[6:7, lanes]),
         lambda lanes: dot(one, weights[1, :, lanes]) + vec[7:8, lanes])
    mine = z * 8 + yl * 4 + x
    sent_kv = exchange(kvs, kv_all.at[mine], kv_send, kv_recv)
    for i in (2, 3):
        relay(i)
    for i in (2, 3):
        finish(i)
    for i in (2, 3):
        complete(i)
    g = grad[...]
    pack(qds,
         lambda lanes: turn(dot(one, weights[2, :, lanes]) + vec[5:6, lanes]) * 0.125,
         lambda lanes: lax.dot_general(g, weights[3, lanes, :], (((1,), (1,)), ((), ())), preferred_element_type=f32))
    sent_q = exchange(qds, qdo.at[x], q_send, q_recv)
    keep_out = pltpu.make_async_copy(weights, weights_out, local_sem.at[4])
    keep_out.start()

    def slot(zz, cc, d):
        return kv_all.at[lax.rem(zz, 4) * 8 + cc * 4 + lax.rem(x + 4 - d, 4)]

    half = ROWS // 2
    up_sem, part_sem, sib_sem = {}, {}, {}
    for d in (0, 1, 3, 2):
        here = slot(z, core, d)
        landed(here, kv_recv.at[d])
        for way in (0, 1):
            up_sem[way, d] = remote(here, here, zs[way])
        sib_sem[0, d] = remote(here, here, sib)
    for d in (0, 1, 3, 2):
        for way in (0, 1):
            here = slot(z + 3 - 2 * way, core, d)
            arrive(here, up_sem[way, d])
            part = here.at[pl.ds(way * half, half)]
            part_sem[way, d] = remote(part, part, zs[way])
            sib_sem[1 + way, d] = remote(here, here, sib)
    for d in (0, 1, 3, 2):
        for way in (0, 1):
            part = slot(z + 2, core, d).at[pl.ds(way * half, half)]
            arrive(part, part_sem[way, d])
            sib_sem[3 + way, d] = remote(part, part, sib)
    for d in range(4):
        arrive(slot(z, 1 - core, d), sib_sem[0, d])
        for way in (0, 1):
            arrive(slot(z + 3 - 2 * way, 1 - core, d), sib_sem[1 + way, d])
            arrive(slot(z + 2, 1 - core, d).at[pl.ds(way * half, half)], sib_sem[3 + way, d])
        landed(qdo.at[lax.rem(x + 4 - d, 4)], q_recv.at[d])
    keep_out.wait()
    for copy in sent:
        copy.wait_send()
    for d, copy in sent_kv + sent_q:
        if d == 0:
            @pl.when(swap)
            def _():
                copy.wait_send()
        else:
            copy.wait_send()


def front(tokens, grad, tables, qkv, dense, vectors, collective_id=0):
    hbm = pl.BlockSpec(memory_space=pl.ANY)
    vmem = pl.BlockSpec(memory_space=pltpu.VMEM)
    dma = pltpu.SemaphoreType.DMA
    bf, f32 = jnp.bfloat16, jnp.float32
    rows = jax.ShapeDtypeStruct((ROWS, 768), bf)
    return pl.pallas_call(
        front_kernel,
        out_shape=(jax.ShapeDtypeStruct((32, ROWS, WIDE), bf), jax.ShapeDtypeStruct((4, ROWS, WIDE), bf), rows, rows,
                   jax.ShapeDtypeStruct((16, 768), f32), jax.ShapeDtypeStruct((4, 768, 768), bf)),
        in_specs=[vmem, vmem, vmem, hbm, hbm, vmem], out_specs=(hbm, hbm, vmem, vmem, vmem, hbm),
        scratch_shapes=[pltpu.VMEM((4, 768, 768), bf), pltpu.VMEM((3, 16, 768), bf), pltpu.VMEM((4, ROWS, WIDE), bf), pltpu.VMEM((4, ROWS, WIDE), bf),
                        dma((5,)), dma((100,)), dma((100,)), dma((4,)), dma((4,)), dma((4,)), dma((4,))],
        compiler_params=pltpu.CompilerParams(collective_id=collective_id, has_side_effects=True, vmem_limit_bytes=40 * 2**20),
        name="front",
    )(tokens, grad, tables, qkv, dense, vectors)


PARTS = ((768, False), (768, True), (384, True), (384, False))
TILE = 384


def erf(values):
    v = jnp.clip(values, -4.0, 4.0)
    s = v * v
    top = jnp.float32(-2.72614225801306e-10)
    for coefficient in (2.77068142495902e-08, -2.10102402082508e-06, -5.69250639462346e-05, -7.34990630326855e-04, -2.95459980854025e-03, -1.60960333262415e-02):
        top = top * s + coefficient
    low = jnp.float32(-1.45660718464996e-05)
    for coefficient in (-2.13374055278905e-04, -1.68282697438203e-03, -7.37332916720468e-03, -1.42647390514189e-02):
        low = low * s + coefficient
    return v * top / low


def back_kernel(odq, dkv, tokens_hbm, grad_hbm, one_hbm, two_hbm, vectors_hbm, tables_hbm, matrices, up_hbm, down_hbm,
                layer_output, input_grad, wide_out, upper_out, lower_out, vector_out, *refs):
    sib_in, far_in, near_in, far_two, near_two, y_in = (refs[4 * i : 4 * i + 4] for i in range(6))
    (tokens, grad, normed_one, normed_two, vectors, tables, up, down_w, upper, lower, mlp, back_two, up_bias, bias_grad,
     held, held_in, held_far, held_near, odq_own, dkv_own, attended, mixed, tiny, tiny_in, send_sem, recv_sem, local_sem) = refs[24:]
    z, yl, x, yh, core = place()
    f32, bf = jnp.float32, jnp.bfloat16
    swapped_place = yl != core
    partner = [device(z, core, lax.rem(x + d, 4), yh, yl) for d in range(4)]
    xs = [device(z, yl, lax.rem(x + d, 4), yh, core) for d in (1, 3, 2)]
    zs = [device(lax.rem(z + d, 4), yl, x, yh, core) for d in (1, 3, 2)]
    ys = [device(z, 1 - yl, x, yh, core), device(z, yl, x, 1 - yh, core), device(z, 1 - yl, x, 1 - yh, core)]
    sib = device(z, yl, x, yh, 1 - core)
    greet([sib] + xs + zs + ys + partner[1:], partner[0], lax.rem(yl + core, 2))
    count = [0]
    local_count = [0]
    sent, maybe = [], []
    pairs = []

    def bring(src, dst):
        copy = pltpu.make_async_copy(src, dst, local_sem.at[local_count[0]])
        local_count[0] += 1
        copy.start()
        return copy

    def number():
        count[0] += 1
        return count[0] - 1

    def describe(src, dst, sem, to):
        return pltpu.make_async_remote_copy(src_ref=src, dst_ref=dst, send_sem=send_sem.at[sem], recv_sem=recv_sem.at[sem], device_id=to, device_id_type=MESH)

    def remote(src, dst, to):
        sem = number()
        copy = describe(src, dst, sem, to)
        copy.start()
        sent.append(copy)
        return sem

    def both(sources, dst, to):
        sem = number()
        for s in (0, 1):
            describe(sources[s], dst.at[s], sem, to).start()
        pairs.append((dst, sem))
        return sem

    def arrive(ref, sem):
        landed(ref, recv_sem.at[sem])

    def exchange(src, dst, d):
        sem = number()
        part = src.at[lax.rem(x + d, 4)]
        copy = describe(part, dst, sem, partner[d])
        if d == 0:
            @pl.when(swapped_place)
            def _():
                copy.start()
            @pl.when(jnp.logical_not(swapped_place))
            def _():
                pltpu.make_async_copy(part, dst, recv_sem.at[sem]).start()
            maybe.append(copy)
        else:
            copy.start()
            sent.append(copy)
        return sem

    def dot(left, right, left_dim, right_dim):
        return lax.dot_general(left, right, (((left_dim,), (right_dim,)), ((), ())), preferred_element_type=f32)

    def group(zz, cc):
        return dkv.at[pl.ds(lax.rem(zz, 4) * 8 + cc * 4, 4)]

    held_sem, held_load = [], []
    for k, zz in enumerate((z + 2, z + 1, z + 3, z)):
        held_sem.append(remote(group(zz, 1 - core), held_in.at[k], sib))
        held_load.append(bring(group(zz, core), held.at[k]))
    inputs = [bring(src, dst) for src, dst in ((two_hbm, normed_two), (grad_hbm, grad), (vectors_hbm, vectors), (up_hbm, up), (down_hbm, down_w),
                                               (tokens_hbm, tokens), (one_hbm, normed_one), (tables_hbm, tables))]
    odq_sem = [exchange(odq, odq_own.at[x], d) for d in range(4)]
    mlp[...] = jnp.zeros_like(mlp)
    back_two[...] = jnp.zeros_like(back_two)
    for copy in inputs:
        copy.wait()
    for i in range(4):
        up_bias[0:1, 768 * i:768 * i + 768] = vectors[8 + i:9 + i]

    def feed(t, _):
        at = pl.ds(pl.multiple_of(t * TILE, TILE), TILE)
        values = dot(normed_two[...], up[:, at], 1, 0) + up_bias[0:1, at]
        inner = 0.5 + 0.5 * erf(values * 0.7071067811865476)
        slope = inner + values * (0.3989422804014327 * jnp.exp(-0.5 * values * values))
        active = (values * inner).astype(bf)
        grads = (dot(grad[...], down_w[at], 1, 1) * slope).astype(bf)
        mlp[...] += dot(active, down_w[at], 1, 0)
        back_two[...] += dot(grads, up[:, at], 1, 1)
        bias_grad[0:1, at] = jnp.sum(grads.astype(f32), 0, keepdims=True)
        upper[:, at] = dot(normed_two[...], grads, 0, 0).astype(bf)
        lower[at] = dot(active, grad[...], 0, 0).astype(bf)
        return 0

    def sum_held(k, chunks, terms):
        def step(i, _):
            j, r = chunks[0] + i // 2, pl.ds(pl.multiple_of(lax.rem(i, 2) * 128, 128), 128)
            value = held[k, j, r].astype(f32) + held_in[k, j, r].astype(f32)
            for ref, low in terms:
                value = value + ref[j - low, r].astype(f32)
            held[k, j, r] = value.astype(bf)
            return 0
        lax.fori_loop(0, 2 * (chunks[1] - chunks[0]), step, 0)

    lax.fori_loop(0, 1, feed, 0)
    held_load[0].wait()
    arrive(held_in.at[0], held_sem[0])
    sum_held(0, (0, 4), [])
    held_far_sem = [remote(held.at[0, pl.ds(2 * way, 2)], held_far.at[way], zs[way]) for way in (0, 1)]
    lax.fori_loop(1, 3, feed, 0)
    held_near_sem = []
    for way in (0, 1):
        k = 1 + way
        held_load[k].wait()
        arrive(held_in.at[k], held_sem[k])
        sum_held(k, (2 - 2 * way, 4 - 2 * way), [])
        arrive(held_far.at[way], held_far_sem[way])
        sum_held(k, (2 * way, 2 * way + 2), [(held_far.at[way], 2 * way)])
        held_near_sem.append(remote(held.at[k], held_near.at[way], zs[way]))
    lax.fori_loop(3, 8, feed, 0)
    fetch = [bring(matrices.at[i], up.at[:, pl.ds(768 * i, 768)]) for i in range(4)]

    def piece(p, w, a):
        if p == 0:
            return down_w.at[pl.ds(pl.multiple_of(a * 768 + w * 192, 192), 192)]
        if p == 1:
            return upper.at[pl.ds(pl.multiple_of(w * 192, 192), 192), pl.ds(pl.multiple_of(a * 768, 768), 768)]
        return lower.at[pl.ds(pl.multiple_of(w * 768 + a * 192, 192), 192), pl.ds(384 * (p - 2), 384)]

    def own(p, k, s):
        return piece(p, 2 * s + core, lax.rem(first[p] + (2, 1, 3, 0)[k], 4))

    def result(p, a, start, size):
        if p < 2:
            return (wide_out, upper_out)[p].at[pl.ds(start, size), pl.ds(pl.multiple_of(a * 768, 768), 768)]
        return lower_out.at[pl.ds(pl.multiple_of(a * 192 + start, 16), size), pl.ds(384 * (p - 2), 384)]

    first = [x if part[1] else z for part in PARTS]
    second = [z if part[1] else x for part in PARTS]
    ring_one = [xs if part[1] else zs for part in PARTS]
    ring_two = [zs if part[1] else xs for part in PARTS]
    sems = {}

    def swap(p):
        for k, ahead in enumerate((2, 1, 3, 0)):
            a = lax.rem(first[p] + ahead, 4)
            sems["sib", p, k] = both([piece(p, 2 * s + 1 - core, a) for s in (0, 1)], sib_in[p].at[k], sib)

    def swapped(p, k):
        arrive(sib_in[p].at[k], sems["sib", p, k])

    def add(rows, into, terms):
        def body(i, _):
            at = pl.ds(pl.multiple_of(i * 48, 48), 48)
            total = into[at].astype(f32)
            for term in terms:
                total = total + term[at].astype(f32)
            into[at] = total.astype(bf)
            return 0
        lax.fori_loop(0, rows // 48, body, 0)

    def quarter(b):
        return pl.ds(pl.multiple_of(lax.rem(b, 4) * 48, 48), 48)

    def far(p):
        swapped(p, 0)
        for s in (0, 1):
            add(192, own(p, 0, s), [sib_in[p].at[0, s]])
            sems["far", p, s] = remote(own(p, 0, s), far_in[p].at[s], ring_one[p][s])

    def near(p):
        for way in (0, 1):
            k = 1 + way
            swapped(p, k)
            add(192, own(p, k, 1 - way), [sib_in[p].at[k, 1 - way]])
            arrive(far_in[p].at[way], sems["far", p, way])
            add(192, own(p, k, way), [sib_in[p].at[k, way], far_in[p].at[way]])
            sems["near", p, way] = both([own(p, k, s) for s in (0, 1)], near_in[p].at[way], ring_one[p][way])

    def mine(p):
        swapped(p, 3)
        for way in (0, 1):
            arrive(near_in[p].at[way], sems["near", p, way])
        for s in (0, 1):
            add(192, own(p, 3, s), [sib_in[p].at[3, s], near_in[p].at[0, s], near_in[p].at[1, s]])
        for s in (0, 1):
            sems["far2", p, s] = remote(own(p, 3, s).at[quarter(second[p] + 2)], far_two[p].at[s], ring_two[p][s])

    def near2(p):
        for way in (0, 1):
            at = quarter(second[p] + 1 + 2 * way)
            arrive(far_two[p].at[way], sems["far2", p, way])
            add(48, own(p, 3, way).at[at], [far_two[p].at[way]])
            sems["near2", p, way] = both([own(p, 3, s).at[at] for s in (0, 1)], near_two[p].at[way], ring_two[p][way])

    def mine2(p):
        at = quarter(second[p])
        for way in (0, 1):
            arrive(near_two[p].at[way], sems["near2", p, way])
        for s in (0, 1):
            add(48, own(p, 3, s).at[at], [near_two[p].at[0, s], near_two[p].at[1, s]])
        for i, half in enumerate((yh, 1 - yh, 1 - yh)):
            sems["y", p, i] = remote(own(p, 3, half).at[at], y_in[p].at[i], ys[i])

    def total(p):
        for i in range(3):
            arrive(y_in[p].at[i], sems["y", p, i])
        value = own(p, 3, yh)[quarter(second[p])].astype(f32)
        for i in range(3):
            value = value + y_in[p][i].astype(f32)
        done = result(p, first[p], pl.multiple_of(second[p] * 48, 16), 48)
        done[...] = value.astype(bf)
        for way in (0, 1):
            sems["ring", p, way] = remote(done, done, ring_two[p][way])

    cuts = ((0, 32), (32, 16))

    def relay(p):
        for way in (0, 1):
            b = lax.rem(second[p] + 3 - 2 * way, 4)
            arrive(result(p, first[p], pl.multiple_of(b * 48, 16), 48), sems["ring", p, way])
            part = result(p, first[p], pl.multiple_of(b * 48 + cuts[way][0], 16), cuts[way][1])
            sems["relay", p, way] = remote(part, part, ring_two[p][way])

    def last(p):
        b = lax.rem(second[p] + 2, 4)
        for way in (0, 1):
            arrive(result(p, first[p], pl.multiple_of(b * 48 + cuts[way][0], 16), cuts[way][1]), sems["relay", p, way])
        block = result(p, first[p], 0, 192)
        for way in (0, 1):
            sems["last", p, way] = remote(block, block, ring_one[p][way])

    def end(p):
        for way in (0, 1):
            a = lax.rem(first[p] + 3 - 2 * way, 4)
            arrive(result(p, a, 0, 192), sems["last", p, way])
            part = result(p, a, 96 * way, 96)
            sems["end", p, way] = remote(part, part, ring_one[p][way])

    def close(p):
        for way in (0, 1):
            arrive(result(p, lax.rem(first[p] + 2, 4), 96 * way, 96), sems["end", p, way])

    def tiny_stage(step):
        groups = ([sib], xs, zs, ys)
        if step > 0:
            for i in range(len(groups[step - 1])):
                arrive(tiny_in.at[step - 1, i], sems["tiny", step - 1, i])
            value = tiny[step - 1]
            for i in range(len(groups[step - 1])):
                value = value + tiny_in[step - 1, i]
            if step == 4:
                vector_out[...] = value
                return
            tiny[step] = value
        for i, to in enumerate(groups[step]):
            sems["tiny", step, i] = remote(tiny.at[step], tiny_in.at[step, i], to)

    group_one = (1, 2, 3)
    for p in group_one:
        swap(p)
    for way in (0, 1):
        arrive(held_near.at[way], held_near_sem[way])
    held_load[3].wait()
    arrive(held_in.at[3], held_sem[3])
    sum_held(3, (0, 4), [(held_near.at[0], 0), (held_near.at[1], 0)])
    dkv_sem = [exchange(held.at[3], dkv_own.at[x], d) for d in range(4)]
    for p in group_one:
        far(p)
    for d in range(4):
        h = lax.rem(x + 4 - d, 4)
        arrive(odq_own.at[h], odq_sem[d])
        arrive(dkv_own.at[h], dkv_sem[d])

    left = lax.broadcasted_iota(jnp.int32, (ROWS, 128), 1) < 64
    keep, ahead, behind = tables[0], tables[1], tables[2]

    def turn_back(tile):
        return tile * keep + pltpu.roll(tile * ahead, 8, 1) + pltpu.roll(tile * behind, 120, 1)

    def unpack(slabs, t):
        even, odd = (slabs[h // 3, :, 128 * (h % 3):128 * (h % 3) + 128].astype(f32) for h in (2 * t, 2 * t + 1))
        return jnp.where(left, even, pltpu.roll(odd, 64, 1)), jnp.where(left, pltpu.roll(even, 64, 1), odd)

    for t in range(6):
        lanes = slice(128 * t, 128 * t + 128)
        out, query = unpack(odq_own, t)
        key, value = unpack(dkv_own, t)
        attended[:, lanes] = out.astype(bf)
        mixed[0, :, lanes] = (turn_back(query) * 0.125).astype(bf)
        mixed[1, :, lanes] = turn_back(key).astype(bf)
        mixed[2, :, lanes] = value.astype(bf)
    g = grad[...]
    one = normed_one[...]
    for i in range(3):
        down_w[768 * i:768 * i + 768] = dot(one, mixed[i], 0, 0).astype(bf)
    down_w[2304:] = dot(attended[...], g, 0, 0).astype(bf)
    swap(0)
    for p in group_one:
        near(p)
    far(0)
    for copy in fetch:
        copy.wait()
    values = tokens[...].astype(f32)
    centered = values - jnp.mean(values, -1, keepdims=True)
    scale = lax.rsqrt(jnp.mean(centered * centered, -1, keepdims=True) + 1e-05)
    unit = centered * scale
    back_one = dot(mixed[0], up[:, 1536:2304], 1, 1) + dot(mixed[1], up[:, 0:768], 1, 1) + dot(mixed[2], up[:, 768:1536], 1, 1)
    wide_grad = g.astype(f32)
    into = wide_grad
    sums = []
    for back, gain in ((back_one, vectors[0:1]), (back_two[...], vectors[2:3])):
        sums.append(jnp.sum(back * unit, 0, keepdims=True))
        sums.append(jnp.sum(back, 0, keepdims=True))
        scaled = back * gain
        into = into + scale * (scaled - jnp.mean(scaled, -1, keepdims=True) - unit * jnp.mean(scaled * unit, -1, keepdims=True))
    input_grad[...] = into.astype(bf)
    sums.append(jnp.sum(wide_grad, 0, keepdims=True))
    sums.extend(jnp.sum(mixed[i].astype(f32), 0, keepdims=True) for i in range(3))
    sums.extend(bias_grad[0:1, 768 * i:768 * i + 768] for i in range(4))
    tiny[0] = jnp.concatenate(sums + [jnp.zeros((4, 768), f32)], 0)
    tiny_stage(0)
    for p in group_one:
        mine(p)
    layer_output[...] = (values + mlp[...] + dot(attended[...], up[:, 2304:3072], 1, 0) + vectors[4:5]).astype(bf)
    tiny_stage(1)
    near(0)
    for p in group_one:
        near2(p)
    tiny_stage(2)
    mine(0)
    for p in group_one:
        mine2(p)
    tiny_stage(3)
    for p in group_one:
        total(p)
    near2(0)
    for p in group_one:
        relay(p)
    mine2(0)
    for p in group_one:
        last(p)
    total(0)
    tiny_stage(4)
    relay(0)
    for p in group_one:
        end(p)
    last(0)
    for p in group_one:
        close(p)
    end(0)
    close(0)
    for ref, sem in pairs:
        landed(ref, send_sem.at[sem])
    for copy in sent:
        copy.wait_send()
    for copy in maybe:
        @pl.when(swapped_place)
        def _():
            copy.wait_send()


def back(odq, dkv, tokens, grad, normed_one, normed_two, vectors, tables, matrices, up, down, collective_id=1):
    hbm = pl.BlockSpec(memory_space=pl.ANY)
    vmem = pl.BlockSpec(memory_space=pltpu.VMEM)
    dma = pltpu.SemaphoreType.DMA
    bf, f32 = jnp.bfloat16, jnp.float32
    scratch = []
    for front_dims, rows in (((4, 2), 192), ((2,), 192), ((2, 2), 192), ((2,), 48), ((2, 2), 48), ((3,), 48)):
        for columns, _ in PARTS:
            scratch.append(pltpu.VMEM(front_dims + (rows, columns), bf))
    plain = ((ROWS, 768), bf)
    for shape, kind in (
        plain, plain, plain, plain, ((16, 768), f32), ((3, ROWS, 128), f32), ((768, 3072), bf), ((3072, 768), bf),
        ((768, 3072), bf), ((3072, 768), bf), ((ROWS, 768), f32), ((ROWS, 768), f32), ((8, 3072), f32), ((8, 3072), f32),
        ((4, 4, ROWS, WIDE), bf), ((4, 4, ROWS, WIDE), bf), ((2, 2, ROWS, WIDE), bf), ((2, 4, ROWS, WIDE), bf),
        ((4, ROWS, WIDE), bf), ((4, ROWS, WIDE), bf), plain, ((3, ROWS, 768), bf), ((4, 16, 768), f32), ((4, 3, 16, 768), f32),
    ):
        scratch.append(pltpu.VMEM(shape, kind))
    scratch += [dma((140,)), dma((140,)), dma((16,))]
    rows = jax.ShapeDtypeStruct((ROWS, 768), bf)
    return pl.pallas_call(
        back_kernel,
        out_shape=(rows, rows, jax.ShapeDtypeStruct((192, 3072), bf), jax.ShapeDtypeStruct((192, 3072), bf),
                   jax.ShapeDtypeStruct((768, 768), bf), jax.ShapeDtypeStruct((16, 768), f32)),
        in_specs=[hbm] * 11, out_specs=(vmem,) * 6,
        scratch_shapes=scratch,
        compiler_params=pltpu.CompilerParams(collective_id=collective_id, has_side_effects=True, vmem_limit_bytes=62 * 2**20),
        name="back",
    )(odq, dkv, tokens, grad, normed_one, normed_two, vectors, tables, matrices, up, down)


D = 768
HEADS = 12
HD = 64
ROT = 16
TOK_DEV = 256


def rotary_tables(positions):
    lanes = jnp.arange(128) % HD
    exponents = (lanes % 8).astype(jnp.float32) * 2.0 / ROT
    inverse = 10000.0 ** (-exponents)
    angles = positions.astype(jnp.float32)[:, None] * inverse[None, :]
    cosine, sine = jnp.cos(angles), jnp.sin(angles)
    keep = jnp.where(lanes < ROT, cosine, 1.0)
    ahead = jnp.where(lanes < 8, -sine, 0.0)
    behind = jnp.where((lanes >= 8) & (lanes < ROT), sine, 0.0)
    return jnp.stack([keep, ahead, behind])


def on_device(
    tokens, cotangent, pairing, first_gain, first_shift, qkv_weight, qkv_bias, dense_weight,
    second_gain, second_shift, up_weight, up_bias, down_weight, out_bias,
):
    bf, f32 = jnp.bfloat16, jnp.float32
    total_blocks = 64
    offsets = jnp.arange(BLK, dtype=jnp.int32)
    ctx_index = lax.axis_index("ctx")
    core = lax.rem(lax.axis_index("wsh"), 2)
    seq_of_layout = jnp.stack([pairing, total_blocks - 1 - pairing], 1).reshape(-1)
    layout_of_seq = (
        jnp.zeros((total_blocks,), jnp.int32)
        .at[seq_of_layout]
        .set(jnp.arange(total_blocks, dtype=jnp.int32))
    )
    own_blocks = lax.dynamic_slice(seq_of_layout, (2 * ctx_index,), (2,))
    row_blocks = lax.dynamic_slice(seq_of_layout, (16 * (ctx_index // 8) + 8 * core,), (8,))
    local_pos = (own_blocks[:, None] * BLK + offsets[None, :]).reshape(-1)
    tables = rotary_tables(local_pos)
    query_scale = HD ** (-0.5)

    shard = lax.broadcasted_iota(jnp.int32, (4, 1), 0) == lax.axis_index("wsh")
    small = (first_gain, first_shift, second_gain, second_shift, out_bias, qkv_bias, up_bias)
    spots = [jnp.where(shard, v[None, :], 0.0).astype(bf).reshape(-1) for v in small]
    vectors = jnp.concatenate(spots + [jnp.zeros((4 * D,), bf)]).reshape(16, D)
    grad_rows = cotangent[0]
    keys_values, queries_grads, normed_one, normed_two, vectors, matrices = front(
        tokens[0], grad_rows, tables, qkv_weight, dense_weight, vectors
    )
    up_shard, down_shard, keys_values = lax.optimization_barrier((up_weight, down_weight, keys_values))
    up_matrix = lax.all_gather(up_shard, "wsh", axis=0, tiled=True)
    down_matrix = lax.all_gather(down_shard, "wsh", axis=0, tiled=True)
    attended_dq, grad_kv = attention(row_blocks, layout_of_seq, queries_grads.reshape(1024, WIDE), keys_values.reshape(8192, WIDE))
    layer_output, input_grad, wide, upper, lower, sums = back(
        attended_dq.reshape(4, ROWS, WIDE), grad_kv.reshape(32, ROWS, WIDE), tokens[0], grad_rows, normed_one, normed_two,
        vectors, tables, matrices, up_matrix, down_matrix,
    )
    mine = lax.axis_index("wsh")
    gains = lax.dynamic_slice(sums, (0, 192 * mine), (5, 192))
    qkv_offset_grad = lax.dynamic_slice(sums[5:8].reshape(-1), (576 * mine,), (576,))
    up_offset_grad = lax.dynamic_slice(sums, (8 + mine, 0), (1, D))[0]
    return (
        layer_output[None], input_grad[None], gains[0], gains[1], wide[:, :2304].astype(f32), qkv_offset_grad,
        wide[:, 2304:].astype(f32), gains[2], gains[3], upper.astype(f32), up_offset_grad, lower.astype(f32), gains[4],
    )


def solution(mesh):
    rows, split, flat = P("wsh", "ctx", None), P("wsh", None), P("wsh")
    return jax.shard_map(
        on_device,
        mesh=mesh,
        in_specs=(rows, rows, P(), flat, flat, split, flat, split, flat, flat, split, flat, split, flat),
        out_specs=(rows, rows, flat, flat, split, flat, split, flat, flat, split, flat, split, flat),
        check_vma=False,
    )
```

```python
import functools

import jax
import jax.numpy as jnp
from jax import lax
from jax.experimental import pallas as pl
from jax.experimental.pallas import tpu as pltpu
from jax.sharding import PartitionSpec as P

G = 3; BLK = 128; LOG2E = 1.4426950408889634
NEG = -1e30

def attn_kernel(chunk, qpos, lay, qdo, kv_hbm, odq, dkv_hbm, kv, kvt, acc, probs, grads, tops, stage, sem, osem):
    blocks = chunk // BLK
    nblk = kv.shape[0] // BLK
    f32, bf = jnp.float32, jnp.bfloat16

    def load(i, _):
        pltpu.make_async_copy(kv_hbm.at[pl.ds(pl.multiple_of(lay[i] * BLK, BLK), BLK)], kv.at[pl.ds(pl.multiple_of(i * BLK, BLK), BLK)], sem.at[i]).start()
        return 0
    lax.fori_loop(0, nblk, load, 0)

    def land(i, _):
        rows = pl.ds(pl.multiple_of(i * chunk, chunk), chunk)
        for j in range(blocks):
            at = pl.ds(pl.multiple_of(i * chunk + j * BLK, BLK), BLK)
            pltpu.make_async_copy(kv_hbm.at[pl.ds(0, BLK)], kv.at[at], sem.at[i * blocks + j]).wait()
        acc[rows] = jnp.zeros((chunk, G * 128), f32)
        kvt[:, rows] = kv[rows].T
        return 0
    lax.fori_loop(0, nblk // blocks, land, 0)

    upper = lax.broadcasted_iota(jnp.int32, (128, 128), 0) < 64
    left = lax.broadcasted_iota(jnp.int32, (128, 128), 1) < 64

    def q_block(i, _):
        b = qpos[i]
        qrows = pl.ds(pl.multiple_of(i * BLK, BLK), BLK)
        last = b // blocks
        pairs = [qdo[qrows, h * 128:(h + 1) * 128] for h in range(G)]
        turned = [p.astype(f32).T for p in pairs]
        wide = [jnp.concatenate([jnp.where(upper, turned[h], 0.0).astype(bf), jnp.where(upper, 0.0, turned[h]).astype(bf)], 1) for h in range(G)]
        rest = b - last * blocks

        def pick(step, state):
            sizes = [chunk * (i + 1) // 4 for i in range(4)]
            return lax.switch(rest // (blocks // 4), [functools.partial(step, size) for size in sizes], state)

        def fwd(c, state, masked, size=chunk):
            at = pl.ds(pl.multiple_of(c * chunk, chunk), size)
            out = []
            every = [jnp.dot(kv[at, h * 128:(h + 1) * 128], wide[h], preferred_element_type=f32) for h in range(G)]
            kept = []
            for h in range(G):
                m, l, o = state[h]
                s = every[h][:, :128]
                grads[at, h * 128:(h + 1) * 128] = every[h][:, 128:]
                if masked:
                    key_i = lax.broadcasted_iota(jnp.int32, (size, BLK), 0)
                    row_i = lax.broadcasted_iota(jnp.int32, (size, BLK), 1) + rest * BLK
                    s = jnp.where(key_i <= row_i, s, NEG)
                new = jnp.maximum(m, jnp.max(s, 0, keepdims=True))
                p = jnp.exp(s - new)
                a = jnp.exp(m - new)
                l = l * a + jnp.sum(p, 0, keepdims=True)
                p = p.astype(bf)
                probs[at, h * 128:(h + 1) * 128] = p
                tops[c, h] = jnp.broadcast_to(new, (8, BLK))
                kept.append((new, l, o * a, p))
            for h in range(G):
                new, l, o, p = kept[h]
                o = o + jnp.dot(kvt[h * 128 + 64:(h + 1) * 128, at], p, preferred_element_type=f32)
                out.append((new, l, o))
            return tuple(out)

        state = tuple((jnp.full((1, BLK), NEG, f32), jnp.zeros((1, BLK), f32), jnp.zeros((64, BLK), f32)) for _ in range(G))
        state = lax.fori_loop(0, last, lambda c, s: fwd(c, s, False), state)
        state = pick(lambda size, s: fwd(last, s, True, size), state)
        lse, delta, outs = [], [], []
        for h in range(G):
            m, l, o = state[h]
            o = o / l
            outs.append(o)
            lse.append(m + jnp.log(l))
            delta.append(jnp.sum(o * turned[h][64:], 0, keepdims=True))
        narrow = [jnp.concatenate([jnp.where(left, pairs[h], jnp.zeros_like(pairs[h])), jnp.where(left, jnp.zeros_like(pairs[h]), pairs[h])], 0) for h in range(G)]

        def bwd(c, state, size=chunk):
            at = pl.ds(pl.multiple_of(c * chunk, chunk), size)
            out, work = [], []
            for h in range(G):
                cols = slice(h * 128, (h + 1) * 128)
                p = probs[at, cols].astype(f32) * jnp.exp(tops[c, h, 0:1] - lse[h])
                ds = (p * (grads[at, cols] - delta[h])).astype(bf)
                work.append((jnp.concatenate([ds, p.astype(bf)], 1), ds))
            for h in range(G):
                pair, ds = work[h]
                acc[at, h * 128:(h + 1) * 128] += jnp.dot(pair, narrow[h], preferred_element_type=f32)
                out.append(state[h] + jnp.dot(kvt[h * 128:h * 128 + 64, at], ds, preferred_element_type=f32))
            return tuple(out)

        dq = tuple(jnp.zeros((64, BLK), f32) for _ in range(G))
        dq = lax.fori_loop(0, last, bwd, dq)
        dq = pick(lambda size, s: bwd(last, s, size), dq)
        for h in range(G):
            odq[qrows, h * 128:(h + 1) * 128] = jnp.concatenate([outs[h], dq[h]], 0).T.astype(bf)
        return 0
    lax.fori_loop(0, qpos.shape[0], q_block, 0)

    def leave(slot, j):
        return pltpu.make_async_copy(stage.at[slot, j], dkv_hbm.at[pl.ds(0, BLK)], osem.at[slot, j])

    def send(i, _):
        slot = lax.rem(i, 2)
        @pl.when(i >= 2)
        def _():
            for j in range(4):
                leave(slot, j).wait()
        for j in range(4):
            at = i * 4 + j
            stage[slot, j] = acc[pl.ds(pl.multiple_of(at * BLK, BLK), BLK)].astype(bf)
            pltpu.make_async_copy(stage.at[slot, j], dkv_hbm.at[pl.ds(pl.multiple_of(lay[at] * BLK, BLK), BLK)], osem.at[slot, j]).start()
        return 0
    lax.fori_loop(0, nblk // 4, send, 0)
    for slot in range(2):
        for j in range(4):
            leave(slot, j).wait()


def attention(qpos, lay, qdo, kv, chunk=1024):
    n = kv.shape[0]
    smem = pl.BlockSpec(memory_space=pltpu.SMEM)
    vmem = pl.BlockSpec(memory_space=pltpu.VMEM)
    hbm = pl.BlockSpec(memory_space=pl.ANY)
    return pl.pallas_call(
        functools.partial(attn_kernel, chunk),
        out_shape=(jax.ShapeDtypeStruct(qdo.shape, jnp.bfloat16), jax.ShapeDtypeStruct(kv.shape, jnp.bfloat16)),
        in_specs=[smem, smem, vmem, hbm], out_specs=(vmem, hbm),
        scratch_shapes=[pltpu.VMEM((n, G * 128), jnp.bfloat16), pltpu.VMEM((G * 128, n), jnp.bfloat16),
            pltpu.VMEM((n, G * 128), jnp.float32), pltpu.VMEM((n, G * 128), jnp.bfloat16), pltpu.VMEM((n, G * 128), jnp.float32), pltpu.VMEM((n // chunk, G, 8, BLK), jnp.float32),
            pltpu.VMEM((2, 4, BLK, G * 128), jnp.bfloat16),
            pltpu.SemaphoreType.DMA((n // BLK,)), pltpu.SemaphoreType.DMA((2, 4))],
        compiler_params=pltpu.CompilerParams(vmem_limit_bytes=62 * 2**20),
        name="attention",
    )(qpos, lay, qdo, kv)


MESH = pl.DeviceIdType.MESH
ROWS, WIDE = 256, 384


def place():
    c, w = lax.axis_index("ctx"), lax.axis_index("wsh")
    return c // 8, lax.rem(c // 4, 2), lax.rem(c, 4), w // 2, lax.rem(w, 2)


def device(z, yl, x, yh, core):
    return (z * 8 + yl * 4 + x, yh * 2 + core)


def greet(devices, extra=None, extra_count=0):
    barrier = pltpu.get_barrier_semaphore()
    for d in devices:
        pl.semaphore_signal(barrier, inc=1, device_id=d, device_id_type=MESH)
    if extra is not None:
        @pl.when(extra_count == 1)
        def _():
            pl.semaphore_signal(barrier, inc=1, device_id=extra, device_id_type=MESH)
    pl.semaphore_wait(barrier, len(devices) + extra_count)


def landed(ref, sem):
    pltpu.make_async_copy(ref, ref, sem).wait()


def front_kernel(tokens_hbm, grad_hbm, tables_hbm, qkv, dense, vectors_hbm, kv_all, qdo, one_hbm, two_hbm, vectors_out, weights_out,
                 tokens, grad, tables, vectors, normed_one, normed_two, all_vectors, bring_sem, weights, vec_in, kvs, qds, local_sem, send_sem, recv_sem, kv_send, kv_recv, q_send, q_recv):
    z, yl, x, yh, core = place()
    bring = [pltpu.make_async_copy(src, dst, bring_sem.at[i]) for i, (src, dst) in enumerate(((vectors_hbm, vectors), (tokens_hbm, tokens), (tables_hbm, tables), (grad_hbm, grad)))]
    for copy in bring:
        copy.start()
    f32, bf = jnp.float32, jnp.bfloat16
    me = yh * 2 + core
    far = (1 - yh) * 2 + core
    other = (1 - yh) * 2 + 1 - core
    swap = yl != core
    partner = [device(z, core, lax.rem(x + d, 4), yh, yl) for d in range(4)]
    sib = device(z, yl, x, yh, 1 - core)
    cross = device(z, 1 - yl, x, 1 - yh, core)
    others = [device(z, yl, x, 1 - yh, core), device(z, yl, x, 1 - yh, 1 - core)]
    xs = [device(z, yl, lax.rem(x + d, 4), yh, core) for d in (1, 3)]
    zs = [device(lax.rem(z + d, 4), yl, x, yh, core) for d in (1, 3)]
    greet([sib, cross] + others + xs + zs + partner[1:], partner[0], lax.rem(yl + core, 2))
    count = [0]
    sent = []

    def remote(src, dst, to):
        sem = count[0]
        count[0] += 1
        copy = pltpu.make_async_remote_copy(src_ref=src, dst_ref=dst, send_sem=send_sem.at[sem], recv_sem=recv_sem.at[sem], device_id=to, device_id_type=MESH)
        copy.start()
        sent.append(copy)
        return sem

    def arrive(ref, sem):
        landed(ref, recv_sem.at[sem])

    def rows(i, start, size):
        return weights.at[i, pl.ds(pl.multiple_of(start, 16), size)]

    shards = [qkv.at[:, pl.ds(768, 768)], qkv.at[:, pl.ds(1536, 768)], qkv.at[:, pl.ds(0, 768)], dense]
    quarter = [x, z, x, z]
    ring = [xs, zs, xs, zs]
    bring[0].wait()
    vec_sem = [remote(vectors, vec_in.at[i], to) for i, to in enumerate([sib] + others)]
    cross_sem = [remote(shards[i].at[pl.ds(pl.multiple_of(quarter[i] * 48, 16), 48)], rows(i, me * 192 + quarter[i] * 48, 48), cross) for i in range(4)]
    own, late = [], [[], [], [], []]
    for i in range(4):
        copy = pltpu.make_async_copy(shards[i], rows(i, me * 192, 192), local_sem.at[i])
        copy.start()
        own.append(copy)
        late[i].append((rows(i, (yh * 2 + 1 - core) * 192, 192), remote(shards[i], rows(i, me * 192, 192), sib)))

    for copy in bring[1:]:
        copy.wait()
    values = tokens[...].astype(f32)
    centered = values - jnp.mean(values, -1, keepdims=True)
    unit = centered * lax.rsqrt(jnp.mean(centered * centered, -1, keepdims=True) + 1e-05)
    for i in range(3):
        arrive(vec_in.at[i], vec_sem[i])
    vec = vectors[...].astype(f32) + vec_in[0].astype(f32) + vec_in[1].astype(f32) + vec_in[2].astype(f32)
    all_vectors[...] = vec
    normed_one[...] = (unit * vec[0:1] + vec[1:2]).astype(bf)
    normed_two[...] = (unit * vec[2:3] + vec[3:4]).astype(bf)

    leave = [pltpu.make_async_copy(src, dst, bring_sem.at[4 + i]) for i, (src, dst) in enumerate(((all_vectors, vectors_out), (normed_one, one_hbm), (normed_two, two_hbm)))]
    for copy in leave:
        copy.start()
    cuts = ((0, 32), (32, 16))
    ring_sem, half_sem = {}, {}

    def start_ring(i):
        mine = rows(i, far * 192 + quarter[i] * 48, 48)
        arrive(mine, cross_sem[i])
        for way in (0, 1):
            ring_sem[i, way] = remote(mine, mine, ring[i][way])
        late[i].append((rows(i, other * 192 + quarter[i] * 48, 48), remote(mine, mine, sib)))

    def relay(i):
        for way in (0, 1):
            b = lax.rem(quarter[i] + 3 - 2 * way, 4)
            got = rows(i, far * 192 + b * 48, 48)
            arrive(got, ring_sem[i, way])
            part = rows(i, far * 192 + b * 48 + cuts[way][0], cuts[way][1])
            half_sem[i, way] = remote(part, part, ring[i][way])
            late[i].append((rows(i, other * 192 + b * 48, 48), remote(got, got, sib)))

    def finish(i):
        for way in (0, 1):
            start = lax.rem(quarter[i] + 2, 4) * 48 + cuts[way][0]
            got = rows(i, far * 192 + start, cuts[way][1])
            arrive(got, half_sem[i, way])
            late[i].append((rows(i, other * 192 + start, cuts[way][1]), remote(got, got, sib)))

    def complete(i):
        for ref, sem in late[i]:
            arrive(ref, sem)
        own[i].wait()

    left = lax.broadcasted_iota(jnp.int32, (ROWS, 128), 1) < 64
    keep, ahead, behind = tables[0], tables[1], tables[2]

    def turn(tile):
        return tile * keep + pltpu.roll(tile, 120, 1) * ahead + pltpu.roll(tile, 8, 1) * behind

    def pack(into, first, second):
        for t in range(6):
            lanes = slice(128 * t, 128 * t + 128)
            a, b = first(lanes), second(lanes)
            for head, tile in ((2 * t, jnp.where(left, a, pltpu.roll(b, 64, 1))), (2 * t + 1, jnp.where(left, pltpu.roll(a, 64, 1), b))):
                into[head // 3, :, 128 * (head % 3):128 * (head % 3) + 128] = tile.astype(bf)

    def dot(a, b):
        return jnp.dot(a, b, preferred_element_type=f32)

    def exchange(src, dst_of, send, recv):
        out = []
        for d in (0, 2, 1, 3):
            args = (src.at[lax.rem(x + d, 4)], dst_of, send.at[d], recv.at[d], partner[d])
            copy = pltpu.make_async_remote_copy(src_ref=args[0], dst_ref=args[1], send_sem=args[2], recv_sem=args[3], device_id=args[4], device_id_type=MESH)
            if d == 0:
                @pl.when(swap)
                def _():
                    copy.start()
                @pl.when(jnp.logical_not(swap))
                def _():
                    pltpu.make_async_copy(args[0], args[1], args[3]).start()
            else:
                copy.start()
            out.append((d, copy))
        return out

    for i in range(4):
        start_ring(i)
    for i in (0, 1):
        relay(i)
    for i in (0, 1):
        finish(i)
    for i in (0, 1):
        complete(i)
    one = normed_one[...]
    pack(kvs,
         lambda lanes: turn(dot(one, weights[0, :, lanes]) + vec[6:7, lanes]),
         lambda lanes: dot(one, weights[1, :, lanes]) + vec[7:8, lanes])
    mine = z * 8 + yl * 4 + x
    sent_kv = exchange(kvs, kv_all.at[mine], kv_send, kv_recv)
    for i in (2, 3):
        relay(i)
    for i in (2, 3):
        finish(i)
    for i in (2, 3):
        complete(i)
    g = grad[...]
    pack(qds,
         lambda lanes: turn(dot(one, weights[2, :, lanes]) + vec[5:6, lanes]) * 0.125,
         lambda lanes: lax.dot_general(g, weights[3, lanes, :], (((1,), (1,)), ((), ())), preferred_element_type=f32))
    sent_q = exchange(qds, qdo.at[x], q_send, q_recv)
    keep_out = pltpu.make_async_copy(weights, weights_out, local_sem.at[4])
    keep_out.start()

    def slot(zz, cc, d):
        return kv_all.at[lax.rem(zz, 4) * 8 + cc * 4 + lax.rem(x + 4 - d, 4)]

    half = ROWS // 2
    up_sem, part_sem, sib_sem = {}, {}, {}
    for d in (0, 1, 3, 2):
        here = slot(z, core, d)
        landed(here, kv_recv.at[d])
        for way in (0, 1):
            up_sem[way, d] = remote(here, here, zs[way])
        sib_sem[0, d] = remote(here, here, sib)
    for d in (0, 1, 3, 2):
        for way in (0, 1):
            here = slot(z + 3 - 2 * way, core, d)
            arrive(here, up_sem[way, d])
            part = here.at[pl.ds(way * half, half)]
            part_sem[way, d] = remote(part, part, zs[way])
            sib_sem[1 + way, d] = remote(here, here, sib)
    for d in (0, 1, 3, 2):
        for way in (0, 1):
            part = slot(z + 2, core, d).at[pl.ds(way * half, half)]
            arrive(part, part_sem[way, d])
            sib_sem[3 + way, d] = remote(part, part, sib)
    for d in range(4):
        arrive(slot(z, 1 - core, d), sib_sem[0, d])
        for way in (0, 1):
            arrive(slot(z + 3 - 2 * way, 1 - core, d), sib_sem[1 + way, d])
            arrive(slot(z + 2, 1 - core, d).at[pl.ds(way * half, half)], sib_sem[3 + way, d])
        landed(qdo.at[lax.rem(x + 4 - d, 4)], q_recv.at[d])
    keep_out.wait()
    for copy in leave:
        copy.wait()
    for copy in sent:
        copy.wait_send()
    for d, copy in sent_kv + sent_q:
        if d == 0:
            @pl.when(swap)
            def _():
                copy.wait_send()
        else:
            copy.wait_send()


def front(tokens, grad, tables, qkv, dense, vectors, collective_id=0):
    hbm = pl.BlockSpec(memory_space=pl.ANY)
    dma = pltpu.SemaphoreType.DMA
    bf, f32 = jnp.bfloat16, jnp.float32
    rows = jax.ShapeDtypeStruct((ROWS, 768), bf)
    return pl.pallas_call(
        front_kernel,
        out_shape=(jax.ShapeDtypeStruct((32, ROWS, WIDE), bf), jax.ShapeDtypeStruct((4, ROWS, WIDE), bf), rows, rows,
                   jax.ShapeDtypeStruct((16, 768), f32), jax.ShapeDtypeStruct((4, 768, 768), bf)),
        in_specs=[hbm] * 6, out_specs=(hbm,) * 6,
        scratch_shapes=[pltpu.VMEM((ROWS, 768), bf), pltpu.VMEM((ROWS, 768), bf), pltpu.VMEM((3, ROWS, 128), f32), pltpu.VMEM((16, 768), bf),
                        pltpu.VMEM((ROWS, 768), bf), pltpu.VMEM((ROWS, 768), bf), pltpu.VMEM((16, 768), f32), dma((7,)), pltpu.VMEM((4, 768, 768), bf), pltpu.VMEM((3, 16, 768), bf), pltpu.VMEM((4, ROWS, WIDE), bf), pltpu.VMEM((4, ROWS, WIDE), bf),
                        dma((5,)), dma((100,)), dma((100,)), dma((4,)), dma((4,)), dma((4,)), dma((4,))],
        compiler_params=pltpu.CompilerParams(collective_id=collective_id, has_side_effects=True, vmem_limit_bytes=62 * 2**20),
        name="front",
    )(tokens, grad, tables, qkv, dense, vectors)


PARTS = ((384, False), (384, True), (768, True), (384, True), (384, False))
TILE = 384


def erf(values):
    v = jnp.clip(values, -4.0, 4.0)
    s = v * v
    top = jnp.float32(-2.72614225801306e-10)
    for coefficient in (2.77068142495902e-08, -2.10102402082508e-06, -5.69250639462346e-05, -7.34990630326855e-04, -2.95459980854025e-03, -1.60960333262415e-02):
        top = top * s + coefficient
    low = jnp.float32(-1.45660718464996e-05)
    for coefficient in (-2.13374055278905e-04, -1.68282697438203e-03, -7.37332916720468e-03, -1.42647390514189e-02):
        low = low * s + coefficient
    return v * top / low


def back_kernel(odq, dkv, tokens_hbm, grad_hbm, one_hbm, two_hbm, vectors_hbm, tables_hbm, matrices, up_hbm, down_hbm,
                layer_output, input_grad, wide_out, upper_out, lower_out, vector_out, *refs):
    sib_in, far_in, near_in, far_two, near_two, y_in = (refs[5 * i : 5 * i + 5] for i in range(6))
    (tokens, grad, normed_one, normed_two, vectors, tables, up, down_w, upper, lower, mlp, back_two, up_bias, bias_grad,
     held, held_in, held_far, held_near, odq_own, dkv_own, attended, mixed, tiny, tiny_in, send_sem, recv_sem, local_sem) = refs[30:]
    z, yl, x, yh, core = place()
    f32, bf = jnp.float32, jnp.bfloat16
    swapped_place = yl != core
    partner = [device(z, core, lax.rem(x + d, 4), yh, yl) for d in range(4)]
    xs = [device(z, yl, lax.rem(x + d, 4), yh, core) for d in (1, 3, 2)]
    zs = [device(lax.rem(z + d, 4), yl, x, yh, core) for d in (1, 3, 2)]
    ys = [device(z, 1 - yl, x, yh, core), device(z, yl, x, 1 - yh, core), device(z, 1 - yl, x, 1 - yh, core)]
    sib = device(z, yl, x, yh, 1 - core)
    greet([sib] + xs + zs + ys + partner[1:], partner[0], lax.rem(yl + core, 2))
    count = [0]
    local_count = [0]
    sent, maybe = [], []
    pairs = []

    def bring(src, dst):
        copy = pltpu.make_async_copy(src, dst, local_sem.at[local_count[0]])
        local_count[0] += 1
        copy.start()
        return copy

    def number():
        count[0] += 1
        return count[0] - 1

    def describe(src, dst, sem, to):
        return pltpu.make_async_remote_copy(src_ref=src, dst_ref=dst, send_sem=send_sem.at[sem], recv_sem=recv_sem.at[sem], device_id=to, device_id_type=MESH)

    def remote(src, dst, to):
        sem = number()
        copy = describe(src, dst, sem, to)
        copy.start()
        sent.append(copy)
        return sem

    def both(sources, dst, to):
        sem = number()
        for s in (0, 1):
            describe(sources[s], dst.at[s], sem, to).start()
        pairs.append((dst, sem))
        return sem

    def arrive(ref, sem):
        landed(ref, recv_sem.at[sem])

    def exchange(src, dst, d):
        sem = number()
        part = src.at[lax.rem(x + d, 4)]
        copy = describe(part, dst, sem, partner[d])
        if d == 0:
            @pl.when(swapped_place)
            def _():
                copy.start()
            @pl.when(jnp.logical_not(swapped_place))
            def _():
                pltpu.make_async_copy(part, dst, recv_sem.at[sem]).start()
            maybe.append(copy)
        else:
            copy.start()
            sent.append(copy)
        return sem

    def dot(left, right, left_dim, right_dim):
        return lax.dot_general(left, right, (((left_dim,), (right_dim,)), ((), ())), preferred_element_type=f32)

    def group(zz, cc):
        return dkv.at[pl.ds(lax.rem(zz, 4) * 8 + cc * 4, 4)]

    held_sem, held_load = [], []
    for k, zz in enumerate((z + 2, z + 1, z + 3, z)):
        held_sem.append(remote(group(zz, 1 - core), held_in.at[k], sib))
        held_load.append(bring(group(zz, core), held.at[k]))
    inputs = [bring(src, dst) for src, dst in ((two_hbm, normed_two), (grad_hbm, grad), (vectors_hbm, vectors), (up_hbm, up), (down_hbm, down_w),
                                               (tokens_hbm, tokens), (one_hbm, normed_one), (tables_hbm, tables))]
    odq_sem = [exchange(odq, odq_own.at[x], d) for d in range(4)]
    mlp[...] = jnp.zeros_like(mlp)
    back_two[...] = jnp.zeros_like(back_two)
    for copy in inputs:
        copy.wait()
    for i in range(4):
        up_bias[0:1, 768 * i:768 * i + 768] = vectors[8 + i:9 + i]

    def feed(t, _):
        at = pl.ds(pl.multiple_of(t * TILE, TILE), TILE)
        values = dot(normed_two[...], up[:, at], 1, 0) + up_bias[0:1, at]
        inner = 0.5 + 0.5 * erf(values * 0.7071067811865476)
        slope = inner + values * (0.3989422804014327 * jnp.exp(-0.5 * values * values))
        active = (values * inner).astype(bf)
        grads = (dot(grad[...], down_w[at], 1, 1) * slope).astype(bf)
        mlp[...] += dot(active, down_w[at], 1, 0)
        back_two[...] += dot(grads, up[:, at], 1, 1)
        bias_grad[0:1, at] = jnp.sum(grads.astype(f32), 0, keepdims=True)
        upper[:, at] = dot(normed_two[...], grads, 0, 0).astype(bf)
        lower[at] = dot(active, grad[...], 0, 0).astype(bf)
        return 0

    def sum_held(k, chunks, terms):
        def step(i, _):
            j, r = chunks[0] + i // 2, pl.ds(pl.multiple_of(lax.rem(i, 2) * 128, 128), 128)
            value = held[k, j, r].astype(f32) + held_in[k, j, r].astype(f32)
            for ref, low in terms:
                value = value + ref[j - low, r].astype(f32)
            held[k, j, r] = value.astype(bf)
            return 0
        lax.fori_loop(0, 2 * (chunks[1] - chunks[0]), step, 0)

    lax.fori_loop(0, 1, feed, 0)
    held_load[0].wait()
    arrive(held_in.at[0], held_sem[0])
    sum_held(0, (0, 4), [])
    held_far_sem = [remote(held.at[0, pl.ds(2 * way, 2)], held_far.at[way], zs[way]) for way in (0, 1)]
    lax.fori_loop(1, 3, feed, 0)
    held_near_sem = []
    for way in (0, 1):
        k = 1 + way
        held_load[k].wait()
        arrive(held_in.at[k], held_sem[k])
        sum_held(k, (2 - 2 * way, 4 - 2 * way), [])
        arrive(held_far.at[way], held_far_sem[way])
        sum_held(k, (2 * way, 2 * way + 2), [(held_far.at[way], 2 * way)])
        held_near_sem.append(remote(held.at[k], held_near.at[way], zs[way]))
    lax.fori_loop(3, 8, feed, 0)
    fetch = [bring(matrices.at[i], up.at[:, pl.ds(768 * i, 768)]) for i in range(4)]

    def piece(p, w, a):
        if p < 2:
            return down_w.at[pl.ds(pl.multiple_of(a * 768 + w * 192, 192), 192), pl.ds(384 * p, 384)]
        if p == 2:
            return upper.at[pl.ds(pl.multiple_of(w * 192, 192), 192), pl.ds(pl.multiple_of(a * 768, 768), 768)]
        return lower.at[pl.ds(pl.multiple_of(w * 768 + a * 192, 192), 192), pl.ds(384 * (p - 3), 384)]

    def own(p, k, s):
        return piece(p, 2 * s + core, lax.rem(first[p] + (2, 1, 3, 0)[k], 4))

    def result(p, a, start, size):
        if p < 2:
            return wide_out.at[pl.ds(start, size), pl.ds(pl.multiple_of(a * 768 + 384 * p, 384), 384)]
        if p == 2:
            return upper_out.at[pl.ds(start, size), pl.ds(pl.multiple_of(a * 768, 768), 768)]
        return lower_out.at[pl.ds(pl.multiple_of(a * 192 + start, 16), size), pl.ds(384 * (p - 3), 384)]

    first = [x if part[1] else z for part in PARTS]
    second = [z if part[1] else x for part in PARTS]
    ring_one = [xs if part[1] else zs for part in PARTS]
    ring_two = [zs if part[1] else xs for part in PARTS]
    sems = {}

    def swap(p):
        for k, ahead in enumerate((2, 1, 3, 0)):
            a = lax.rem(first[p] + ahead, 4)
            sems["sib", p, k] = both([piece(p, 2 * s + 1 - core, a) for s in (0, 1)], sib_in[p].at[k], sib)

    def swapped(p, k):
        arrive(sib_in[p].at[k], sems["sib", p, k])

    def add(rows, into, terms):
        def body(i, _):
            at = pl.ds(pl.multiple_of(i * 48, 48), 48)
            total = into[at].astype(f32)
            for term in terms:
                total = total + term[at].astype(f32)
            into[at] = total.astype(bf)
            return 0
        lax.fori_loop(0, rows // 48, body, 0)

    def quarter(b):
        return pl.ds(pl.multiple_of(lax.rem(b, 4) * 48, 48), 48)

    def far(p):
        swapped(p, 0)
        for s in (0, 1):
            add(192, own(p, 0, s), [sib_in[p].at[0, s]])
            sems["far", p, s] = remote(own(p, 0, s), far_in[p].at[s], ring_one[p][s])

    def near(p):
        for way in (0, 1):
            k = 1 + way
            swapped(p, k)
            add(192, own(p, k, 1 - way), [sib_in[p].at[k, 1 - way]])
            arrive(far_in[p].at[way], sems["far", p, way])
            add(192, own(p, k, way), [sib_in[p].at[k, way], far_in[p].at[way]])
            sems["near", p, way] = both([own(p, k, s) for s in (0, 1)], near_in[p].at[way], ring_one[p][way])

    def mine(p):
        swapped(p, 3)
        for way in (0, 1):
            arrive(near_in[p].at[way], sems["near", p, way])
        for s in (0, 1):
            add(192, own(p, 3, s), [sib_in[p].at[3, s], near_in[p].at[0, s], near_in[p].at[1, s]])
        for s in (0, 1):
            sems["far2", p, s] = remote(own(p, 3, s).at[quarter(second[p] + 2)], far_two[p].at[s], ring_two[p][s])

    def near2(p):
        for way in (0, 1):
            at = quarter(second[p] + 1 + 2 * way)
            arrive(far_two[p].at[way], sems["far2", p, way])
            add(48, own(p, 3, way).at[at], [far_two[p].at[way]])
            sems["near2", p, way] = both([own(p, 3, s).at[at] for s in (0, 1)], near_two[p].at[way], ring_two[p][way])

    def mine2(p):
        at = quarter(second[p])
        for way in (0, 1):
            arrive(near_two[p].at[way], sems["near2", p, way])
        for s in (0, 1):
            add(48, own(p, 3, s).at[at], [near_two[p].at[0, s], near_two[p].at[1, s]])
        for i, half in enumerate((yh, 1 - yh, 1 - yh)):
            sems["y", p, i] = remote(own(p, 3, half).at[at], y_in[p].at[i], ys[i])

    def total(p):
        for i in range(3):
            arrive(y_in[p].at[i], sems["y", p, i])
        value = own(p, 3, yh)[quarter(second[p])].astype(f32)
        for i in range(3):
            value = value + y_in[p][i].astype(f32)
        done = result(p, first[p], pl.multiple_of(second[p] * 48, 16), 48)
        done[...] = value.astype(bf)
        for way in (0, 1):
            sems["ring", p, way] = remote(done, done, ring_two[p][way])

    cuts = ((0, 32), (32, 16))

    def relay(p):
        for way in (0, 1):
            b = lax.rem(second[p] + 3 - 2 * way, 4)
            arrive(result(p, first[p], pl.multiple_of(b * 48, 16), 48), sems["ring", p, way])
            part = result(p, first[p], pl.multiple_of(b * 48 + cuts[way][0], 16), cuts[way][1])
            sems["relay", p, way] = remote(part, part, ring_two[p][way])

    def last(p):
        b = lax.rem(second[p] + 2, 4)
        for way in (0, 1):
            arrive(result(p, first[p], pl.multiple_of(b * 48 + cuts[way][0], 16), cuts[way][1]), sems["relay", p, way])
        block = result(p, first[p], 0, 192)
        for way in (0, 1):
            sems["last", p, way] = remote(block, block, ring_one[p][way])

    def end(p):
        for way in (0, 1):
            a = lax.rem(first[p] + 3 - 2 * way, 4)
            arrive(result(p, a, 0, 192), sems["last", p, way])
            part = result(p, a, 96 * way, 96)
            sems["end", p, way] = remote(part, part, ring_one[p][way])

    def close(p):
        for way in (0, 1):
            arrive(result(p, lax.rem(first[p] + 2, 4), 96 * way, 96), sems["end", p, way])

    def tiny_stage(step):
        groups = ([sib], xs, zs, ys)
        if step > 0:
            for i in range(len(groups[step - 1])):
                arrive(tiny_in.at[step - 1, i], sems["tiny", step - 1, i])
            value = tiny[step - 1]
            for i in range(len(groups[step - 1])):
                value = value + tiny_in[step - 1, i]
            if step == 4:
                vector_out[...] = value
                return
            tiny[step] = value
        for i, to in enumerate(groups[step]):
            sems["tiny", step, i] = remote(tiny.at[step], tiny_in.at[step, i], to)

    group_one, group_two = (2, 3, 4), (0, 1)
    for p in group_one:
        swap(p)
    for way in (0, 1):
        arrive(held_near.at[way], held_near_sem[way])
    held_load[3].wait()
    arrive(held_in.at[3], held_sem[3])
    sum_held(3, (0, 4), [(held_near.at[0], 0), (held_near.at[1], 0)])
    dkv_sem = [exchange(held.at[3], dkv_own.at[x], d) for d in range(4)]
    for p in group_one:
        far(p)
    for d in range(4):
        h = lax.rem(x + 4 - d, 4)
        arrive(odq_own.at[h], odq_sem[d])
        arrive(dkv_own.at[h], dkv_sem[d])

    left = lax.broadcasted_iota(jnp.int32, (ROWS, 128), 1) < 64
    keep, ahead, behind = tables[0], tables[1], tables[2]

    def turn_back(tile):
        return tile * keep + pltpu.roll(tile * ahead, 8, 1) + pltpu.roll(tile * behind, 120, 1)

    def unpack(slabs, t):
        even, odd = (slabs[h // 3, :, 128 * (h % 3):128 * (h % 3) + 128].astype(f32) for h in (2 * t, 2 * t + 1))
        return jnp.where(left, even, pltpu.roll(odd, 64, 1)), jnp.where(left, pltpu.roll(even, 64, 1), odd)

    for t in range(6):
        lanes = slice(128 * t, 128 * t + 128)
        out, query = unpack(odq_own, t)
        key, value = unpack(dkv_own, t)
        attended[:, lanes] = out.astype(bf)
        mixed[0, :, lanes] = (turn_back(query) * 0.125).astype(bf)
        mixed[1, :, lanes] = turn_back(key).astype(bf)
        mixed[2, :, lanes] = value.astype(bf)
    g = grad[...]
    one = normed_one[...]
    for i in range(3):
        down_w[768 * i:768 * i + 768] = dot(one, mixed[i], 0, 0).astype(bf)
    down_w[2304:] = dot(attended[...], g, 0, 0).astype(bf)
    for p in group_two:
        swap(p)
    for p in group_one:
        near(p)
    for p in group_two:
        far(p)
    for copy in fetch:
        copy.wait()
    values = tokens[...].astype(f32)
    centered = values - jnp.mean(values, -1, keepdims=True)
    scale = lax.rsqrt(jnp.mean(centered * centered, -1, keepdims=True) + 1e-05)
    unit = centered * scale
    back_one = dot(mixed[0], up[:, 1536:2304], 1, 1) + dot(mixed[1], up[:, 0:768], 1, 1) + dot(mixed[2], up[:, 768:1536], 1, 1)
    wide_grad = g.astype(f32)
    into = wide_grad
    sums = []
    for back, gain in ((back_one, vectors[0:1]), (back_two[...], vectors[2:3])):
        sums.append(jnp.sum(back * unit, 0, keepdims=True))
        sums.append(jnp.sum(back, 0, keepdims=True))
        scaled = back * gain
        into = into + scale * (scaled - jnp.mean(scaled, -1, keepdims=True) - unit * jnp.mean(scaled * unit, -1, keepdims=True))
    input_grad[...] = into.astype(bf)
    sums.append(jnp.sum(wide_grad, 0, keepdims=True))
    sums.extend(jnp.sum(mixed[i].astype(f32), 0, keepdims=True) for i in range(3))
    sums.extend(bias_grad[0:1, 768 * i:768 * i + 768] for i in range(4))
    tiny[0] = jnp.concatenate(sums + [jnp.zeros((4, 768), f32)], 0)
    tiny_stage(0)
    for p in group_one:
        mine(p)
    layer_output[...] = (values + mlp[...] + dot(attended[...], up[:, 2304:3072], 1, 0) + vectors[4:5]).astype(bf)
    tiny_stage(1)
    for p in group_two:
        near(p)
    for p in group_one:
        near2(p)
    tiny_stage(2)
    for p in group_two:
        mine(p)
    for p in group_one:
        mine2(p)
    tiny_stage(3)
    for p in group_one:
        total(p)
    for p in group_two:
        near2(p)
    for p in group_one:
        relay(p)
    for p in group_two:
        mine2(p)
    for p in group_one:
        last(p)
    for p in group_two:
        total(p)
    tiny_stage(4)
    for p in group_two:
        relay(p)
    for p in group_one:
        end(p)
    for p in group_two:
        last(p)
    for p in group_one:
        close(p)
    for p in group_two:
        end(p)
    for p in group_two:
        close(p)
    for ref, sem in pairs:
        landed(ref, send_sem.at[sem])
    for copy in sent:
        copy.wait_send()
    for copy in maybe:
        @pl.when(swapped_place)
        def _():
            copy.wait_send()


def back(odq, dkv, tokens, grad, normed_one, normed_two, vectors, tables, matrices, up, down, collective_id=1):
    hbm = pl.BlockSpec(memory_space=pl.ANY)
    vmem = pl.BlockSpec(memory_space=pltpu.VMEM)
    dma = pltpu.SemaphoreType.DMA
    bf, f32 = jnp.bfloat16, jnp.float32
    scratch = []
    for front_dims, rows in (((4, 2), 192), ((2,), 192), ((2, 2), 192), ((2,), 48), ((2, 2), 48), ((3,), 48)):
        for columns, _ in PARTS:
            scratch.append(pltpu.VMEM(front_dims + (rows, columns), bf))
    plain = ((ROWS, 768), bf)
    for shape, kind in (
        plain, plain, plain, plain, ((16, 768), f32), ((3, ROWS, 128), f32), ((768, 3072), bf), ((3072, 768), bf),
        ((768, 3072), bf), ((3072, 768), bf), ((ROWS, 768), f32), ((ROWS, 768), f32), ((8, 3072), f32), ((8, 3072), f32),
        ((4, 4, ROWS, WIDE), bf), ((4, 4, ROWS, WIDE), bf), ((2, 2, ROWS, WIDE), bf), ((2, 4, ROWS, WIDE), bf),
        ((4, ROWS, WIDE), bf), ((4, ROWS, WIDE), bf), plain, ((3, ROWS, 768), bf), ((4, 16, 768), f32), ((4, 3, 16, 768), f32),
    ):
        scratch.append(pltpu.VMEM(shape, kind))
    scratch += [dma((170,)), dma((170,)), dma((16,))]
    rows = jax.ShapeDtypeStruct((ROWS, 768), bf)
    return pl.pallas_call(
        back_kernel,
        out_shape=(rows, rows, jax.ShapeDtypeStruct((192, 3072), bf), jax.ShapeDtypeStruct((192, 3072), bf),
                   jax.ShapeDtypeStruct((768, 768), bf), jax.ShapeDtypeStruct((16, 768), f32)),
        in_specs=[hbm] * 11, out_specs=(vmem,) * 6,
        scratch_shapes=scratch,
        compiler_params=pltpu.CompilerParams(collective_id=collective_id, has_side_effects=True, vmem_limit_bytes=62 * 2**20),
        name="back",
    )(odq, dkv, tokens, grad, normed_one, normed_two, vectors, tables, matrices, up, down)


D = 768
HEADS = 12
HD = 64
ROT = 16
TOK_DEV = 256


def rotary_tables(positions):
    lanes = jnp.arange(128) % HD
    exponents = (lanes % 8).astype(jnp.float32) * 2.0 / ROT
    inverse = 10000.0 ** (-exponents)
    angles = positions.astype(jnp.float32)[:, None] * inverse[None, :]
    cosine, sine = jnp.cos(angles), jnp.sin(angles)
    keep = jnp.where(lanes < ROT, cosine, 1.0)
    ahead = jnp.where(lanes < 8, -sine, 0.0)
    behind = jnp.where((lanes >= 8) & (lanes < ROT), sine, 0.0)
    return jnp.stack([keep, ahead, behind])


def on_device(
    tokens, cotangent, pairing, first_gain, first_shift, qkv_weight, qkv_bias, dense_weight,
    second_gain, second_shift, up_weight, up_bias, down_weight, out_bias,
):
    bf, f32 = jnp.bfloat16, jnp.float32
    total_blocks = 64
    offsets = jnp.arange(BLK, dtype=jnp.int32)
    ctx_index = lax.axis_index("ctx")
    core = lax.rem(lax.axis_index("wsh"), 2)
    seq_of_layout = jnp.stack([pairing, total_blocks - 1 - pairing], 1).reshape(-1)
    layout_of_seq = (
        jnp.zeros((total_blocks,), jnp.int32)
        .at[seq_of_layout]
        .set(jnp.arange(total_blocks, dtype=jnp.int32))
    )
    own_blocks = lax.dynamic_slice(seq_of_layout, (2 * ctx_index,), (2,))
    row_blocks = lax.dynamic_slice(seq_of_layout, (16 * (ctx_index // 8) + 8 * core,), (8,))
    local_pos = (own_blocks[:, None] * BLK + offsets[None, :]).reshape(-1)
    tables = rotary_tables(local_pos)
    query_scale = HD ** (-0.5)

    shard = lax.broadcasted_iota(jnp.int32, (4, 1), 0) == lax.axis_index("wsh")
    small = (first_gain, first_shift, second_gain, second_shift, out_bias, qkv_bias, up_bias)
    spots = [jnp.where(shard, v[None, :], 0.0).astype(bf).reshape(-1) for v in small]
    vectors = jnp.concatenate(spots + [jnp.zeros((4 * D,), bf)]).reshape(16, D)
    grad_rows = cotangent[0]
    keys_values, queries_grads, normed_one, normed_two, vectors, matrices = front(
        tokens[0], grad_rows, tables, qkv_weight, dense_weight, vectors
    )
    up_shard, down_shard, keys_values = lax.optimization_barrier((up_weight, down_weight, keys_values))
    up_matrix = lax.all_gather(up_shard, "wsh", axis=0, tiled=True)
    down_matrix = lax.all_gather(down_shard, "wsh", axis=0, tiled=True)
    attended_dq, grad_kv = attention(row_blocks, layout_of_seq, queries_grads.reshape(1024, WIDE), keys_values.reshape(8192, WIDE))
    layer_output, input_grad, wide, upper, lower, sums = back(
        attended_dq.reshape(4, ROWS, WIDE), grad_kv.reshape(32, ROWS, WIDE), tokens[0], grad_rows, normed_one, normed_two,
        vectors, tables, matrices, up_matrix, down_matrix,
    )
    mine = lax.axis_index("wsh")
    gains = lax.dynamic_slice(sums, (0, 192 * mine), (5, 192))
    qkv_offset_grad = lax.dynamic_slice(sums[5:8].reshape(-1), (576 * mine,), (576,))
    up_offset_grad = lax.dynamic_slice(sums, (8 + mine, 0), (1, D))[0]
    return (
        layer_output[None], input_grad[None], gains[0], gains[1], wide[:, :2304].astype(f32), qkv_offset_grad,
        wide[:, 2304:].astype(f32), gains[2], gains[3], upper.astype(f32), up_offset_grad, lower.astype(f32), gains[4],
    )


def solution(mesh):
    rows, split, flat = P("wsh", "ctx", None), P("wsh", None), P("wsh")
    return jax.shard_map(
        on_device,
        mesh=mesh,
        in_specs=(rows, rows, P(), flat, flat, split, flat, split, flat, flat, split, flat, split, flat),
        out_specs=(rows, rows, flat, flat, split, flat, split, flat, flat, split, flat, split, flat),
        check_vma=False,
    )
```

```python
import functools

import jax
import jax.numpy as jnp
from jax import lax
from jax.experimental import pallas as pl
from jax.experimental.pallas import tpu as pltpu
from jax.sharding import PartitionSpec as P

G = 3; BLK = 128; LOG2E = 1.4426950408889634
NEG = -1e30

def attn_kernel(chunk, qpos, lay, qdo, kv_hbm, odq, dkv_hbm, kv, kvt, acc, probs, grads, tops, stage, sem, osem):
    blocks = chunk // BLK
    nblk = kv.shape[0] // BLK
    f32, bf = jnp.float32, jnp.bfloat16

    def load(i, _):
        pltpu.make_async_copy(kv_hbm.at[pl.ds(pl.multiple_of(lay[i] * BLK, BLK), BLK)], kv.at[pl.ds(pl.multiple_of(i * BLK, BLK), BLK)], sem.at[i]).start()
        return 0
    lax.fori_loop(0, nblk, load, 0)

    def land(i, _):
        rows = pl.ds(pl.multiple_of(i * chunk, chunk), chunk)
        for j in range(blocks):
            at = pl.ds(pl.multiple_of(i * chunk + j * BLK, BLK), BLK)
            pltpu.make_async_copy(kv_hbm.at[pl.ds(0, BLK)], kv.at[at], sem.at[i * blocks + j]).wait()
        acc[rows] = jnp.zeros((chunk, G * 128), f32)
        kvt[:, rows] = kv[rows].T
        return 0
    lax.fori_loop(0, nblk // blocks, land, 0)

    upper = lax.broadcasted_iota(jnp.int32, (128, 128), 0) < 64
    left = lax.broadcasted_iota(jnp.int32, (128, 128), 1) < 64

    def q_block(i, _):
        b = qpos[i]
        qrows = pl.ds(pl.multiple_of(i * BLK, BLK), BLK)
        last = b // blocks
        pairs = [qdo[qrows, h * 128:(h + 1) * 128] for h in range(G)]
        turned = [p.astype(f32).T for p in pairs]
        wide = [jnp.concatenate([jnp.where(upper, turned[h], 0.0).astype(bf), jnp.where(upper, 0.0, turned[h]).astype(bf)], 1) for h in range(G)]
        rest = b - last * blocks

        def pick(step, state):
            sizes = [chunk * (i + 1) // 4 for i in range(4)]
            return lax.switch(rest // (blocks // 4), [functools.partial(step, size) for size in sizes], state)

        def fwd(c, state, masked, size=chunk):
            at = pl.ds(pl.multiple_of(c * chunk, chunk), size)
            out = []
            every = [jnp.dot(kv[at, h * 128:(h + 1) * 128], wide[h], preferred_element_type=f32) for h in range(G)]
            kept = []
            for h in range(G):
                m, l, o = state[h]
                s = every[h][:, :128]
                grads[at, h * 128:(h + 1) * 128] = every[h][:, 128:]
                if masked:
                    key_i = lax.broadcasted_iota(jnp.int32, (size, BLK), 0)
                    row_i = lax.broadcasted_iota(jnp.int32, (size, BLK), 1) + rest * BLK
                    s = jnp.where(key_i <= row_i, s, NEG)
                new = jnp.maximum(m, jnp.max(s, 0, keepdims=True))
                p = jnp.exp(s - new)
                a = jnp.exp(m - new)
                l = l * a + jnp.sum(p, 0, keepdims=True)
                p = p.astype(bf)
                probs[at, h * 128:(h + 1) * 128] = p
                tops[c, h] = jnp.broadcast_to(new, (8, BLK))
                kept.append((new, l, o * a, p))
            for h in range(G):
                new, l, o, p = kept[h]
                o = o + jnp.dot(kvt[h * 128 + 64:(h + 1) * 128, at], p, preferred_element_type=f32)
                out.append((new, l, o))
            return tuple(out)

        state = tuple((jnp.full((1, BLK), NEG, f32), jnp.zeros((1, BLK), f32), jnp.zeros((64, BLK), f32)) for _ in range(G))
        state = lax.fori_loop(0, last, lambda c, s: fwd(c, s, False), state)
        state = pick(lambda size, s: fwd(last, s, True, size), state)
        lse, delta, outs = [], [], []
        for h in range(G):
            m, l, o = state[h]
            o = o / l
            outs.append(o)
            lse.append(m + jnp.log(l))
            delta.append(jnp.sum(o * turned[h][64:], 0, keepdims=True))
        narrow = [jnp.concatenate([jnp.where(left, pairs[h], jnp.zeros_like(pairs[h])), jnp.where(left, jnp.zeros_like(pairs[h]), pairs[h])], 0) for h in range(G)]

        def bwd(c, state, size=chunk):
            at = pl.ds(pl.multiple_of(c * chunk, chunk), size)
            out, work = [], []
            for h in range(G):
                cols = slice(h * 128, (h + 1) * 128)
                p = probs[at, cols].astype(f32) * jnp.exp(tops[c, h, 0:1] - lse[h])
                ds = (p * (grads[at, cols] - delta[h])).astype(bf)
                work.append((jnp.concatenate([ds, p.astype(bf)], 1), ds))
            for h in range(G):
                pair, ds = work[h]
                acc[at, h * 128:(h + 1) * 128] += jnp.dot(pair, narrow[h], preferred_element_type=f32)
                out.append(state[h] + jnp.dot(kvt[h * 128:h * 128 + 64, at], ds, preferred_element_type=f32))
            return tuple(out)

        dq = tuple(jnp.zeros((64, BLK), f32) for _ in range(G))
        dq = lax.fori_loop(0, last, bwd, dq)
        dq = pick(lambda size, s: bwd(last, s, size), dq)
        for h in range(G):
            odq[qrows, h * 128:(h + 1) * 128] = jnp.concatenate([outs[h], dq[h]], 0).T.astype(bf)
        return 0
    lax.fori_loop(0, qpos.shape[0], q_block, 0)

    def leave(slot, j):
        return pltpu.make_async_copy(stage.at[slot, j], dkv_hbm.at[pl.ds(0, BLK)], osem.at[slot, j])

    def send(i, _):
        slot = lax.rem(i, 2)
        @pl.when(i >= 2)
        def _():
            for j in range(4):
                leave(slot, j).wait()
        for j in range(4):
            at = i * 4 + j
            stage[slot, j] = acc[pl.ds(pl.multiple_of(at * BLK, BLK), BLK)].astype(bf)
            pltpu.make_async_copy(stage.at[slot, j], dkv_hbm.at[pl.ds(pl.multiple_of(lay[at] * BLK, BLK), BLK)], osem.at[slot, j]).start()
        return 0
    lax.fori_loop(0, nblk // 4, send, 0)
    for slot in range(2):
        for j in range(4):
            leave(slot, j).wait()


def attention(qpos, lay, qdo, kv, chunk=1024):
    n = kv.shape[0]
    smem = pl.BlockSpec(memory_space=pltpu.SMEM)
    vmem = pl.BlockSpec(memory_space=pltpu.VMEM)
    hbm = pl.BlockSpec(memory_space=pl.ANY)
    return pl.pallas_call(
        functools.partial(attn_kernel, chunk),
        out_shape=(jax.ShapeDtypeStruct(qdo.shape, jnp.bfloat16), jax.ShapeDtypeStruct(kv.shape, jnp.bfloat16)),
        in_specs=[smem, smem, vmem, hbm], out_specs=(vmem, hbm),
        scratch_shapes=[pltpu.VMEM((n, G * 128), jnp.bfloat16), pltpu.VMEM((G * 128, n), jnp.bfloat16),
            pltpu.VMEM((n, G * 128), jnp.float32), pltpu.VMEM((n, G * 128), jnp.bfloat16), pltpu.VMEM((n, G * 128), jnp.float32), pltpu.VMEM((n // chunk, G, 8, BLK), jnp.float32),
            pltpu.VMEM((2, 4, BLK, G * 128), jnp.bfloat16),
            pltpu.SemaphoreType.DMA((n // BLK,)), pltpu.SemaphoreType.DMA((2, 4))],
        compiler_params=pltpu.CompilerParams(vmem_limit_bytes=62 * 2**20),
        name="attention",
    )(qpos, lay, qdo, kv)


MESH = pl.DeviceIdType.MESH
ROWS, WIDE = 256, 384


def place():
    c, w = lax.axis_index("ctx"), lax.axis_index("wsh")
    return c // 8, lax.rem(c // 4, 2), lax.rem(c, 4), w // 2, lax.rem(w, 2)


def device(z, yl, x, yh, core):
    return (z * 8 + yl * 4 + x, yh * 2 + core)


def greet(devices, extra=None, extra_count=0):
    barrier = pltpu.get_barrier_semaphore()
    for d in devices:
        pl.semaphore_signal(barrier, inc=1, device_id=d, device_id_type=MESH)
    if extra is not None:
        @pl.when(extra_count == 1)
        def _():
            pl.semaphore_signal(barrier, inc=1, device_id=extra, device_id_type=MESH)
    pl.semaphore_wait(barrier, len(devices) + extra_count)


def landed(ref, sem):
    pltpu.make_async_copy(ref, ref, sem).wait()


def front_kernel(tokens_hbm, grad_hbm, tables_hbm, qkv, dense, vectors_hbm, kv_all, qdo, one_hbm, two_hbm, vectors_out, weights_out,
                 tokens, grad, tables, vectors, normed_one, normed_two, all_vectors, bring_sem, weights, vec_in, kvs, qds, local_sem, send_sem, recv_sem, kv_send, kv_recv, q_send, q_recv):
    z, yl, x, yh, core = place()
    bring = [pltpu.make_async_copy(src, dst, bring_sem.at[i]) for i, (src, dst) in enumerate(((vectors_hbm, vectors), (tokens_hbm, tokens), (tables_hbm, tables), (grad_hbm, grad)))]
    for copy in bring:
        copy.start()
    f32, bf = jnp.float32, jnp.bfloat16
    me = yh * 2 + core
    far = (1 - yh) * 2 + core
    other = (1 - yh) * 2 + 1 - core
    swap = yl != core
    partner = [device(z, core, lax.rem(x + d, 4), yh, yl) for d in range(4)]
    sib = device(z, yl, x, yh, 1 - core)
    cross = device(z, 1 - yl, x, 1 - yh, core)
    others = [device(z, yl, x, 1 - yh, core), device(z, yl, x, 1 - yh, 1 - core)]
    xs = [device(z, yl, lax.rem(x + d, 4), yh, core) for d in (1, 3)]
    zs = [device(lax.rem(z + d, 4), yl, x, yh, core) for d in (1, 3)]
    greet([sib, cross] + others + xs + zs + partner[1:], partner[0], lax.rem(yl + core, 2))
    count = [0]
    sent = []

    def remote(src, dst, to):
        sem = count[0]
        count[0] += 1
        copy = pltpu.make_async_remote_copy(src_ref=src, dst_ref=dst, send_sem=send_sem.at[sem], recv_sem=recv_sem.at[sem], device_id=to, device_id_type=MESH)
        copy.start()
        sent.append(copy)
        return sem

    def arrive(ref, sem):
        landed(ref, recv_sem.at[sem])

    def rows(i, start, size):
        return weights.at[i, pl.ds(pl.multiple_of(start, 16), size)]

    shards = [qkv.at[:, pl.ds(768, 768)], qkv.at[:, pl.ds(1536, 768)], qkv.at[:, pl.ds(0, 768)], dense]
    quarter = [x, z, x, z]
    ring = [xs, zs, xs, zs]
    bring[0].wait()
    vec_sem = [remote(vectors, vec_in.at[i], to) for i, to in enumerate([sib] + others)]
    cross_sem = [remote(shards[i].at[pl.ds(pl.multiple_of(quarter[i] * 48, 16), 48)], rows(i, me * 192 + quarter[i] * 48, 48), cross) for i in range(4)]
    own, late = [], [[], [], [], []]
    for i in range(4):
        copy = pltpu.make_async_copy(shards[i], rows(i, me * 192, 192), local_sem.at[i])
        copy.start()
        own.append(copy)
        late[i].append((rows(i, (yh * 2 + 1 - core) * 192, 192), remote(shards[i], rows(i, me * 192, 192), sib)))

    for copy in bring[1:]:
        copy.wait()
    values = tokens[...].astype(f32)
    centered = values - jnp.mean(values, -1, keepdims=True)
    unit = centered * lax.rsqrt(jnp.mean(centered * centered, -1, keepdims=True) + 1e-05)
    for i in range(3):
        arrive(vec_in.at[i], vec_sem[i])
    vec = vectors[...].astype(f32) + vec_in[0].astype(f32) + vec_in[1].astype(f32) + vec_in[2].astype(f32)
    all_vectors[...] = vec
    normed_one[...] = (unit * vec[0:1] + vec[1:2]).astype(bf)
    normed_two[...] = (unit * vec[2:3] + vec[3:4]).astype(bf)

    leave = [pltpu.make_async_copy(src, dst, bring_sem.at[4 + i]) for i, (src, dst) in enumerate(((all_vectors, vectors_out), (normed_one, one_hbm), (normed_two, two_hbm)))]
    for copy in leave:
        copy.start()
    cuts = ((0, 32), (32, 16))
    ring_sem, half_sem = {}, {}

    def start_ring(i):
        mine = rows(i, far * 192 + quarter[i] * 48, 48)
        arrive(mine, cross_sem[i])
        for way in (0, 1):
            ring_sem[i, way] = remote(mine, mine, ring[i][way])
        late[i].append((rows(i, other * 192 + quarter[i] * 48, 48), remote(mine, mine, sib)))

    def relay(i):
        for way in (0, 1):
            b = lax.rem(quarter[i] + 3 - 2 * way, 4)
            got = rows(i, far * 192 + b * 48, 48)
            arrive(got, ring_sem[i, way])
            part = rows(i, far * 192 + b * 48 + cuts[way][0], cuts[way][1])
            half_sem[i, way] = remote(part, part, ring[i][way])
            late[i].append((rows(i, other * 192 + b * 48, 48), remote(got, got, sib)))

    def finish(i):
        for way in (0, 1):
            start = lax.rem(quarter[i] + 2, 4) * 48 + cuts[way][0]
            got = rows(i, far * 192 + start, cuts[way][1])
            arrive(got, half_sem[i, way])
            late[i].append((rows(i, other * 192 + start, cuts[way][1]), remote(got, got, sib)))

    def complete(i):
        for ref, sem in late[i]:
            arrive(ref, sem)
        own[i].wait()

    left = lax.broadcasted_iota(jnp.int32, (ROWS, 128), 1) < 64
    keep, ahead, behind = tables[0], tables[1], tables[2]

    def turn(tile):
        return tile * keep + pltpu.roll(tile, 120, 1) * ahead + pltpu.roll(tile, 8, 1) * behind

    def pack(into, first, second):
        for t in range(6):
            lanes = slice(128 * t, 128 * t + 128)
            a, b = first(lanes), second(lanes)
            for head, tile in ((2 * t, jnp.where(left, a, pltpu.roll(b, 64, 1))), (2 * t + 1, jnp.where(left, pltpu.roll(a, 64, 1), b))):
                into[head // 3, :, 128 * (head % 3):128 * (head % 3) + 128] = tile.astype(bf)

    def dot(a, b):
        return jnp.dot(a, b, preferred_element_type=f32)

    def exchange(src, dst_of, send, recv):
        out = []
        for d in (0, 2, 1, 3):
            args = (src.at[lax.rem(x + d, 4)], dst_of, send.at[d], recv.at[d], partner[d])
            copy = pltpu.make_async_remote_copy(src_ref=args[0], dst_ref=args[1], send_sem=args[2], recv_sem=args[3], device_id=args[4], device_id_type=MESH)
            if d == 0:
                @pl.when(swap)
                def _():
                    copy.start()
                @pl.when(jnp.logical_not(swap))
                def _():
                    pltpu.make_async_copy(args[0], args[1], args[3]).start()
            else:
                copy.start()
            out.append((d, copy))
        return out

    for i in range(4):
        start_ring(i)
    for i in (0, 1):
        relay(i)
    for i in (0, 1):
        finish(i)
    for i in (0, 1):
        complete(i)
    one = normed_one[...]
    pack(kvs,
         lambda lanes: turn(dot(one, weights[0, :, lanes]) + vec[6:7, lanes]),
         lambda lanes: dot(one, weights[1, :, lanes]) + vec[7:8, lanes])
    mine = z * 8 + yl * 4 + x
    sent_kv = exchange(kvs, kv_all.at[mine], kv_send, kv_recv)
    def slot(zz, cc, d):
        return kv_all.at[lax.rem(zz, 4) * 8 + cc * 4 + lax.rem(x + 4 - d, 4)]

    half = ROWS // 2
    up_sem, part_sem, sib_sem = {}, {}, {}
    for d in (0, 1, 3, 2):
        here = slot(z, core, d)
        landed(here, kv_recv.at[d])
        for way in (0, 1):
            up_sem[way, d] = remote(here, here, zs[way])
        sib_sem[0, d] = remote(here, here, sib)
    for i in (2, 3):
        relay(i)
    for i in (2, 3):
        finish(i)
    for i in (2, 3):
        complete(i)
    g = grad[...]
    pack(qds,
         lambda lanes: turn(dot(one, weights[2, :, lanes]) + vec[5:6, lanes]) * 0.125,
         lambda lanes: lax.dot_general(g, weights[3, lanes, :], (((1,), (1,)), ((), ())), preferred_element_type=f32))
    sent_q = exchange(qds, qdo.at[x], q_send, q_recv)
    keep_out = pltpu.make_async_copy(weights, weights_out, local_sem.at[4])
    keep_out.start()

    for d in (0, 1, 3, 2):
        for way in (0, 1):
            here = slot(z + 3 - 2 * way, core, d)
            arrive(here, up_sem[way, d])
            part = here.at[pl.ds(way * half, half)]
            part_sem[way, d] = remote(part, part, zs[way])
            sib_sem[1 + way, d] = remote(here, here, sib)
    for d in (0, 1, 3, 2):
        for way in (0, 1):
            part = slot(z + 2, core, d).at[pl.ds(way * half, half)]
            arrive(part, part_sem[way, d])
            sib_sem[3 + way, d] = remote(part, part, sib)
    for d in range(4):
        arrive(slot(z, 1 - core, d), sib_sem[0, d])
        for way in (0, 1):
            arrive(slot(z + 3 - 2 * way, 1 - core, d), sib_sem[1 + way, d])
            arrive(slot(z + 2, 1 - core, d).at[pl.ds(way * half, half)], sib_sem[3 + way, d])
        landed(qdo.at[lax.rem(x + 4 - d, 4)], q_recv.at[d])
    keep_out.wait()
    for copy in leave:
        copy.wait()
    for copy in sent:
        copy.wait_send()
    for d, copy in sent_kv + sent_q:
        if d == 0:
            @pl.when(swap)
            def _():
                copy.wait_send()
        else:
            copy.wait_send()


def front(tokens, grad, tables, qkv, dense, vectors, collective_id=0):
    hbm = pl.BlockSpec(memory_space=pl.ANY)
    dma = pltpu.SemaphoreType.DMA
    bf, f32 = jnp.bfloat16, jnp.float32
    rows = jax.ShapeDtypeStruct((ROWS, 768), bf)
    return pl.pallas_call(
        front_kernel,
        out_shape=(jax.ShapeDtypeStruct((32, ROWS, WIDE), bf), jax.ShapeDtypeStruct((4, ROWS, WIDE), bf), rows, rows,
                   jax.ShapeDtypeStruct((16, 768), f32), jax.ShapeDtypeStruct((4, 768, 768), bf)),
        in_specs=[hbm] * 6, out_specs=(hbm,) * 6,
        scratch_shapes=[pltpu.VMEM((ROWS, 768), bf), pltpu.VMEM((ROWS, 768), bf), pltpu.VMEM((3, ROWS, 128), f32), pltpu.VMEM((16, 768), bf),
                        pltpu.VMEM((ROWS, 768), bf), pltpu.VMEM((ROWS, 768), bf), pltpu.VMEM((16, 768), f32), dma((7,)), pltpu.VMEM((4, 768, 768), bf), pltpu.VMEM((3, 16, 768), bf), pltpu.VMEM((4, ROWS, WIDE), bf), pltpu.VMEM((4, ROWS, WIDE), bf),
                        dma((5,)), dma((100,)), dma((100,)), dma((4,)), dma((4,)), dma((4,)), dma((4,))],
        compiler_params=pltpu.CompilerParams(collective_id=collective_id, has_side_effects=True, vmem_limit_bytes=62 * 2**20),
        name="front",
    )(tokens, grad, tables, qkv, dense, vectors)


PARTS = ((384, False), (384, True), (768, True), (384, False), (384, False))
TILE = 384


def erf(values):
    v = jnp.clip(values, -4.0, 4.0)
    s = v * v
    top = jnp.float32(-2.72614225801306e-10)
    for coefficient in (2.77068142495902e-08, -2.10102402082508e-06, -5.69250639462346e-05, -7.34990630326855e-04, -2.95459980854025e-03, -1.60960333262415e-02):
        top = top * s + coefficient
    low = jnp.float32(-1.45660718464996e-05)
    for coefficient in (-2.13374055278905e-04, -1.68282697438203e-03, -7.37332916720468e-03, -1.42647390514189e-02):
        low = low * s + coefficient
    return v * top / low


def back_kernel(odq, dkv, tokens_hbm, grad_hbm, one_hbm, two_hbm, vectors_hbm, tables_hbm, matrices, up_hbm, down_hbm,
                layer_output, input_grad, wide_out, upper_out, lower_out, vector_out, *refs):
    sib_in, far_in, near_in, far_two, near_two, y_in = (refs[5 * i : 5 * i + 5] for i in range(6))
    (tokens, grad, normed_one, normed_two, vectors, tables, up, down_w, upper, lower, mlp, back_two, up_bias, bias_grad,
     held, held_in, held_far, held_near, odq_own, dkv_own, attended, mixed, tiny, tiny_in, send_sem, recv_sem, local_sem) = refs[30:]
    z, yl, x, yh, core = place()
    f32, bf = jnp.float32, jnp.bfloat16
    swapped_place = yl != core
    partner = [device(z, core, lax.rem(x + d, 4), yh, yl) for d in range(4)]
    xs = [device(z, yl, lax.rem(x + d, 4), yh, core) for d in (1, 3, 2)]
    zs = [device(lax.rem(z + d, 4), yl, x, yh, core) for d in (1, 3, 2)]
    ys = [device(z, 1 - yl, x, yh, core), device(z, yl, x, 1 - yh, core), device(z, 1 - yl, x, 1 - yh, core)]
    sib = device(z, yl, x, yh, 1 - core)
    greet([sib] + xs + zs + ys + partner[1:], partner[0], lax.rem(yl + core, 2))
    count = [0]
    local_count = [0]
    sent, maybe = [], []
    pairs = []

    def bring(src, dst):
        copy = pltpu.make_async_copy(src, dst, local_sem.at[local_count[0]])
        local_count[0] += 1
        copy.start()
        return copy

    def number():
        count[0] += 1
        return count[0] - 1

    def describe(src, dst, sem, to):
        return pltpu.make_async_remote_copy(src_ref=src, dst_ref=dst, send_sem=send_sem.at[sem], recv_sem=recv_sem.at[sem], device_id=to, device_id_type=MESH)

    def remote(src, dst, to):
        sem = number()
        copy = describe(src, dst, sem, to)
        copy.start()
        sent.append(copy)
        return sem

    def both(sources, dst, to):
        sem = number()
        for s in (0, 1):
            describe(sources[s], dst.at[s], sem, to).start()
        pairs.append((dst, sem))
        return sem

    def arrive(ref, sem):
        landed(ref, recv_sem.at[sem])

    def exchange(src, dst, d):
        sem = number()
        part = src.at[lax.rem(x + d, 4)]
        copy = describe(part, dst, sem, partner[d])
        if d == 0:
            @pl.when(swapped_place)
            def _():
                copy.start()
            @pl.when(jnp.logical_not(swapped_place))
            def _():
                pltpu.make_async_copy(part, dst, recv_sem.at[sem]).start()
            maybe.append(copy)
        else:
            copy.start()
            sent.append(copy)
        return sem

    def dot(left, right, left_dim, right_dim):
        return lax.dot_general(left, right, (((left_dim,), (right_dim,)), ((), ())), preferred_element_type=f32)

    def group(zz, cc):
        return dkv.at[pl.ds(lax.rem(zz, 4) * 8 + cc * 4, 4)]

    held_sem, held_load = [], []
    for k, zz in enumerate((z + 2, z + 1, z + 3, z)):
        held_sem.append(remote(group(zz, 1 - core), held_in.at[k], sib))
        held_load.append(bring(group(zz, core), held.at[k]))
    inputs = [bring(src, dst) for src, dst in ((two_hbm, normed_two), (grad_hbm, grad), (vectors_hbm, vectors), (up_hbm, up), (down_hbm, down_w),
                                               (tokens_hbm, tokens), (one_hbm, normed_one), (tables_hbm, tables))]
    odq_sem = [exchange(odq, odq_own.at[x], d) for d in range(4)]
    def feed(t, _):
        at = pl.ds(pl.multiple_of(t * TILE, TILE), TILE)
        values = dot(normed_two[...], up[:, at], 1, 0) + up_bias[0:1, at]
        inner = 0.5 + 0.5 * erf(values * 0.7071067811865476)
        slope = inner + values * (0.3989422804014327 * jnp.exp(-0.5 * values * values))
        active = (values * inner).astype(bf)
        grads = (dot(grad[...], down_w[at], 1, 1) * slope).astype(bf)
        mlp[...] += dot(active, down_w[at], 1, 0)
        back_two[...] += dot(grads, up[:, at], 1, 1)
        bias_grad[0:1, at] = jnp.sum(grads.astype(f32), 0, keepdims=True)
        upper[:, at] = dot(normed_two[...], grads, 0, 0).astype(bf)
        lower[at] = dot(active, grad[...], 0, 0).astype(bf)
        return 0

    def sum_held(k, chunks, terms):
        def step(i, _):
            j, r = chunks[0] + i // 2, pl.ds(pl.multiple_of(lax.rem(i, 2) * 128, 128), 128)
            value = held[k, j, r].astype(f32) + held_in[k, j, r].astype(f32)
            for ref, low in terms:
                value = value + ref[j - low, r].astype(f32)
            held[k, j, r] = value.astype(bf)
            return 0
        lax.fori_loop(0, 2 * (chunks[1] - chunks[0]), step, 0)

    held_load[0].wait()
    arrive(held_in.at[0], held_sem[0])
    sum_held(0, (0, 4), [])
    held_far_sem = [remote(held.at[0, pl.ds(2 * way, 2)], held_far.at[way], zs[way]) for way in (0, 1)]
    mlp[...] = jnp.zeros_like(mlp)
    back_two[...] = jnp.zeros_like(back_two)
    for copy in inputs:
        copy.wait()
    for i in range(4):
        up_bias[0:1, 768 * i:768 * i + 768] = vectors[8 + i:9 + i]
    lax.fori_loop(0, 3, feed, 0)
    held_near_sem = []
    for way in (0, 1):
        k = 1 + way
        held_load[k].wait()
        arrive(held_in.at[k], held_sem[k])
        sum_held(k, (2 - 2 * way, 4 - 2 * way), [])
        arrive(held_far.at[way], held_far_sem[way])
        sum_held(k, (2 * way, 2 * way + 2), [(held_far.at[way], 2 * way)])
        held_near_sem.append(remote(held.at[k], held_near.at[way], zs[way]))
    lax.fori_loop(3, 8, feed, 0)
    fetch = [bring(matrices.at[i], up.at[:, pl.ds(768 * i, 768)]) for i in range(4)]

    def piece(p, w, a):
        if p < 2:
            return down_w.at[pl.ds(pl.multiple_of(a * 768 + w * 192, 192), 192), pl.ds(384 * p, 384)]
        if p == 2:
            return upper.at[pl.ds(pl.multiple_of(w * 192, 192), 192), pl.ds(pl.multiple_of(a * 768, 768), 768)]
        return lower.at[pl.ds(pl.multiple_of(w * 768 + a * 192, 192), 192), pl.ds(384 * (p - 3), 384)]

    def own(p, k, s):
        return piece(p, 2 * s + core, lax.rem(first[p] + (2, 1, 3, 0)[k], 4))

    def result(p, a, start, size):
        if p < 2:
            return wide_out.at[pl.ds(start, size), pl.ds(pl.multiple_of(a * 768 + 384 * p, 384), 384)]
        if p == 2:
            return upper_out.at[pl.ds(start, size), pl.ds(pl.multiple_of(a * 768, 768), 768)]
        return lower_out.at[pl.ds(pl.multiple_of(a * 192 + start, 16), size), pl.ds(384 * (p - 3), 384)]

    first = [x if part[1] else z for part in PARTS]
    second = [z if part[1] else x for part in PARTS]
    ring_one = [xs if part[1] else zs for part in PARTS]
    ring_two = [zs if part[1] else xs for part in PARTS]
    sems = {}

    def swap(p):
        for k, ahead in enumerate((2, 1, 3, 0)):
            a = lax.rem(first[p] + ahead, 4)
            sems["sib", p, k] = both([piece(p, 2 * s + 1 - core, a) for s in (0, 1)], sib_in[p].at[k], sib)

    def swapped(p, k):
        arrive(sib_in[p].at[k], sems["sib", p, k])

    def add(rows, into, terms):
        def body(i, _):
            at = pl.ds(pl.multiple_of(i * 48, 48), 48)
            total = into[at].astype(f32)
            for term in terms:
                total = total + term[at].astype(f32)
            into[at] = total.astype(bf)
            return 0
        lax.fori_loop(0, rows // 48, body, 0)

    def quarter(b):
        return pl.ds(pl.multiple_of(lax.rem(b, 4) * 48, 48), 48)

    def far(p):
        swapped(p, 0)
        for s in (0, 1):
            add(192, own(p, 0, s), [sib_in[p].at[0, s]])
            sems["far", p, s] = remote(own(p, 0, s), far_in[p].at[s], ring_one[p][s])

    def near(p):
        for way in (0, 1):
            k = 1 + way
            swapped(p, k)
            add(192, own(p, k, 1 - way), [sib_in[p].at[k, 1 - way]])
            arrive(far_in[p].at[way], sems["far", p, way])
            add(192, own(p, k, way), [sib_in[p].at[k, way], far_in[p].at[way]])
            sems["near", p, way] = both([own(p, k, s) for s in (0, 1)], near_in[p].at[way], ring_one[p][way])

    def mine(p):
        swapped(p, 3)
        for way in (0, 1):
            arrive(near_in[p].at[way], sems["near", p, way])
        for s in (0, 1):
            add(192, own(p, 3, s), [sib_in[p].at[3, s], near_in[p].at[0, s], near_in[p].at[1, s]])
        for s in (0, 1):
            sems["far2", p, s] = remote(own(p, 3, s).at[quarter(second[p] + 2)], far_two[p].at[s], ring_two[p][s])

    def near2(p):
        for way in (0, 1):
            at = quarter(second[p] + 1 + 2 * way)
            arrive(far_two[p].at[way], sems["far2", p, way])
            add(48, own(p, 3, way).at[at], [far_two[p].at[way]])
            sems["near2", p, way] = both([own(p, 3, s).at[at] for s in (0, 1)], near_two[p].at[way], ring_two[p][way])

    def mine2(p):
        at = quarter(second[p])
        for way in (0, 1):
            arrive(near_two[p].at[way], sems["near2", p, way])
        for s in (0, 1):
            add(48, own(p, 3, s).at[at], [near_two[p].at[0, s], near_two[p].at[1, s]])
        for i, half in enumerate((yh, 1 - yh, 1 - yh)):
            sems["y", p, i] = remote(own(p, 3, half).at[at], y_in[p].at[i], ys[i])

    def total(p):
        for i in range(3):
            arrive(y_in[p].at[i], sems["y", p, i])
        value = own(p, 3, yh)[quarter(second[p])].astype(f32)
        for i in range(3):
            value = value + y_in[p][i].astype(f32)
        done = result(p, first[p], pl.multiple_of(second[p] * 48, 16), 48)
        done[...] = value.astype(bf)
        for way in (0, 1):
            sems["ring", p, way] = remote(done, done, ring_two[p][way])

    cuts = ((0, 32), (32, 16))

    def relay(p):
        for way in (0, 1):
            b = lax.rem(second[p] + 3 - 2 * way, 4)
            arrive(result(p, first[p], pl.multiple_of(b * 48, 16), 48), sems["ring", p, way])
            part = result(p, first[p], pl.multiple_of(b * 48 + cuts[way][0], 16), cuts[way][1])
            sems["relay", p, way] = remote(part, part, ring_two[p][way])

    def last(p):
        b = lax.rem(second[p] + 2, 4)
        for way in (0, 1):
            arrive(result(p, first[p], pl.multiple_of(b * 48 + cuts[way][0], 16), cuts[way][1]), sems["relay", p, way])
        block = result(p, first[p], 0, 192)
        for way in (0, 1):
            sems["last", p, way] = remote(block, block, ring_one[p][way])

    def end(p):
        for way in (0, 1):
            a = lax.rem(first[p] + 3 - 2 * way, 4)
            arrive(result(p, a, 0, 192), sems["last", p, way])
            part = result(p, a, 96 * way, 96)
            sems["end", p, way] = remote(part, part, ring_one[p][way])

    def close(p):
        for way in (0, 1):
            arrive(result(p, lax.rem(first[p] + 2, 4), 96 * way, 96), sems["end", p, way])

    def tiny_stage(step):
        groups = ([sib], xs, zs, ys)
        if step > 0:
            for i in range(len(groups[step - 1])):
                arrive(tiny_in.at[step - 1, i], sems["tiny", step - 1, i])
            value = tiny[step - 1]
            for i in range(len(groups[step - 1])):
                value = value + tiny_in[step - 1, i]
            if step == 4:
                vector_out[...] = value
                return
            tiny[step] = value
        for i, to in enumerate(groups[step]):
            sems["tiny", step, i] = remote(tiny.at[step], tiny_in.at[step, i], to)

    group_one, group_two = (2, 3, 4), (0, 1)
    for p in group_one:
        swap(p)
    for way in (0, 1):
        arrive(held_near.at[way], held_near_sem[way])
    held_load[3].wait()
    arrive(held_in.at[3], held_sem[3])
    sum_held(3, (0, 4), [(held_near.at[0], 0), (held_near.at[1], 0)])
    dkv_sem = [exchange(held.at[3], dkv_own.at[x], d) for d in range(4)]
    for p in group_one:
        far(p)
    for d in range(4):
        h = lax.rem(x + 4 - d, 4)
        arrive(odq_own.at[h], odq_sem[d])
        arrive(dkv_own.at[h], dkv_sem[d])

    left = lax.broadcasted_iota(jnp.int32, (ROWS, 128), 1) < 64
    keep, ahead, behind = tables[0], tables[1], tables[2]

    def turn_back(tile):
        return tile * keep + pltpu.roll(tile * ahead, 8, 1) + pltpu.roll(tile * behind, 120, 1)

    def unpack(slabs, t):
        even, odd = (slabs[h // 3, :, 128 * (h % 3):128 * (h % 3) + 128].astype(f32) for h in (2 * t, 2 * t + 1))
        return jnp.where(left, even, pltpu.roll(odd, 64, 1)), jnp.where(left, pltpu.roll(even, 64, 1), odd)

    for t in range(6):
        lanes = slice(128 * t, 128 * t + 128)
        out, query = unpack(odq_own, t)
        key, value = unpack(dkv_own, t)
        attended[:, lanes] = out.astype(bf)
        mixed[0, :, lanes] = (turn_back(query) * 0.125).astype(bf)
        mixed[1, :, lanes] = turn_back(key).astype(bf)
        mixed[2, :, lanes] = value.astype(bf)
    g = grad[...]
    one = normed_one[...]
    for i in range(3):
        down_w[768 * i:768 * i + 768] = dot(one, mixed[i], 0, 0).astype(bf)
    down_w[2304:] = dot(attended[...], g, 0, 0).astype(bf)
    for p in group_two:
        swap(p)
    for p in group_two:
        far(p)
    for p in group_one:
        near(p)
    for copy in fetch:
        copy.wait()
    values = tokens[...].astype(f32)
    centered = values - jnp.mean(values, -1, keepdims=True)
    scale = lax.rsqrt(jnp.mean(centered * centered, -1, keepdims=True) + 1e-05)
    unit = centered * scale
    back_one = dot(mixed[0], up[:, 1536:2304], 1, 1) + dot(mixed[1], up[:, 0:768], 1, 1) + dot(mixed[2], up[:, 768:1536], 1, 1)
    wide_grad = g.astype(f32)
    into = wide_grad
    sums = []
    for back, gain in ((back_one, vectors[0:1]), (back_two[...], vectors[2:3])):
        sums.append(jnp.sum(back * unit, 0, keepdims=True))
        sums.append(jnp.sum(back, 0, keepdims=True))
        scaled = back * gain
        into = into + scale * (scaled - jnp.mean(scaled, -1, keepdims=True) - unit * jnp.mean(scaled * unit, -1, keepdims=True))
    input_grad[...] = into.astype(bf)
    sums.append(jnp.sum(wide_grad, 0, keepdims=True))
    sums.extend(jnp.sum(mixed[i].astype(f32), 0, keepdims=True) for i in range(3))
    sums.extend(bias_grad[0:1, 768 * i:768 * i + 768] for i in range(4))
    tiny[0] = jnp.concatenate(sums + [jnp.zeros((4, 768), f32)], 0)
    tiny_stage(0)
    for p in group_two:
        near(p)
    for p in group_one:
        mine(p)
    layer_output[...] = (values + mlp[...] + dot(attended[...], up[:, 2304:3072], 1, 0) + vectors[4:5]).astype(bf)
    tiny_stage(1)
    for p in group_one:
        near2(p)
    tiny_stage(2)
    for p in group_two:
        mine(p)
    for p in group_one:
        mine2(p)
    tiny_stage(3)
    for p in group_one:
        total(p)
    for p in group_two:
        near2(p)
    for p in group_one:
        relay(p)
    for p in group_two:
        mine2(p)
    for p in group_one:
        last(p)
    for p in group_two:
        total(p)
    tiny_stage(4)
    for p in group_two:
        relay(p)
    for p in group_one:
        end(p)
    for p in group_two:
        last(p)
    for p in group_one:
        close(p)
    for p in group_two:
        end(p)
    for p in group_two:
        close(p)
    for ref, sem in pairs:
        landed(ref, send_sem.at[sem])
    for copy in sent:
        copy.wait_send()
    for copy in maybe:
        @pl.when(swapped_place)
        def _():
            copy.wait_send()


def back(odq, dkv, tokens, grad, normed_one, normed_two, vectors, tables, matrices, up, down, collective_id=1):
    hbm = pl.BlockSpec(memory_space=pl.ANY)
    vmem = pl.BlockSpec(memory_space=pltpu.VMEM)
    dma = pltpu.SemaphoreType.DMA
    bf, f32 = jnp.bfloat16, jnp.float32
    scratch = []
    for front_dims, rows in (((4, 2), 192), ((2,), 192), ((2, 2), 192), ((2,), 48), ((2, 2), 48), ((3,), 48)):
        for columns, _ in PARTS:
            scratch.append(pltpu.VMEM(front_dims + (rows, columns), bf))
    plain = ((ROWS, 768), bf)
    for shape, kind in (
        plain, plain, plain, plain, ((16, 768), f32), ((3, ROWS, 128), f32), ((768, 3072), bf), ((3072, 768), bf),
        ((768, 3072), bf), ((3072, 768), bf), ((ROWS, 768), f32), ((ROWS, 768), f32), ((8, 3072), f32), ((8, 3072), f32),
        ((4, 4, ROWS, WIDE), bf), ((4, 4, ROWS, WIDE), bf), ((2, 2, ROWS, WIDE), bf), ((2, 4, ROWS, WIDE), bf),
        ((4, ROWS, WIDE), bf), ((4, ROWS, WIDE), bf), plain, ((3, ROWS, 768), bf), ((4, 16, 768), f32), ((4, 3, 16, 768), f32),
    ):
        scratch.append(pltpu.VMEM(shape, kind))
    scratch += [dma((170,)), dma((170,)), dma((16,))]
    rows = jax.ShapeDtypeStruct((ROWS, 768), bf)
    return pl.pallas_call(
        back_kernel,
        out_shape=(rows, rows, jax.ShapeDtypeStruct((192, 3072), bf), jax.ShapeDtypeStruct((192, 3072), bf),
                   jax.ShapeDtypeStruct((768, 768), bf), jax.ShapeDtypeStruct((16, 768), f32)),
        in_specs=[hbm] * 11, out_specs=(vmem,) * 6,
        scratch_shapes=scratch,
        compiler_params=pltpu.CompilerParams(collective_id=collective_id, has_side_effects=True, vmem_limit_bytes=62 * 2**20),
        name="back",
    )(odq, dkv, tokens, grad, normed_one, normed_two, vectors, tables, matrices, up, down)


D = 768
HEADS = 12
HD = 64
ROT = 16
TOK_DEV = 256


def rotary_tables(positions):
    lanes = jnp.arange(128) % HD
    exponents = (lanes % 8).astype(jnp.float32) * 2.0 / ROT
    inverse = 10000.0 ** (-exponents)
    angles = positions.astype(jnp.float32)[:, None] * inverse[None, :]
    cosine, sine = jnp.cos(angles), jnp.sin(angles)
    keep = jnp.where(lanes < ROT, cosine, 1.0)
    ahead = jnp.where(lanes < 8, -sine, 0.0)
    behind = jnp.where((lanes >= 8) & (lanes < ROT), sine, 0.0)
    return jnp.stack([keep, ahead, behind])


def on_device(
    tokens, cotangent, pairing, first_gain, first_shift, qkv_weight, qkv_bias, dense_weight,
    second_gain, second_shift, up_weight, up_bias, down_weight, out_bias,
):
    bf, f32 = jnp.bfloat16, jnp.float32
    total_blocks = 64
    offsets = jnp.arange(BLK, dtype=jnp.int32)
    ctx_index = lax.axis_index("ctx")
    core = lax.rem(lax.axis_index("wsh"), 2)
    seq_of_layout = jnp.stack([pairing, total_blocks - 1 - pairing], 1).reshape(-1)
    layout_of_seq = (
        jnp.zeros((total_blocks,), jnp.int32)
        .at[seq_of_layout]
        .set(jnp.arange(total_blocks, dtype=jnp.int32))
    )
    own_blocks = lax.dynamic_slice(seq_of_layout, (2 * ctx_index,), (2,))
    row_blocks = lax.dynamic_slice(seq_of_layout, (16 * (ctx_index // 8) + 8 * core,), (8,))
    local_pos = (own_blocks[:, None] * BLK + offsets[None, :]).reshape(-1)
    tables = rotary_tables(local_pos)
    query_scale = HD ** (-0.5)

    shard = lax.broadcasted_iota(jnp.int32, (4, 1), 0) == lax.axis_index("wsh")
    small = (first_gain, first_shift, second_gain, second_shift, out_bias, qkv_bias, up_bias)
    spots = [jnp.where(shard, v[None, :], 0.0).astype(bf).reshape(-1) for v in small]
    vectors = jnp.concatenate(spots + [jnp.zeros((4 * D,), bf)]).reshape(16, D)
    grad_rows = cotangent[0]
    keys_values, queries_grads, normed_one, normed_two, vectors, matrices = front(
        tokens[0], grad_rows, tables, qkv_weight, dense_weight, vectors
    )
    up_shard, down_shard, keys_values = lax.optimization_barrier((up_weight, down_weight, keys_values))
    up_matrix = lax.all_gather(up_shard, "wsh", axis=0, tiled=True)
    down_matrix = lax.all_gather(down_shard, "wsh", axis=0, tiled=True)
    attended_dq, grad_kv = attention(row_blocks, layout_of_seq, queries_grads.reshape(1024, WIDE), keys_values.reshape(8192, WIDE))
    layer_output, input_grad, wide, upper, lower, sums = back(
        attended_dq.reshape(4, ROWS, WIDE), grad_kv.reshape(32, ROWS, WIDE), tokens[0], grad_rows, normed_one, normed_two,
        vectors, tables, matrices, up_matrix, down_matrix,
    )
    mine = lax.axis_index("wsh")
    gains = lax.dynamic_slice(sums, (0, 192 * mine), (5, 192))
    qkv_offset_grad = lax.dynamic_slice(sums[5:8].reshape(-1), (576 * mine,), (576,))
    up_offset_grad = lax.dynamic_slice(sums, (8 + mine, 0), (1, D))[0]
    return (
        layer_output[None], input_grad[None], gains[0], gains[1], wide[:, :2304].astype(f32), qkv_offset_grad,
        wide[:, 2304:].astype(f32), gains[2], gains[3], upper.astype(f32), up_offset_grad, lower.astype(f32), gains[4],
    )


def solution(mesh):
    rows, split, flat = P("wsh", "ctx", None), P("wsh", None), P("wsh")
    return jax.shard_map(
        on_device,
        mesh=mesh,
        in_specs=(rows, rows, P(), flat, flat, split, flat, split, flat, flat, split, flat, split, flat),
        out_specs=(rows, rows, flat, flat, split, flat, split, flat, flat, split, flat, split, flat),
        check_vma=False,
    )
```

```python
import functools

import jax
import jax.numpy as jnp
from jax import lax
from jax.experimental import pallas as pl
from jax.experimental.pallas import tpu as pltpu
from jax.sharding import PartitionSpec as P

G = 3; BLK = 128; LOG2E = 1.4426950408889634
NEG = -1e30

def attn_kernel(chunk, qpos, lay, qdo, kv_hbm, odq, dkv_hbm, kv, kvt, acc, probs, grads, tops, stage, sem, osem):
    blocks = chunk // BLK
    nblk = kv.shape[0] // BLK
    f32, bf = jnp.float32, jnp.bfloat16

    def load(i, _):
        pltpu.make_async_copy(kv_hbm.at[pl.ds(pl.multiple_of(lay[i] * BLK, BLK), BLK)], kv.at[pl.ds(pl.multiple_of(i * BLK, BLK), BLK)], sem.at[i]).start()
        return 0
    lax.fori_loop(0, nblk, load, 0)

    def land(i, _):
        rows = pl.ds(pl.multiple_of(i * chunk, chunk), chunk)
        for j in range(blocks):
            at = pl.ds(pl.multiple_of(i * chunk + j * BLK, BLK), BLK)
            pltpu.make_async_copy(kv_hbm.at[pl.ds(0, BLK)], kv.at[at], sem.at[i * blocks + j]).wait()
        acc[rows] = jnp.zeros((chunk, G * 128), f32)
        kvt[:, rows] = kv[rows].T
        return 0
    lax.fori_loop(0, nblk // blocks, land, 0)

    upper = lax.broadcasted_iota(jnp.int32, (128, 128), 0) < 64
    left = lax.broadcasted_iota(jnp.int32, (128, 128), 1) < 64

    def q_block(i, _):
        b = qpos[i]
        qrows = pl.ds(pl.multiple_of(i * BLK, BLK), BLK)
        last = b // blocks
        pairs = [qdo[qrows, h * 128:(h + 1) * 128] for h in range(G)]
        turned = [p.astype(f32).T for p in pairs]
        wide = [jnp.concatenate([jnp.where(upper, turned[h], 0.0).astype(bf), jnp.where(upper, 0.0, turned[h]).astype(bf)], 1) for h in range(G)]
        rest = b - last * blocks

        def pick(step, state):
            sizes = [chunk * (i + 1) // 4 for i in range(4)]
            return lax.switch(rest // (blocks // 4), [functools.partial(step, size) for size in sizes], state)

        def fwd(c, state, masked, size=chunk):
            at = pl.ds(pl.multiple_of(c * chunk, chunk), size)
            out = []
            every = [jnp.dot(kv[at, h * 128:(h + 1) * 128], wide[h], preferred_element_type=f32) for h in range(G)]
            kept = []
            for h in range(G):
                m, l, o = state[h]
                s = every[h][:, :128]
                grads[at, h * 128:(h + 1) * 128] = every[h][:, 128:]
                if masked:
                    key_i = lax.broadcasted_iota(jnp.int32, (size, BLK), 0)
                    row_i = lax.broadcasted_iota(jnp.int32, (size, BLK), 1) + rest * BLK
                    s = jnp.where(key_i <= row_i, s, NEG)
                new = jnp.maximum(m, jnp.max(s, 0, keepdims=True))
                p = jnp.exp(s - new)
                a = jnp.exp(m - new)
                l = l * a + jnp.sum(p, 0, keepdims=True)
                p = p.astype(bf)
                probs[at, h * 128:(h + 1) * 128] = p
                tops[c, h] = jnp.broadcast_to(new, (8, BLK))
                kept.append((new, l, o * a, p))
            for h in range(G):
                new, l, o, p = kept[h]
                o = o + jnp.dot(kvt[h * 128 + 64:(h + 1) * 128, at], p, preferred_element_type=f32)
                out.append((new, l, o))
            return tuple(out)

        state = tuple((jnp.full((1, BLK), NEG, f32), jnp.zeros((1, BLK), f32), jnp.zeros((64, BLK), f32)) for _ in range(G))
        state = lax.fori_loop(0, last, lambda c, s: fwd(c, s, False), state)
        state = pick(lambda size, s: fwd(last, s, True, size), state)
        lse, delta, outs = [], [], []
        for h in range(G):
            m, l, o = state[h]
            o = o / l
            outs.append(o)
            lse.append(m + jnp.log(l))
            delta.append(jnp.sum(o * turned[h][64:], 0, keepdims=True))
        narrow = [jnp.concatenate([jnp.where(left, pairs[h], jnp.zeros_like(pairs[h])), jnp.where(left, jnp.zeros_like(pairs[h]), pairs[h])], 0) for h in range(G)]

        def bwd(c, state, size=chunk):
            at = pl.ds(pl.multiple_of(c * chunk, chunk), size)
            out, work = [], []
            for h in range(G):
                cols = slice(h * 128, (h + 1) * 128)
                p = probs[at, cols].astype(f32) * jnp.exp(tops[c, h, 0:1] - lse[h])
                ds = (p * (grads[at, cols] - delta[h])).astype(bf)
                work.append((jnp.concatenate([ds, p.astype(bf)], 1), ds))
            for h in range(G):
                pair, ds = work[h]
                acc[at, h * 128:(h + 1) * 128] += jnp.dot(pair, narrow[h], preferred_element_type=f32)
                out.append(state[h] + jnp.dot(kvt[h * 128:h * 128 + 64, at], ds, preferred_element_type=f32))
            return tuple(out)

        dq = tuple(jnp.zeros((64, BLK), f32) for _ in range(G))
        dq = lax.fori_loop(0, last, bwd, dq)
        dq = pick(lambda size, s: bwd(last, s, size), dq)
        for h in range(G):
            odq[qrows, h * 128:(h + 1) * 128] = jnp.concatenate([outs[h], dq[h]], 0).T.astype(bf)
        return 0
    lax.fori_loop(0, qpos.shape[0], q_block, 0)

    def leave(slot, j):
        return pltpu.make_async_copy(stage.at[slot, j], dkv_hbm.at[pl.ds(0, BLK)], osem.at[slot, j])

    def send(i, _):
        slot = lax.rem(i, 2)
        @pl.when(i >= 2)
        def _():
            for j in range(4):
                leave(slot, j).wait()
        for j in range(4):
            at = i * 4 + j
            stage[slot, j] = acc[pl.ds(pl.multiple_of(at * BLK, BLK), BLK)].astype(bf)
            pltpu.make_async_copy(stage.at[slot, j], dkv_hbm.at[pl.ds(pl.multiple_of(lay[at] * BLK, BLK), BLK)], osem.at[slot, j]).start()
        return 0
    lax.fori_loop(0, nblk // 4, send, 0)
    for slot in range(2):
        for j in range(4):
            leave(slot, j).wait()


def attention(qpos, lay, qdo, kv, chunk=1024):
    n = kv.shape[0]
    smem = pl.BlockSpec(memory_space=pltpu.SMEM)
    vmem = pl.BlockSpec(memory_space=pltpu.VMEM)
    hbm = pl.BlockSpec(memory_space=pl.ANY)
    return pl.pallas_call(
        functools.partial(attn_kernel, chunk),
        out_shape=(jax.ShapeDtypeStruct(qdo.shape, jnp.bfloat16), jax.ShapeDtypeStruct(kv.shape, jnp.bfloat16)),
        in_specs=[smem, smem, vmem, hbm], out_specs=(vmem, hbm),
        scratch_shapes=[pltpu.VMEM((n, G * 128), jnp.bfloat16), pltpu.VMEM((G * 128, n), jnp.bfloat16),
            pltpu.VMEM((n, G * 128), jnp.float32), pltpu.VMEM((n, G * 128), jnp.bfloat16), pltpu.VMEM((n, G * 128), jnp.float32), pltpu.VMEM((n // chunk, G, 8, BLK), jnp.float32),
            pltpu.VMEM((2, 4, BLK, G * 128), jnp.bfloat16),
            pltpu.SemaphoreType.DMA((n // BLK,)), pltpu.SemaphoreType.DMA((2, 4))],
        compiler_params=pltpu.CompilerParams(vmem_limit_bytes=62 * 2**20),
        name="attention",
    )(qpos, lay, qdo, kv)


MESH = pl.DeviceIdType.MESH
ROWS, WIDE = 256, 384


def place():
    c, w = lax.axis_index("ctx"), lax.axis_index("wsh")
    return c // 8, lax.rem(c // 4, 2), lax.rem(c, 4), w // 2, lax.rem(w, 2)


def device(z, yl, x, yh, core):
    return (z * 8 + yl * 4 + x, yh * 2 + core)


def greet(devices, extra=None, extra_count=0):
    barrier = pltpu.get_barrier_semaphore()
    for d in devices:
        pl.semaphore_signal(barrier, inc=1, device_id=d, device_id_type=MESH)
    if extra is not None:
        @pl.when(extra_count == 1)
        def _():
            pl.semaphore_signal(barrier, inc=1, device_id=extra, device_id_type=MESH)
    pl.semaphore_wait(barrier, len(devices) + extra_count)


def landed(ref, sem):
    pltpu.make_async_copy(ref, ref, sem).wait()


def front_kernel(tokens_hbm, grad_hbm, tables_hbm, qkv, dense, vectors_hbm, kv_all, qdo, one_hbm, two_hbm, vectors_out, weights_out,
                 tokens, grad, tables, vectors, normed_one, normed_two, all_vectors, bring_sem, weights, vec_in, kvs, qds, local_sem, send_sem, recv_sem, kv_send, kv_recv, q_send, q_recv):
    z, yl, x, yh, core = place()
    bring = [pltpu.make_async_copy(src, dst, bring_sem.at[i]) for i, (src, dst) in enumerate(((vectors_hbm, vectors), (tokens_hbm, tokens), (tables_hbm, tables), (grad_hbm, grad)))]
    for copy in bring:
        copy.start()
    f32, bf = jnp.float32, jnp.bfloat16
    me = yh * 2 + core
    far = (1 - yh) * 2 + core
    other = (1 - yh) * 2 + 1 - core
    swap = yl != core
    partner = [device(z, core, lax.rem(x + d, 4), yh, yl) for d in range(4)]
    sib = device(z, yl, x, yh, 1 - core)
    cross = device(z, 1 - yl, x, 1 - yh, core)
    others = [device(z, yl, x, 1 - yh, core), device(z, yl, x, 1 - yh, 1 - core)]
    xs = [device(z, yl, lax.rem(x + d, 4), yh, core) for d in (1, 3)]
    zs = [device(lax.rem(z + d, 4), yl, x, yh, core) for d in (1, 3)]
    greet([sib, cross] + others + xs + zs + partner[1:], partner[0], lax.rem(yl + core, 2))
    count = [0]
    sent = []

    def remote(src, dst, to):
        sem = count[0]
        count[0] += 1
        copy = pltpu.make_async_remote_copy(src_ref=src, dst_ref=dst, send_sem=send_sem.at[sem], recv_sem=recv_sem.at[sem], device_id=to, device_id_type=MESH)
        copy.start()
        sent.append(copy)
        return sem

    def arrive(ref, sem):
        landed(ref, recv_sem.at[sem])

    def rows(i, start, size):
        return weights.at[i, pl.ds(pl.multiple_of(start, 16), size)]

    shards = [qkv.at[:, pl.ds(768, 768)], qkv.at[:, pl.ds(1536, 768)], qkv.at[:, pl.ds(0, 768)], dense]
    quarter = [x, z, x, z]
    ring = [xs, zs, xs, zs]
    bring[0].wait()
    vec_sem = [remote(vectors, vec_in.at[i], to) for i, to in enumerate([sib] + others)]
    cross_sem = [remote(shards[i].at[pl.ds(pl.multiple_of(quarter[i] * 48, 16), 48)], rows(i, me * 192 + quarter[i] * 48, 48), cross) for i in range(4)]
    own, late = [], [[], [], [], []]
    for i in range(4):
        copy = pltpu.make_async_copy(shards[i], rows(i, me * 192, 192), local_sem.at[i])
        copy.start()
        own.append(copy)
        late[i].append((rows(i, (yh * 2 + 1 - core) * 192, 192), remote(shards[i], rows(i, me * 192, 192), sib)))

    for copy in bring[1:]:
        copy.wait()
    values = tokens[...].astype(f32)
    centered = values - jnp.mean(values, -1, keepdims=True)
    unit = centered * lax.rsqrt(jnp.mean(centered * centered, -1, keepdims=True) + 1e-05)
    for i in range(3):
        arrive(vec_in.at[i], vec_sem[i])
    vec = vectors[...].astype(f32) + vec_in[0].astype(f32) + vec_in[1].astype(f32) + vec_in[2].astype(f32)
    all_vectors[...] = vec
    normed_one[...] = (unit * vec[0:1] + vec[1:2]).astype(bf)
    normed_two[...] = (unit * vec[2:3] + vec[3:4]).astype(bf)

    leave = [pltpu.make_async_copy(src, dst, bring_sem.at[4 + i]) for i, (src, dst) in enumerate(((all_vectors, vectors_out), (normed_one, one_hbm), (normed_two, two_hbm)))]
    for copy in leave:
        copy.start()
    cuts = ((0, 32), (32, 16))
    ring_sem, half_sem = {}, {}

    def start_ring(i):
        mine = rows(i, far * 192 + quarter[i] * 48, 48)
        arrive(mine, cross_sem[i])
        for way in (0, 1):
            ring_sem[i, way] = remote(mine, mine, ring[i][way])
        late[i].append((rows(i, other * 192 + quarter[i] * 48, 48), remote(mine, mine, sib)))

    def relay(i):
        for way in (0, 1):
            b = lax.rem(quarter[i] + 3 - 2 * way, 4)
            got = rows(i, far * 192 + b * 48, 48)
            arrive(got, ring_sem[i, way])
            part = rows(i, far * 192 + b * 48 + cuts[way][0], cuts[way][1])
            half_sem[i, way] = remote(part, part, ring[i][way])
            late[i].append((rows(i, other * 192 + b * 48, 48), remote(got, got, sib)))

    def finish(i):
        for way in (0, 1):
            start = lax.rem(quarter[i] + 2, 4) * 48 + cuts[way][0]
            got = rows(i, far * 192 + start, cuts[way][1])
            arrive(got, half_sem[i, way])
            late[i].append((rows(i, other * 192 + start, cuts[way][1]), remote(got, got, sib)))

    def complete(i):
        for ref, sem in late[i]:
            arrive(ref, sem)
        own[i].wait()

    left = lax.broadcasted_iota(jnp.int32, (ROWS, 128), 1) < 64
    keep, ahead, behind = tables[0], tables[1], tables[2]

    def turn(tile):
        return tile * keep + pltpu.roll(tile, 120, 1) * ahead + pltpu.roll(tile, 8, 1) * behind

    def pack(into, first, second):
        for t in range(6):
            lanes = slice(128 * t, 128 * t + 128)
            a, b = first(lanes), second(lanes)
            for head, tile in ((2 * t, jnp.where(left, a, pltpu.roll(b, 64, 1))), (2 * t + 1, jnp.where(left, pltpu.roll(a, 64, 1), b))):
                into[head // 3, :, 128 * (head % 3):128 * (head % 3) + 128] = tile.astype(bf)

    def dot(a, b):
        return jnp.dot(a, b, preferred_element_type=f32)

    def exchange(src, dst_of, send, recv):
        out = []
        for d in (0, 2, 1, 3):
            args = (src.at[lax.rem(x + d, 4)], dst_of, send.at[d], recv.at[d], partner[d])
            copy = pltpu.make_async_remote_copy(src_ref=args[0], dst_ref=args[1], send_sem=args[2], recv_sem=args[3], device_id=args[4], device_id_type=MESH)
            if d == 0:
                @pl.when(swap)
                def _():
                    copy.start()
                @pl.when(jnp.logical_not(swap))
                def _():
                    pltpu.make_async_copy(args[0], args[1], args[3]).start()
            else:
                copy.start()
            out.append((d, copy))
        return out

    for i in range(4):
        start_ring(i)
    for i in (0, 1):
        relay(i)
    for i in (0, 1):
        finish(i)
    for i in (0, 1):
        complete(i)
    one = normed_one[...]
    pack(kvs,
         lambda lanes: turn(dot(one, weights[0, :, lanes]) + vec[6:7, lanes]),
         lambda lanes: dot(one, weights[1, :, lanes]) + vec[7:8, lanes])
    mine = z * 8 + yl * 4 + x
    sent_kv = exchange(kvs, kv_all.at[mine], kv_send, kv_recv)
    def slot(zz, cc, d):
        return kv_all.at[lax.rem(zz, 4) * 8 + cc * 4 + lax.rem(x + 4 - d, 4)]

    half = ROWS // 2
    up_sem, part_sem, sib_sem = {}, {}, {}
    for d in (0, 1, 3, 2):
        here = slot(z, core, d)
        landed(here, kv_recv.at[d])
        for way in (0, 1):
            up_sem[way, d] = remote(here, here, zs[way])
        sib_sem[0, d] = remote(here, here, sib)
    for i in (2, 3):
        relay(i)
    for i in (2, 3):
        finish(i)
    for i in (2, 3):
        complete(i)
    g = grad[...]
    pack(qds,
         lambda lanes: turn(dot(one, weights[2, :, lanes]) + vec[5:6, lanes]) * 0.125,
         lambda lanes: lax.dot_general(g, weights[3, lanes, :], (((1,), (1,)), ((), ())), preferred_element_type=f32))
    sent_q = exchange(qds, qdo.at[x], q_send, q_recv)
    keep_out = pltpu.make_async_copy(weights, weights_out, local_sem.at[4])
    keep_out.start()

    for d in (0, 1, 3, 2):
        for way in (0, 1):
            here = slot(z + 3 - 2 * way, core, d)
            arrive(here, up_sem[way, d])
            part = here.at[pl.ds(way * half, half)]
            part_sem[way, d] = remote(part, part, zs[way])
            sib_sem[1 + way, d] = remote(here, here, sib)
    for d in (0, 1, 3, 2):
        for way in (0, 1):
            part = slot(z + 2, core, d).at[pl.ds(way * half, half)]
            arrive(part, part_sem[way, d])
            sib_sem[3 + way, d] = remote(part, part, sib)
    for d in range(4):
        arrive(slot(z, 1 - core, d), sib_sem[0, d])
        for way in (0, 1):
            arrive(slot(z + 3 - 2 * way, 1 - core, d), sib_sem[1 + way, d])
            arrive(slot(z + 2, 1 - core, d).at[pl.ds(way * half, half)], sib_sem[3 + way, d])
        landed(qdo.at[lax.rem(x + 4 - d, 4)], q_recv.at[d])
    keep_out.wait()
    for copy in leave:
        copy.wait()
    for copy in sent:
        copy.wait_send()
    for d, copy in sent_kv + sent_q:
        if d == 0:
            @pl.when(swap)
            def _():
                copy.wait_send()
        else:
            copy.wait_send()


def front(tokens, grad, tables, qkv, dense, vectors, collective_id=0):
    hbm = pl.BlockSpec(memory_space=pl.ANY)
    dma = pltpu.SemaphoreType.DMA
    bf, f32 = jnp.bfloat16, jnp.float32
    rows = jax.ShapeDtypeStruct((ROWS, 768), bf)
    return pl.pallas_call(
        front_kernel,
        out_shape=(jax.ShapeDtypeStruct((32, ROWS, WIDE), bf), jax.ShapeDtypeStruct((4, ROWS, WIDE), bf), rows, rows,
                   jax.ShapeDtypeStruct((16, 768), f32), jax.ShapeDtypeStruct((4, 768, 768), bf)),
        in_specs=[hbm] * 6, out_specs=(hbm,) * 6,
        scratch_shapes=[pltpu.VMEM((ROWS, 768), bf), pltpu.VMEM((ROWS, 768), bf), pltpu.VMEM((3, ROWS, 128), f32), pltpu.VMEM((16, 768), bf),
                        pltpu.VMEM((ROWS, 768), bf), pltpu.VMEM((ROWS, 768), bf), pltpu.VMEM((16, 768), f32), dma((7,)), pltpu.VMEM((4, 768, 768), bf), pltpu.VMEM((3, 16, 768), bf), pltpu.VMEM((4, ROWS, WIDE), bf), pltpu.VMEM((4, ROWS, WIDE), bf),
                        dma((5,)), dma((100,)), dma((100,)), dma((4,)), dma((4,)), dma((4,)), dma((4,))],
        compiler_params=pltpu.CompilerParams(collective_id=collective_id, has_side_effects=True, vmem_limit_bytes=62 * 2**20),
        name="front",
    )(tokens, grad, tables, qkv, dense, vectors)


PARTS = ((384, False), (384, True), (768, True), (384, False), (384, False))
TILE = 384


def erf(values):
    v = jnp.clip(values, -4.0, 4.0)
    s = v * v
    top = jnp.float32(-2.72614225801306e-10)
    for coefficient in (2.77068142495902e-08, -2.10102402082508e-06, -5.69250639462346e-05, -7.34990630326855e-04, -2.95459980854025e-03, -1.60960333262415e-02):
        top = top * s + coefficient
    low = jnp.float32(-1.45660718464996e-05)
    for coefficient in (-2.13374055278905e-04, -1.68282697438203e-03, -7.37332916720468e-03, -1.42647390514189e-02):
        low = low * s + coefficient
    return v * top / low


def back_kernel(odq, dkv, tokens_hbm, grad_hbm, one_hbm, two_hbm, vectors_hbm, tables_hbm, matrices, up_hbm, down_hbm,
                layer_output, input_grad, wide_out, upper_out, lower_out, vector_out, *refs):
    sib_in, far_in, near_in, far_two, near_two, y_in = (refs[5 * i : 5 * i + 5] for i in range(6))
    (tokens, grad, normed_one, normed_two, vectors, tables, up, down_w, upper, lower, mlp, back_two, up_bias, bias_grad,
     held, held_in, held_far, held_near, odq_own, dkv_own, attended, mixed, tiny, tiny_in, send_sem, recv_sem, local_sem) = refs[30:]
    z, yl, x, yh, core = place()
    f32, bf = jnp.float32, jnp.bfloat16
    swapped_place = yl != core
    partner = [device(z, core, lax.rem(x + d, 4), yh, yl) for d in range(4)]
    xs = [device(z, yl, lax.rem(x + d, 4), yh, core) for d in (1, 3, 2)]
    zs = [device(lax.rem(z + d, 4), yl, x, yh, core) for d in (1, 3, 2)]
    ys = [device(z, 1 - yl, x, yh, core), device(z, yl, x, 1 - yh, core), device(z, 1 - yl, x, 1 - yh, core)]
    sib = device(z, yl, x, yh, 1 - core)
    greet([sib] + xs + zs + ys + partner[1:], partner[0], lax.rem(yl + core, 2))
    count = [0]
    local_count = [0]
    sent, maybe = [], []
    pairs = []

    def bring(src, dst):
        copy = pltpu.make_async_copy(src, dst, local_sem.at[local_count[0]])
        local_count[0] += 1
        copy.start()
        return copy

    def number():
        count[0] += 1
        return count[0] - 1

    def describe(src, dst, sem, to):
        return pltpu.make_async_remote_copy(src_ref=src, dst_ref=dst, send_sem=send_sem.at[sem], recv_sem=recv_sem.at[sem], device_id=to, device_id_type=MESH)

    def remote(src, dst, to):
        sem = number()
        copy = describe(src, dst, sem, to)
        copy.start()
        sent.append(copy)
        return sem

    def both(sources, dst, to):
        sem = number()
        for s in (0, 1):
            describe(sources[s], dst.at[s], sem, to).start()
        pairs.append((dst, sem))
        return sem

    def arrive(ref, sem):
        landed(ref, recv_sem.at[sem])

    def exchange(src, dst, d):
        sem = number()
        part = src.at[lax.rem(x + d, 4)]
        copy = describe(part, dst, sem, partner[d])
        if d == 0:
            @pl.when(swapped_place)
            def _():
                copy.start()
            @pl.when(jnp.logical_not(swapped_place))
            def _():
                pltpu.make_async_copy(part, dst, recv_sem.at[sem]).start()
            maybe.append(copy)
        else:
            copy.start()
            sent.append(copy)
        return sem

    def dot(left, right, left_dim, right_dim):
        return lax.dot_general(left, right, (((left_dim,), (right_dim,)), ((), ())), preferred_element_type=f32)

    def group(zz, cc):
        return dkv.at[pl.ds(lax.rem(zz, 4) * 8 + cc * 4, 4)]

    held_sem, held_load = [], []
    for k, zz in enumerate((z + 2, z + 1, z + 3, z)):
        held_sem.append(remote(group(zz, 1 - core), held_in.at[k], sib))
        held_load.append(bring(group(zz, core), held.at[k]))
    inputs = [bring(src, dst) for src, dst in ((two_hbm, normed_two), (grad_hbm, grad), (vectors_hbm, vectors), (up_hbm, up), (down_hbm, down_w),
                                               (tokens_hbm, tokens), (one_hbm, normed_one), (tables_hbm, tables))]
    odq_sem = [exchange(odq, odq_own.at[x], d) for d in range(4)]
    def feed(t, _):
        at = pl.ds(pl.multiple_of(t * TILE, TILE), TILE)
        values = dot(normed_two[...], up[:, at], 1, 0) + up_bias[0:1, at]
        inner = 0.5 + 0.5 * erf(values * 0.7071067811865476)
        slope = inner + values * (0.3989422804014327 * jnp.exp(-0.5 * values * values))
        active = (values * inner).astype(bf)
        grads = (dot(grad[...], down_w[at], 1, 1) * slope).astype(bf)
        mlp[...] += dot(active, down_w[at], 1, 0)
        back_two[...] += dot(grads, up[:, at], 1, 1)
        bias_grad[0:1, at] = jnp.sum(grads.astype(f32), 0, keepdims=True)
        upper[:, at] = dot(normed_two[...], grads, 0, 0).astype(bf)
        lower[at] = dot(active, grad[...], 0, 0).astype(bf)
        return 0

    def sum_held(k, chunks, terms):
        def step(i, _):
            j, r = chunks[0] + i // 2, pl.ds(pl.multiple_of(lax.rem(i, 2) * 128, 128), 128)
            value = held[k, j, r].astype(f32) + held_in[k, j, r].astype(f32)
            for ref, low in terms:
                value = value + ref[j - low, r].astype(f32)
            held[k, j, r] = value.astype(bf)
            return 0
        lax.fori_loop(0, 2 * (chunks[1] - chunks[0]), step, 0)

    held_load[0].wait()
    arrive(held_in.at[0], held_sem[0])
    sum_held(0, (0, 4), [])
    held_far_sem = [remote(held.at[0, pl.ds(2 * way, 2)], held_far.at[way], zs[way]) for way in (0, 1)]
    mlp[...] = jnp.zeros_like(mlp)
    back_two[...] = jnp.zeros_like(back_two)
    for copy in inputs:
        copy.wait()
    for i in range(4):
        up_bias[0:1, 768 * i:768 * i + 768] = vectors[8 + i:9 + i]
    lax.fori_loop(0, 3, feed, 0)
    held_near_sem = []
    for way in (0, 1):
        k = 1 + way
        held_load[k].wait()
        arrive(held_in.at[k], held_sem[k])
        sum_held(k, (2 - 2 * way, 4 - 2 * way), [])
        arrive(held_far.at[way], held_far_sem[way])
        sum_held(k, (2 * way, 2 * way + 2), [(held_far.at[way], 2 * way)])
        held_near_sem.append(remote(held.at[k], held_near.at[way], zs[way]))
    lax.fori_loop(3, 8, feed, 0)
    fetch = [bring(matrices.at[i], up.at[:, pl.ds(768 * i, 768)]) for i in range(4)]

    def piece(p, w, a):
        if p < 2:
            return down_w.at[pl.ds(pl.multiple_of(a * 768 + w * 192, 192), 192), pl.ds(384 * p, 384)]
        if p == 2:
            return upper.at[pl.ds(pl.multiple_of(w * 192, 192), 192), pl.ds(pl.multiple_of(a * 768, 768), 768)]
        return lower.at[pl.ds(pl.multiple_of(w * 768 + a * 192, 192), 192), pl.ds(384 * (p - 3), 384)]

    def own(p, k, s):
        return piece(p, 2 * s + core, lax.rem(first[p] + (2, 1, 3, 0)[k], 4))

    def result(p, a, start, size):
        if p < 2:
            return wide_out.at[pl.ds(start, size), pl.ds(pl.multiple_of(a * 768 + 384 * p, 384), 384)]
        if p == 2:
            return upper_out.at[pl.ds(start, size), pl.ds(pl.multiple_of(a * 768, 768), 768)]
        return lower_out.at[pl.ds(pl.multiple_of(a * 192 + start, 16), size), pl.ds(384 * (p - 3), 384)]

    first = [x if part[1] else z for part in PARTS]
    second = [z if part[1] else x for part in PARTS]
    ring_one = [xs if part[1] else zs for part in PARTS]
    ring_two = [zs if part[1] else xs for part in PARTS]
    sems = {}

    def swap(p):
        for k, ahead in enumerate((2, 1, 3, 0)):
            a = lax.rem(first[p] + ahead, 4)
            sems["sib", p, k] = both([piece(p, 2 * s + 1 - core, a) for s in (0, 1)], sib_in[p].at[k], sib)

    def swapped(p, k):
        arrive(sib_in[p].at[k], sems["sib", p, k])

    def add(rows, into, terms):
        def body(i, _):
            at = pl.ds(pl.multiple_of(i * 48, 48), 48)
            total = into[at].astype(f32)
            for term in terms:
                total = total + term[at].astype(f32)
            into[at] = total.astype(bf)
            return 0
        lax.fori_loop(0, rows // 48, body, 0)

    def quarter(b):
        return pl.ds(pl.multiple_of(lax.rem(b, 4) * 48, 48), 48)

    def far(p):
        swapped(p, 0)
        for s in (0, 1):
            add(192, own(p, 0, s), [sib_in[p].at[0, s]])
            sems["far", p, s] = remote(own(p, 0, s), far_in[p].at[s], ring_one[p][s])

    def near(p):
        for way in (0, 1):
            k = 1 + way
            swapped(p, k)
            add(192, own(p, k, 1 - way), [sib_in[p].at[k, 1 - way]])
            arrive(far_in[p].at[way], sems["far", p, way])
            add(192, own(p, k, way), [sib_in[p].at[k, way], far_in[p].at[way]])
            sems["near", p, way] = both([own(p, k, s) for s in (0, 1)], near_in[p].at[way], ring_one[p][way])

    def mine(p):
        swapped(p, 3)
        for way in (0, 1):
            arrive(near_in[p].at[way], sems["near", p, way])
        for s in (0, 1):
            add(192, own(p, 3, s), [sib_in[p].at[3, s], near_in[p].at[0, s], near_in[p].at[1, s]])
        for s in (0, 1):
            sems["far2", p, s] = remote(own(p, 3, s).at[quarter(second[p] + 2)], far_two[p].at[s], ring_two[p][s])

    def near2(p):
        for way in (0, 1):
            at = quarter(second[p] + 1 + 2 * way)
            arrive(far_two[p].at[way], sems["far2", p, way])
            add(48, own(p, 3, way).at[at], [far_two[p].at[way]])
            sems["near2", p, way] = both([own(p, 3, s).at[at] for s in (0, 1)], near_two[p].at[way], ring_two[p][way])

    def mine2(p):
        at = quarter(second[p])
        for way in (0, 1):
            arrive(near_two[p].at[way], sems["near2", p, way])
        for s in (0, 1):
            add(48, own(p, 3, s).at[at], [near_two[p].at[0, s], near_two[p].at[1, s]])
        for i, half in enumerate((yh, 1 - yh, 1 - yh)):
            sems["y", p, i] = remote(own(p, 3, half).at[at], y_in[p].at[i], ys[i])

    def total(p):
        for i in range(3):
            arrive(y_in[p].at[i], sems["y", p, i])
        value = own(p, 3, yh)[quarter(second[p])].astype(f32)
        for i in range(3):
            value = value + y_in[p][i].astype(f32)
        done = result(p, first[p], pl.multiple_of(second[p] * 48, 16), 48)
        done[...] = value.astype(bf)
        for way in (0, 1):
            sems["ring", p, way] = remote(done, done, ring_two[p][way])

    cuts = ((0, 32), (32, 16))

    def relay(p):
        for way in (0, 1):
            b = lax.rem(second[p] + 3 - 2 * way, 4)
            arrive(result(p, first[p], pl.multiple_of(b * 48, 16), 48), sems["ring", p, way])
            part = result(p, first[p], pl.multiple_of(b * 48 + cuts[way][0], 16), cuts[way][1])
            sems["relay", p, way] = remote(part, part, ring_two[p][way])

    def last(p):
        b = lax.rem(second[p] + 2, 4)
        for way in (0, 1):
            arrive(result(p, first[p], pl.multiple_of(b * 48 + cuts[way][0], 16), cuts[way][1]), sems["relay", p, way])
        block = result(p, first[p], 0, 192)
        for way in (0, 1):
            sems["last", p, way] = remote(block, block, ring_one[p][way])

    def end(p):
        for way in (0, 1):
            a = lax.rem(first[p] + 3 - 2 * way, 4)
            arrive(result(p, a, 0, 192), sems["last", p, way])
            part = result(p, a, 96 * way, 96)
            sems["end", p, way] = remote(part, part, ring_one[p][way])

    def close(p):
        for way in (0, 1):
            arrive(result(p, lax.rem(first[p] + 2, 4), 96 * way, 96), sems["end", p, way])

    def tiny_stage(step):
        groups = ([sib], xs, zs, ys)
        if step > 0:
            for i in range(len(groups[step - 1])):
                arrive(tiny_in.at[step - 1, i], sems["tiny", step - 1, i])
            value = tiny[step - 1]
            for i in range(len(groups[step - 1])):
                value = value + tiny_in[step - 1, i]
            if step == 4:
                vector_out[...] = value
                return
            tiny[step] = value
        for i, to in enumerate(groups[step]):
            sems["tiny", step, i] = remote(tiny.at[step], tiny_in.at[step, i], to)

    group_one, group_two = (2, 3, 4), (0, 1)
    for p in group_one:
        swap(p)
    for p in group_one:
        far(p)
    for way in (0, 1):
        arrive(held_near.at[way], held_near_sem[way])
    held_load[3].wait()
    arrive(held_in.at[3], held_sem[3])
    sum_held(3, (0, 4), [(held_near.at[0], 0), (held_near.at[1], 0)])
    dkv_sem = [exchange(held.at[3], dkv_own.at[x], d) for d in range(4)]
    for p in group_one:
        near(p)
    for d in range(4):
        h = lax.rem(x + 4 - d, 4)
        arrive(odq_own.at[h], odq_sem[d])
        arrive(dkv_own.at[h], dkv_sem[d])

    left = lax.broadcasted_iota(jnp.int32, (ROWS, 128), 1) < 64
    keep, ahead, behind = tables[0], tables[1], tables[2]

    def turn_back(tile):
        return tile * keep + pltpu.roll(tile * ahead, 8, 1) + pltpu.roll(tile * behind, 120, 1)

    def unpack(slabs, t):
        even, odd = (slabs[h // 3, :, 128 * (h % 3):128 * (h % 3) + 128].astype(f32) for h in (2 * t, 2 * t + 1))
        return jnp.where(left, even, pltpu.roll(odd, 64, 1)), jnp.where(left, pltpu.roll(even, 64, 1), odd)

    for t in range(6):
        lanes = slice(128 * t, 128 * t + 128)
        out, query = unpack(odq_own, t)
        key, value = unpack(dkv_own, t)
        attended[:, lanes] = out.astype(bf)
        mixed[0, :, lanes] = (turn_back(query) * 0.125).astype(bf)
        mixed[1, :, lanes] = turn_back(key).astype(bf)
        mixed[2, :, lanes] = value.astype(bf)
    g = grad[...]
    one = normed_one[...]
    for i in range(3):
        down_w[768 * i:768 * i + 768] = dot(one, mixed[i], 0, 0).astype(bf)
    down_w[2304:] = dot(attended[...], g, 0, 0).astype(bf)
    for p in group_two:
        swap(p)
    for p in group_two:
        far(p)
    for copy in fetch:
        copy.wait()
    values = tokens[...].astype(f32)
    centered = values - jnp.mean(values, -1, keepdims=True)
    scale = lax.rsqrt(jnp.mean(centered * centered, -1, keepdims=True) + 1e-05)
    unit = centered * scale
    back_one = dot(mixed[0], up[:, 1536:2304], 1, 1) + dot(mixed[1], up[:, 0:768], 1, 1) + dot(mixed[2], up[:, 768:1536], 1, 1)
    wide_grad = g.astype(f32)
    into = wide_grad
    sums = []
    for back, gain in ((back_one, vectors[0:1]), (back_two[...], vectors[2:3])):
        sums.append(jnp.sum(back * unit, 0, keepdims=True))
        sums.append(jnp.sum(back, 0, keepdims=True))
        scaled = back * gain
        into = into + scale * (scaled - jnp.mean(scaled, -1, keepdims=True) - unit * jnp.mean(scaled * unit, -1, keepdims=True))
    input_grad[...] = into.astype(bf)
    sums.append(jnp.sum(wide_grad, 0, keepdims=True))
    sums.extend(jnp.sum(mixed[i].astype(f32), 0, keepdims=True) for i in range(3))
    sums.extend(bias_grad[0:1, 768 * i:768 * i + 768] for i in range(4))
    tiny[0] = jnp.concatenate(sums + [jnp.zeros((4, 768), f32)], 0)
    tiny_stage(0)
    for p in group_one:
        mine(p)
    for p in group_two:
        near(p)
    layer_output[...] = (values + mlp[...] + dot(attended[...], up[:, 2304:3072], 1, 0) + vectors[4:5]).astype(bf)
    tiny_stage(1)
    for p in group_one:
        near2(p)
    tiny_stage(2)
    for p in group_two:
        mine(p)
    for p in group_one:
        mine2(p)
    tiny_stage(3)
    for p in group_one:
        total(p)
    for p in group_two:
        near2(p)
    for p in group_one:
        relay(p)
    for p in group_two:
        mine2(p)
    for p in group_one:
        last(p)
    for p in group_two:
        total(p)
    tiny_stage(4)
    for p in group_two:
        relay(p)
    for p in group_one:
        end(p)
    for p in group_two:
        last(p)
    for p in group_one:
        close(p)
    for p in group_two:
        end(p)
    for p in group_two:
        close(p)
    for ref, sem in pairs:
        landed(ref, send_sem.at[sem])
    for copy in sent:
        copy.wait_send()
    for copy in maybe:
        @pl.when(swapped_place)
        def _():
            copy.wait_send()


def back(odq, dkv, tokens, grad, normed_one, normed_two, vectors, tables, matrices, up, down, collective_id=1):
    hbm = pl.BlockSpec(memory_space=pl.ANY)
    vmem = pl.BlockSpec(memory_space=pltpu.VMEM)
    dma = pltpu.SemaphoreType.DMA
    bf, f32 = jnp.bfloat16, jnp.float32
    scratch = []
    for front_dims, rows in (((4, 2), 192), ((2,), 192), ((2, 2), 192), ((2,), 48), ((2, 2), 48), ((3,), 48)):
        for columns, _ in PARTS:
            scratch.append(pltpu.VMEM(front_dims + (rows, columns), bf))
    plain = ((ROWS, 768), bf)
    for shape, kind in (
        plain, plain, plain, plain, ((16, 768), f32), ((3, ROWS, 128), f32), ((768, 3072), bf), ((3072, 768), bf),
        ((768, 3072), bf), ((3072, 768), bf), ((ROWS, 768), f32), ((ROWS, 768), f32), ((8, 3072), f32), ((8, 3072), f32),
        ((4, 4, ROWS, WIDE), bf), ((4, 4, ROWS, WIDE), bf), ((2, 2, ROWS, WIDE), bf), ((2, 4, ROWS, WIDE), bf),
        ((4, ROWS, WIDE), bf), ((4, ROWS, WIDE), bf), plain, ((3, ROWS, 768), bf), ((4, 16, 768), f32), ((4, 3, 16, 768), f32),
    ):
        scratch.append(pltpu.VMEM(shape, kind))
    scratch += [dma((170,)), dma((170,)), dma((16,))]
    rows = jax.ShapeDtypeStruct((ROWS, 768), bf)
    return pl.pallas_call(
        back_kernel,
        out_shape=(rows, rows, jax.ShapeDtypeStruct((192, 3072), bf), jax.ShapeDtypeStruct((192, 3072), bf),
                   jax.ShapeDtypeStruct((768, 768), bf), jax.ShapeDtypeStruct((16, 768), f32)),
        in_specs=[hbm] * 11, out_specs=(vmem,) * 6,
        scratch_shapes=scratch,
        compiler_params=pltpu.CompilerParams(collective_id=collective_id, has_side_effects=True, vmem_limit_bytes=62 * 2**20),
        name="back",
    )(odq, dkv, tokens, grad, normed_one, normed_two, vectors, tables, matrices, up, down)


D = 768
HEADS = 12
HD = 64
ROT = 16
TOK_DEV = 256


def rotary_tables(positions):
    lanes = jnp.arange(128) % HD
    exponents = (lanes % 8).astype(jnp.float32) * 2.0 / ROT
    inverse = 10000.0 ** (-exponents)
    angles = positions.astype(jnp.float32)[:, None] * inverse[None, :]
    cosine, sine = jnp.cos(angles), jnp.sin(angles)
    keep = jnp.where(lanes < ROT, cosine, 1.0)
    ahead = jnp.where(lanes < 8, -sine, 0.0)
    behind = jnp.where((lanes >= 8) & (lanes < ROT), sine, 0.0)
    return jnp.stack([keep, ahead, behind])


def on_device(
    tokens, cotangent, pairing, first_gain, first_shift, qkv_weight, qkv_bias, dense_weight,
    second_gain, second_shift, up_weight, up_bias, down_weight, out_bias,
):
    bf, f32 = jnp.bfloat16, jnp.float32
    total_blocks = 64
    offsets = jnp.arange(BLK, dtype=jnp.int32)
    ctx_index = lax.axis_index("ctx")
    core = lax.rem(lax.axis_index("wsh"), 2)
    seq_of_layout = jnp.stack([pairing, total_blocks - 1 - pairing], 1).reshape(-1)
    layout_of_seq = (
        jnp.zeros((total_blocks,), jnp.int32)
        .at[seq_of_layout]
        .set(jnp.arange(total_blocks, dtype=jnp.int32))
    )
    own_blocks = lax.dynamic_slice(seq_of_layout, (2 * ctx_index,), (2,))
    row_blocks = lax.dynamic_slice(seq_of_layout, (16 * (ctx_index // 8) + 8 * core,), (8,))
    local_pos = (own_blocks[:, None] * BLK + offsets[None, :]).reshape(-1)
    tables = rotary_tables(local_pos)
    query_scale = HD ** (-0.5)

    shard = lax.broadcasted_iota(jnp.int32, (4, 1), 0) == lax.axis_index("wsh")
    small = (first_gain, first_shift, second_gain, second_shift, out_bias, qkv_bias, up_bias)
    spots = [jnp.where(shard, v[None, :], 0.0).astype(bf).reshape(-1) for v in small]
    vectors = jnp.concatenate(spots + [jnp.zeros((4 * D,), bf)]).reshape(16, D)
    grad_rows = cotangent[0]
    keys_values, queries_grads, normed_one, normed_two, vectors, matrices = front(
        tokens[0], grad_rows, tables, qkv_weight, dense_weight, vectors
    )
    up_shard, down_shard, keys_values = lax.optimization_barrier((up_weight, down_weight, keys_values))
    up_matrix = lax.all_gather(up_shard, "wsh", axis=0, tiled=True)
    down_matrix = lax.all_gather(down_shard, "wsh", axis=0, tiled=True)
    attended_dq, grad_kv = attention(row_blocks, layout_of_seq, queries_grads.reshape(1024, WIDE), keys_values.reshape(8192, WIDE))
    layer_output, input_grad, wide, upper, lower, sums = back(
        attended_dq.reshape(4, ROWS, WIDE), grad_kv.reshape(32, ROWS, WIDE), tokens[0], grad_rows, normed_one, normed_two,
        vectors, tables, matrices, up_matrix, down_matrix,
    )
    mine = lax.axis_index("wsh")
    gains = lax.dynamic_slice(sums, (0, 192 * mine), (5, 192))
    qkv_offset_grad = lax.dynamic_slice(sums[5:8].reshape(-1), (576 * mine,), (576,))
    up_offset_grad = lax.dynamic_slice(sums, (8 + mine, 0), (1, D))[0]
    return (
        layer_output[None], input_grad[None], gains[0], gains[1], wide[:, :2304].astype(f32), qkv_offset_grad,
        wide[:, 2304:].astype(f32), gains[2], gains[3], upper.astype(f32), up_offset_grad, lower.astype(f32), gains[4],
    )


def solution(mesh):
    rows, split, flat = P("wsh", "ctx", None), P("wsh", None), P("wsh")
    return jax.shard_map(
        on_device,
        mesh=mesh,
        in_specs=(rows, rows, P(), flat, flat, split, flat, split, flat, flat, split, flat, split, flat),
        out_specs=(rows, rows, flat, flat, split, flat, split, flat, flat, split, flat, split, flat),
        check_vma=False,
    )
```
